32 devices in a mesh: dp: 4 (over y, core), row: 2 (over x), col: 4 (over z).
Axes of the slice: x: 2, y: 2, z: 4, core: 2. Of those that a mesh axis runs over, the one named last changes fastest.
Arguments:
- tokens: bfloat16 [16384, 1536], P(('dp', 'row', 'col')), may hold values from -6 to 6
- attention_gain: float32 [1536], replicated, may hold values from 0.25 to 1.75
- feedforward_gain: float32 [1536], replicated, may hold values from 0.25 to 1.75
- query_weight: bfloat16 [1536, 1536], P('row', 'col'), may hold values from -0.15625 to 0.15625
- key_value_matrix: bfloat16 [1536, 2, 768], P('row', None, 'col'), may hold values from -0.15625 to 0.15625
- projection_weight: bfloat16 [1536, 1536], P('col', 'row'), may hold values from -2.5 to 2.5
- gate_up_weight: bfloat16 [1536, 2, 4096], P('row', None, 'col'), may hold values from -0.15625 to 0.15625
- down_weight: bfloat16 [4096, 1536], P('col', 'row'), may hold values from -0.09375 to 0.09375
- cotangent: bfloat16 [16384, 1536], P(('dp', 'row', 'col')), may hold values from -6 to 6
Outputs:
- output: bfloat16 [16384, 1536], P(('dp', 'row', 'col'))
- input_grad: bfloat16 [16384, 1536], P(('dp', 'row', 'col'))
- attention_gain_grad: float32 [1536], replicated
- feedforward_gain_grad: float32 [1536], replicated
- query_grad: float32 [1536, 1536], P('row', 'col')
- key_value_grad: float32 [1536, 2, 768], P('row', None, 'col')
- projection_grad: float32 [1536, 1536], P('col', 'row')
- gate_up_grad: float32 [1536, 2, 4096], P('row', None, 'col')
- down_grad: float32 [4096, 1536], P('col', 'row')
The draws below stay inside these ranges and needn't reach their ends.
All inputs are finite; a program needn't handle non-finite values.
Results may differ from the reference program's by a relative error of at most 0.018.
Values may be sent and summed in bfloat16 or wider, within the bound.
No kernel may reach another device: no remote copies, remote signals or barrier semaphores. Data moves between devices by JAX's collectives and lax.ppermute only.
A program may use at most 192 MiB of HBM per device.

```python
import math
import jax
import jax.numpy as jnp
from jax import lax

MODEL_DIM = 1536
QUERY_HEADS = 16
KEY_VALUE_HEADS = 8
HEAD_DIM = 96
FF = 4096
SEQUENCE_TOKENS = 1024
SEQS = 2
ATT = 1536
KEY_VALUE_WIDTH = 768
TOKENS = 16384


def block_levels(rng, shape, pieces, low, high):
    factor_of, own = 1.0, jax.random.fold_in(rng, 6)
    for position, shards_of in pieces:
        steps = jnp.exp(jax.random.uniform(jax.random.fold_in(own, position), (shards_of,), jnp.float32, low / len(pieces), high / len(pieces)))
        factor_of = factor_of * jnp.repeat(steps, shape[position] // shards_of).reshape([-1 if axis == position else 1 for axis in range(len(shape))])
    return factor_of


def noise(stream_key, extent, spread, limit, split=(), kind=jnp.bfloat16):
    gain = block_levels(stream_key, extent, split, -0.22, 0.18) if split else 1.0
    values = jax.random.normal(stream_key, extent, jnp.float32) * spread * gain
    return jnp.minimum(jnp.maximum(values, -limit), limit).astype(kind)


def setup_inputs(seed: int = 0) -> dict:
    splits = jax.random.split(jax.random.key(seed), 10)
    return {
        "tokens": noise(splits[0], (TOKENS, MODEL_DIM), 1.0, 6.0, ((0, 32),)),
        "attention_gain": jnp.clip(1.0 + 0.15 * jax.random.normal(splits[1], (MODEL_DIM,), jnp.float32), 0.25, 1.75),
        "feedforward_gain": jnp.clip(1.0 + 0.15 * jax.random.normal(splits[2], (MODEL_DIM,), jnp.float32), 0.25, 1.75),
        "query_weight": noise(splits[3], (MODEL_DIM, ATT), MODEL_DIM ** -0.5, 0.15625, ((0, 2), (1, 4))),
        "key_value_matrix": noise(splits[4], (MODEL_DIM, 2, KEY_VALUE_WIDTH), MODEL_DIM ** -0.5, 0.15625, ((0, 2), (2, 4))),
        "projection_weight": noise(splits[5], (ATT, MODEL_DIM), (max(ATT // 256, 1)) ** -0.5, 2.5, ((0, 4), (1, 2))),
        "gate_up_weight": noise(splits[6], (MODEL_DIM, 2, FF), MODEL_DIM ** -0.5, 0.15625, ((0, 2), (2, 4))),
        "down_weight": noise(splits[7], (FF, MODEL_DIM), FF ** -0.5, 0.09375, ((0, 4), (1, 2))),
        "cotangent": noise(splits[8], (TOKENS, MODEL_DIM), 1.0, 6.0, ((0, 32),)),
    }


@jax.custom_vjp
def lower_split(v):
    return lax.optimization_barrier(v.astype(jnp.bfloat16)).astype(jnp.float32)

@jax.custom_vjp
def lower_split_back(v):
    return v

def low_keep(v):
    return (lower_split(v), None)

def low_pass(kept, grad):
    return (grad,)

def back_keep(v):
    return (v, None)

def back_low(kept, grad):
    return (lower_split(grad),)
lower_split.defvjp(low_keep, low_pass)
lower_split_back.defvjp(back_keep, back_low)
eps = 1e-05
rope_base = 100000.0

def product_highest(left, right):
    return jnp.dot(left, right, precision=lax.Precision.HIGHEST)

def norm_rows(field, gain_vec):
    return field * lax.rsqrt(lax.optimization_barrier(jnp.mean(field * field, axis=-1, keepdims=True)) + eps) * gain_vec

def apply_rotary(field, seq_len):
    half_size = field.shape[-1] // 2
    positions = (jnp.arange(field.shape[0]) % seq_len).astype(jnp.float32)
    inverse_freq = jnp.exp(jnp.arange(half_size).astype(jnp.float32) * (-2.0 * math.log(rope_base) / field.shape[-1]))
    angles = positions[:, None] * inverse_freq[None, :]
    cosine = jnp.cos(angles)[:, None, :]
    sine_part = jnp.sin(angles)[:, None, :]
    first_half = field[..., :half_size]
    second_half = field[..., half_size:]
    return jnp.concatenate([first_half * cosine - second_half * sine_part, second_half * cosine + first_half * sine_part], axis=-1)

def attend_one(packed):
    query_rows, key_matrix, value_matrix = packed
    seq_len = key_matrix.shape[0]
    scores = jnp.einsum('qkgd,skd->kgqs', query_rows, key_matrix, precision=lax.Precision.HIGHEST) * HEAD_DIM ** (-0.5)
    scores = lower_split_back(scores)
    causal = jnp.arange(seq_len)[:, None] >= jnp.arange(seq_len)[None, :]
    scores = jnp.where(causal, scores, -1e+30)
    attn_probs = lower_split(jax.nn.softmax(scores, axis=-1))
    return jnp.einsum('kgqs,skd->qkgd', attn_probs, value_matrix, precision=lax.Precision.HIGHEST)

def layer_forward(inputs, attention_gain, feedforward_gain, query_weight, key_value_matrix, projection_weight, gate_up_weight, down_weight):
    grouped_tokens = inputs.shape[0]
    sequence_count = grouped_tokens // SEQUENCE_TOKENS
    normalized_rows = lower_split(norm_rows(inputs, attention_gain))
    query_matrix = lower_split_back(product_highest(normalized_rows, query_weight)).reshape(grouped_tokens, QUERY_HEADS, HEAD_DIM)
    key_value_pair = lower_split_back(product_highest(normalized_rows, key_value_matrix.reshape(MODEL_DIM, 2 * KEY_VALUE_WIDTH))).reshape(grouped_tokens, 2, KEY_VALUE_HEADS, HEAD_DIM)
    query_matrix = lower_split(apply_rotary(query_matrix, SEQUENCE_TOKENS)).reshape(sequence_count, SEQUENCE_TOKENS, KEY_VALUE_HEADS, QUERY_HEADS // KEY_VALUE_HEADS, HEAD_DIM)
    key_matrix = lower_split(apply_rotary(key_value_pair[:, 0], SEQUENCE_TOKENS)).reshape(sequence_count, SEQUENCE_TOKENS, KEY_VALUE_HEADS, HEAD_DIM)
    value_matrix = lower_split(key_value_pair[:, 1]).reshape(sequence_count, SEQUENCE_TOKENS, KEY_VALUE_HEADS, HEAD_DIM)
    attended = lax.map(jax.checkpoint(attend_one), (query_matrix, key_matrix, value_matrix))
    attended = lower_split(lower_split_back(attended.reshape(grouped_tokens, ATT)))
    middle = inputs + lower_split_back(product_highest(attended, projection_weight))
    normed_two = lower_split(norm_rows(middle, feedforward_gain))
    gate_up = lower_split_back(product_highest(normed_two, gate_up_weight.reshape(MODEL_DIM, 2 * FF))).reshape(grouped_tokens, 2, FF)
    hidden = lower_split(jax.nn.silu(gate_up[:, 0]) * gate_up[:, 1])
    return middle + lower_split_back(product_highest(hidden, down_weight))

def reference(tokens, attention_gain, feedforward_gain, query_weight, key_value_matrix, projection_weight, gate_up_weight, down_weight, cotangent):
    params = (attention_gain.astype(jnp.float32), feedforward_gain.astype(jnp.float32), query_weight.astype(jnp.float32), key_value_matrix.astype(jnp.float32), projection_weight.astype(jnp.float32), gate_up_weight.astype(jnp.float32), down_weight.astype(jnp.float32))
    grouped_tokens = SEQS * SEQUENCE_TOKENS
    inputs = tokens.astype(jnp.float32).reshape(-1, grouped_tokens, MODEL_DIM)
    seeds = cotangent.astype(jnp.float32).reshape(-1, grouped_tokens, MODEL_DIM)

    def group_step(grad_total, group_item):
        group_in, group_seed = group_item
        result, pull_back = jax.vjp(layer_forward, group_in, *params)
        grad_list = pull_back(group_seed)
        summed = tuple((old + new for old, new in zip(grad_total, grad_list[1:])))
        return (summed, (result, grad_list[0]))
    start_total = tuple((jnp.zeros_like(weight_arr) for weight_arr in params))
    grad_total, (results, input_grads) = lax.scan(group_step, start_total, (inputs, seeds))
    return (results.reshape(TOKENS, MODEL_DIM).astype(jnp.bfloat16), input_grads.reshape(TOKENS, MODEL_DIM).astype(jnp.bfloat16), grad_total[0], grad_total[1], grad_total[2], grad_total[3], grad_total[4], grad_total[5], grad_total[6])
```

```python
import functools
import math

import jax
import jax.numpy as jnp
from jax import lax
from jax.experimental import pallas as pl
from jax.experimental.pallas import tpu as pltpu
from jax.sharding import PartitionSpec as P

QUERY_HEADS = 16
KEY_VALUE_HEADS = 8
HEAD_DIM = 96
SEQUENCE_TOKENS = 1024

eps = 1e-05
rope_base = 100000.0

BF = jnp.bfloat16
F32 = jnp.float32

HALF = HEAD_DIM // 2
LANES = 128
GROUP = 4 * HEAD_DIM
GROUP_LANES = 4 * LANES
BLOCK = 256
SCALE = HEAD_DIM ** (-0.5)
PARTS = 2
SPLIT_MODEL = 768


def dot(a, b):
    return lax.dot_general(a, b, (((1,), (0,)), ((), ())), preferred_element_type=F32)


def dot_nt(a, b):
    return lax.dot_general(a, b, (((1,), (1,)), ((), ())), preferred_element_type=F32)


def dot_tn(a, b):
    return lax.dot_general(a, b, (((0,), (0,)), ((), ())), preferred_element_type=F32)


def scores_t(keys, queries, block):
    s = dot_nt(keys, queries)
    length = s.shape[0]
    key_pos = lax.broadcasted_iota(jnp.int32, s.shape, 0)
    query_pos = lax.broadcasted_iota(jnp.int32, s.shape, 1) + block * BLOCK
    s = jnp.where(key_pos <= query_pos, s, -1e30)
    top = jnp.max(s, axis=0, keepdims=True)
    e = jnp.exp2((s - top) * (SCALE * math.log2(math.e)))
    return e * (1.0 / jnp.sum(e, axis=0, keepdims=True))


def attention_forward_kernel(n1_ref, w_ref, spread_ref, cos_ref, sin_ref, qkv_ref, o_ref):
    w = dot(w_ref[...], spread_ref[...]).astype(BF)
    h = dot(n1_ref[...], w)
    cos, sin = cos_ref[...], sin_ref[...]
    for part in range(4):
        c = h[:, part * LANES : (part + 1) * LANES]
        if part < 3:
            c = c * cos + pltpu.roll(c, LANES // 2, 1) * sin
        qkv_ref[:, part * LANES : (part + 1) * LANES] = c.astype(BF)
    v_t = h[:, 3 * LANES :].T.astype(BF)
    for head in range(2):
        lanes = slice(head * LANES, (head + 1) * LANES)
        for block in range(SEQUENCE_TOKENS // BLOCK):
            rows = slice(block * BLOCK, (block + 1) * BLOCK)
            length = (block + 1) * BLOCK
            p = scores_t(qkv_ref[:length, 2 * LANES : 3 * LANES], qkv_ref[rows, lanes], block)
            o_t = dot(v_t[:, :length], p.astype(BF))
            o_ref[rows, lanes] = o_t.T.astype(BF)


def attention_backward_kernel(qkv_ref, do_ref, gather_ref, cos_ref, sin_ref, out_ref, dk_ref, dv_ref, dq_ref, d_ref):
    cos, sin = cos_ref[...], sin_ref[...]

    def unrotate(c):
        c = c * SCALE
        return (c * cos - pltpu.roll(c, LANES // 2, 1) * sin).astype(BF)

    k_t = qkv_ref[:, 2 * LANES : 3 * LANES].astype(F32).T.astype(BF)
    dk_ref[...] = jnp.zeros_like(dk_ref)
    dv_ref[...] = jnp.zeros_like(dv_ref)
    for head in range(2):
        lanes = slice(head * LANES, (head + 1) * LANES)
        for block in range(SEQUENCE_TOKENS // BLOCK):
            rows = slice(block * BLOCK, (block + 1) * BLOCK)
            length = (block + 1) * BLOCK
            q = qkv_ref[rows, lanes]
            do = do_ref[rows, lanes]
            p = scores_t(qkv_ref[:length, 2 * LANES : 3 * LANES], q, block)
            dp = dot_nt(qkv_ref[:length, 3 * LANES :], do)
            ds = (p * (dp - jnp.sum(p * dp, axis=0, keepdims=True))).astype(BF)
            dv_ref[:length, :] += dot(p.astype(BF), do)
            dk_ref[:length, :] += dot(ds, q)
            dq_ref[rows, :] = dot(k_t[:, :length], ds).T
        d_ref[:, lanes] = unrotate(dq_ref[...])
    d_ref[:, 2 * LANES : 3 * LANES] = unrotate(dk_ref[...])
    d_ref[:, 3 * LANES :] = dv_ref[...].astype(BF)
    out_ref[...] = dot(d_ref[...], gather_ref[...]).astype(BF)


def rotary_tables():
    positions = jnp.arange(SEQUENCE_TOKENS).astype(F32)
    inverse_freq = jnp.exp(jnp.arange(HALF).astype(F32) * (-2.0 * math.log(rope_base) / HEAD_DIM))
    angles = positions[:, None] * inverse_freq[None, :]
    gap = ((0, 0), (0, LANES // 2 - HALF))
    cos, sin = jnp.pad(jnp.cos(angles), gap), jnp.pad(jnp.sin(angles), gap)
    return jnp.concatenate([cos, cos], axis=1), jnp.concatenate([-sin, sin], axis=1)


def spread_matrix():
    src = lax.broadcasted_iota(jnp.int32, (GROUP, GROUP_LANES), 0)
    lane = lax.broadcasted_iota(jnp.int32, (GROUP, GROUP_LANES), 1)
    head, comp = src // HEAD_DIM, src % HEAD_DIM
    place = head * LANES + jnp.where(comp < HALF, comp, comp + LANES // 2 - HALF)
    return (place == lane).astype(BF)


def attention_forward(n1, w, spread, cos, sin):
    tokens, width = n1.shape
    groups = w.shape[1] // GROUP
    whole = lambda a: pl.BlockSpec(a.shape, lambda j: (0, 0))
    return pl.pallas_call(
        attention_forward_kernel,
        grid=(groups,),
        in_specs=[
            whole(n1),
            pl.BlockSpec((width, GROUP), lambda j: (0, j)),
            whole(spread),
            whole(cos),
            whole(sin),
        ],
        out_specs=[
            pl.BlockSpec((tokens, GROUP_LANES), lambda j: (0, j)),
            pl.BlockSpec((tokens, 2 * LANES), lambda j: (0, j)),
        ],
        out_shape=[
            jax.ShapeDtypeStruct((tokens, groups * GROUP_LANES), BF),
            jax.ShapeDtypeStruct((tokens, groups * 2 * LANES), BF),
        ],
        compiler_params=pltpu.CompilerParams(vmem_limit_bytes=48 * 1024 * 1024),
        cost_estimate=pl.CostEstimate(
            flops=2 * tokens * width * groups * GROUP_LANES * 2, bytes_accessed=16 << 20, transcendentals=tokens * tokens * groups * 2
        ),
        name="attention_forward",
    )(n1, w, spread, cos, sin)


def attention_backward(qkv, do, gather, cos, sin):
    tokens = qkv.shape[0]
    groups = qkv.shape[1] // GROUP_LANES
    whole = lambda a: pl.BlockSpec(a.shape, lambda j: (0, 0))
    return pl.pallas_call(
        attention_backward_kernel,
        grid=(groups,),
        in_specs=[
            pl.BlockSpec((tokens, GROUP_LANES), lambda j: (0, j)),
            pl.BlockSpec((tokens, 2 * LANES), lambda j: (0, j)),
            whole(gather),
            whole(cos),
            whole(sin),
        ],
        out_specs=pl.BlockSpec((tokens, GROUP), lambda j: (0, j)),
        out_shape=jax.ShapeDtypeStruct((tokens, groups * GROUP), BF),
        scratch_shapes=[
            pltpu.VMEM((tokens, LANES), F32),
            pltpu.VMEM((tokens, LANES), F32),
            pltpu.VMEM((tokens, LANES), F32),
            pltpu.VMEM((tokens, GROUP_LANES), BF),
        ],
        compiler_params=pltpu.CompilerParams(vmem_limit_bytes=48 * 1024 * 1024),
        cost_estimate=pl.CostEstimate(
            flops=10 * tokens * tokens * LANES * groups * 2, bytes_accessed=16 << 20, transcendentals=tokens * tokens * groups * 2
        ),
        name="attention_backward",
    )(qkv, do, gather, cos, sin)


def feedforward_kernel(col_step, sub, rows_of, n2_ref, cot_ref, *refs):
    take = iter(refs)
    grid_of = lambda: [[next(take) for _ in range(rows_of)] for _ in range(2)]
    gate_up, down, gate_up_grad, down_grad = grid_of(), grid_of(), grid_of(), grid_of()
    out_ref, dn2_ref, n2_t_ref, h_ref, dgu_ref = take
    step, half = pl.program_id(0), pl.num_programs(0) // 2
    width = n2_ref.shape[1] // rows_of
    cut = [slice(i * width, (i + 1) * width) for i in range(rows_of)]

    @pl.when(step == 0)
    def _():
        n2_t_ref[...] = n2_ref[...].T
        out_ref[...] = jnp.zeros_like(out_ref)
        dn2_ref[...] = jnp.zeros_like(dn2_ref)

    def work(whose):
        weights = [r[...].reshape(col_step * sub, width) for r in down[whose]]
        dh = sum(dot_nt(cot_ref[:, cut[i]], weights[i]) for i in range(rows_of))
        for c in range(col_step):
            gu = sum(dot(n2_ref[:, cut[i]], gate_up[whose][i][c]) for i in range(rows_of))
            gate, up = gu[:, :sub], gu[:, sub:]
            sig = jax.nn.sigmoid(gate)
            silu = gate * sig
            lanes = slice(c * sub, (c + 1) * sub)
            part = dh[:, lanes]
            h_ref[:, lanes] = (silu * up).astype(BF)
            dgu_ref[c, :, :sub] = (part * up * (sig + silu * (1 - sig))).astype(BF)
            dgu_ref[c, :, sub:] = (part * silu).astype(BF)
        hidden_t = h_ref[...].T
        for i in range(rows_of):
            out_ref[:, cut[i]] += dot(h_ref[...], weights[i])
            g = dot(hidden_t, cot_ref[:, cut[i]])
            down_grad[whose][i][...] = g.astype(BF).reshape(col_step, sub, width)
            for c in range(col_step):
                gate_up_grad[whose][i][c] = dot(n2_t_ref[cut[i], :], dgu_ref[c]).astype(BF)
            dn2_ref[:, cut[i]] += sum(dot_nt(dgu_ref[c], gate_up[whose][i][c]) for c in range(col_step))

    pl.when(step < half)(lambda: work(1))
    pl.when(step >= half)(lambda: work(0))


def feedforward(n2, cot, gate_up, down, col_step):
    tokens, model = n2.shape
    rows_of = len(down[0])
    columns, sub, width = down[0][0].shape
    half = columns // col_step
    once = lambda a: pl.BlockSpec(a.shape, lambda s: (0, 0), pipeline_mode=pl.Buffered(1))
    place = [lambda s: (jnp.maximum(s - half, 0), 0, 0), lambda s: (jnp.minimum(s, half - 1), 0, 0)]
    spec = lambda a, whose: pl.BlockSpec((col_step,) + a.shape[1:], place[whose])
    flat = [a for side in gate_up for a in side] + [a for side in down for a in side]
    specs = [spec(a, w) for w, side in enumerate(gate_up) for a in side]
    specs += [spec(a, w) for w, side in enumerate(down) for a in side]
    total = jax.ShapeDtypeStruct((tokens, model), F32)
    flops = 18 * tokens * model * 2 * columns * sub
    outs = pl.pallas_call(
        functools.partial(feedforward_kernel, col_step, sub, rows_of),
        grid=(2 * half,),
        in_specs=[once(n2), once(cot)] + specs,
        out_specs=specs + [once(total), once(total)],
        out_shape=[jax.ShapeDtypeStruct(a.shape, BF) for a in flat] + [total, total],
        scratch_shapes=[
            pltpu.VMEM((model, tokens), BF),
            pltpu.VMEM((tokens, col_step * sub), BF),
            pltpu.VMEM((col_step, tokens, 2 * sub), BF),
        ],
        compiler_params=pltpu.CompilerParams(vmem_limit_bytes=60 * 1024 * 1024),
        cost_estimate=pl.CostEstimate(flops=flops, bytes_accessed=48 << 20, transcendentals=tokens * 2 * columns * sub),
        name="feedforward",
    )(n2, cot, *flat)
    n = rows_of
    sides = lambda k: [list(outs[k : k + n]), list(outs[k + n : k + 2 * n])]
    return sides(0), sides(2 * n), outs[4 * n], outs[4 * n + 1]


def inverse_rms(field):
    return lax.rsqrt(jnp.mean(field * field, axis=-1, keepdims=True) + eps)


def norm_back(field, gain, grad):
    r = inverse_rms(field)
    scaled = gain * grad
    inner = jnp.mean(field * scaled, axis=-1, keepdims=True)
    return r * scaled - field * (r * r * r * inner), jnp.sum(grad * field * r, axis=0)


def halves(first_is_mine, mine, other, axis):
    return jnp.where(
        first_is_mine, jnp.concatenate([mine, other], axis), jnp.concatenate([other, mine], axis)
    )


def per_device(
    tokens,
    attention_gain,
    feedforward_gain,
    query_weight,
    key_value_matrix,
    projection_weight,
    gate_up_weight,
    down_weight,
    cotangent,
    *,
    sizes,
):
    dp_size, row_size, col_size = sizes
    x, z, d = lax.axis_index("row"), lax.axis_index("col"), lax.axis_index("dp")
    core, y, parity = d % 2, d // 2, z % 2
    model = tokens.shape[1]
    own = tokens.shape[0]
    block = model // row_size
    hidden_block = down_weight.shape[0]
    sub = hidden_block // 4 // PARTS

    def swap(a, axis, bit):
        n = {"dp": dp_size, "col": col_size}[axis]
        return lax.ppermute(a, axis, [(i, i ^ bit) for i in range(n)])

    def to_core(a):
        return swap(a, "dp", 1)

    def to_y(a):
        return swap(a, "dp", 2)

    def to_pair(a):
        return swap(a, "col", 1)

    def shift(a, axis, by):
        n = {"row": row_size, "col": col_size}[axis]
        return lax.ppermute(a, axis, [(i, (i + by) % n) for i in range(n)])

    def rel(a):
        if row_size == 2:
            return jnp.where(x == 0, a, jnp.concatenate([a[..., block:], a[..., :block]], axis=-1))
        return lax.dynamic_slice_in_dim(jnp.concatenate([a, a], axis=-1), x * block, model, a.ndim - 1)

    def unrel(a):
        if row_size == 2:
            return rel(a)
        return lax.dynamic_slice_in_dim(
            jnp.concatenate([a, a], axis=-1), (row_size - x) % row_size * block, model, a.ndim - 1
        )

    def gather_rows(piece):
        return [piece] + [shift(piece, "row", -i) for i in range(1, row_size)]

    def gather(piece_of):
        mine = [piece_of(parity ^ (j & 1)) for j in range(col_size)]
        along = [mine[0]] + [shift(mine[j], "col", j) for j in range(1, col_size)]
        return [gather_rows(piece) for piece in along]

    def pick(a, index, axis):
        return lax.dynamic_index_in_dim(a, index, axis, keepdims=False)

    query_blocks = query_weight.reshape(block, 2, 2 * HEAD_DIM)
    pair_blocks = key_value_matrix.reshape(block, 2, 2, HEAD_DIM)
    packed = jnp.concatenate([query_blocks, pair_blocks[:, 0], pair_blocks[:, 1]], axis=-1)
    packed = lax.dynamic_slice_in_dim(packed, core * (block // 2), block // 2, 0)
    got = got_qkv = gather(lambda which: pick(packed, which, 1))
    mine = jnp.stack([jnp.concatenate([got[j][i] for j in range(col_size)], axis=1) for i in range(row_size)])
    weight_qkv = halves(core == 0, mine[:, None], to_core(mine)[:, None], 1).reshape(model, -1)

    head_rows = projection_weight.reshape(2, 2, HEAD_DIM, block)
    head_rows = pick(head_rows, core, 1)
    got = gather(lambda which: pick(head_rows, which, 0))
    mine = jnp.stack([jnp.concatenate(got[j], axis=1) for j in range(col_size)])
    heads = halves(core == 0, mine[:, None], to_core(mine)[:, None], 1)
    gap = jnp.zeros(heads.shape[:2] + (LANES // 2 - HALF, model), BF)
    weight_projection = jnp.concatenate(
        [heads[:, :, :HALF], gap, heads[:, :, HALF:], gap], axis=2
    ).reshape(-1, model)

    def after(a, *earlier):
        return lax.optimization_barrier((a,) + earlier)[0]

    def both_cores(rows, axis):
        rows = rows if len(rows) * SPLIT_MODEL <= model else [jnp.concatenate(rows, axis=axis)]
        return [rows, [to_core(r) for r in rows]]

    weights_two = []
    for part in range(PARTS):
        start = ((2 * y + core) * PARTS + part) * sub
        piece = lax.dynamic_slice_in_dim(gate_up_weight, start, sub, 2).reshape(block, 2 * sub)
        piece = after(piece, got_qkv[-1][0])
        gate_up = both_cores(gather_rows(lax.all_gather(piece, "col")), 1)
        piece = after(lax.dynamic_slice_in_dim(down_weight, start, sub, 0), got_qkv[-1][0])
        down = both_cores(gather_rows(lax.all_gather(piece, "col")), 2)
        weights_two.append((gate_up, down))

    def in_sequence(a, other):
        return halves(parity == 0, a, other, 0)

    def over_pair(product, a):
        theirs = lax.dynamic_slice_in_dim(a, (1 - parity) * own, own, 0)
        arrived = to_pair(product(theirs).astype(BF))
        return product(lax.dynamic_slice_in_dim(a, parity * own, own, 0)) + arrived.astype(F32)

    gain_one, gain_two = rel(attention_gain), rel(feedforward_gain)
    inputs = rel(tokens).astype(F32)
    grad_out = rel(cotangent)
    grad_out_all = jnp.concatenate([grad_out, to_y(grad_out)], axis=0)
    normed = (inputs * inverse_rms(inputs) * gain_one).astype(BF)
    normed_all = in_sequence(normed, to_pair(normed))
    cos, sin = rotary_tables()
    spread = spread_matrix()
    qkv, attended = attention_forward(normed_all, weight_qkv, spread, cos, sin)
    middle = inputs + over_pair(lambda a: dot(a, weight_projection), attended)
    normed_two = (middle * inverse_rms(middle) * gain_two).astype(BF)
    normed_two_all = jnp.concatenate([normed_two, to_y(normed_two)], axis=0)

    grads_two, outs, dn2s = [], [], []
    for gate_up, down in weights_two:
        gate_up_grad, down_grad, out, dn2 = feedforward(normed_two_all, grad_out_all, gate_up, down, PARTS)
        grads_two.append((gate_up_grad, down_grad))
        outs.append(out)
        dn2s.append(dn2)

    def over_y(parts):
        kept, sent = (functools.reduce(jnp.add, [p[rows] for p in parts]) for rows in (slice(own), slice(own, None)))
        return kept + to_y(sent.astype(BF)).astype(F32)

    grad_two = over_y(dn2s)
    output = middle + over_y(outs)
    grad_middle, gain_two_term = norm_back(middle, gain_two, grad_two)
    grad_middle = grad_middle + grad_out.astype(F32)

    branch = grad_middle.astype(BF)
    branch_all = in_sequence(branch, to_pair(branch))
    grad_attended = dot_nt(branch_all, weight_projection).astype(BF)
    projection_grad = dot_tn(attended, branch_all).astype(BF)
    grad_qkv = attention_backward(qkv, grad_attended, spread.T, cos, sin)
    qkv_grad = dot_tn(normed_all, grad_qkv).astype(BF)
    grad_one = over_pair(lambda a: dot_nt(a, weight_qkv), grad_qkv)
    grad_inputs, gain_one_term = norm_back(inputs, gain_one, grad_one)
    grad_inputs = grad_inputs + grad_middle

    def total(*parts):
        return sum(part.astype(F32) for part in parts)

    def reduce_rows(blocks):
        return total(blocks[0], *[shift(blocks[i], "row", i) for i in range(1, row_size)]).astype(BF)

    def reduce_columns(parts):
        return [parts[0]] + [shift(parts[j], "col", -j) for j in range(1, col_size)]

    def by_core(a, axis):
        mine, other = pick(a, core, axis), pick(a, 1 - core, axis)
        return total(mine, to_core(other)).astype(BF)

    def by_parity(arrived, axis):
        same = total(*arrived[0::2]).astype(BF)
        cross = total(*arrived[1::2]).astype(BF)
        both = halves(parity == 0, jnp.expand_dims(same, axis), jnp.expand_dims(cross, axis), axis)
        return total(both, to_y(both)).astype(BF)

    g = qkv_grad.reshape(row_size, 2, block // 2, col_size * GROUP)
    g = reduce_rows(by_core(g, 1))
    g = reduce_columns([g[:, j * GROUP : (j + 1) * GROUP] for j in range(col_size)])
    g = by_parity(g, 1)
    g = halves(core == 0, g, to_core(g), 0).astype(F32)
    query_grad = g[:, :, : 2 * HEAD_DIM].reshape(block, -1)
    key_value_grad = jnp.stack(
        [
            g[:, :, 2 * HEAD_DIM : 3 * HEAD_DIM].reshape(block, -1),
            g[:, :, 3 * HEAD_DIM :].reshape(block, -1),
        ],
        axis=1,
    )

    g = projection_grad.reshape(col_size, 2, LANES, model)
    g = jnp.concatenate([g[:, :, :HALF], g[:, :, LANES // 2 : LANES // 2 + HALF]], axis=2)
    g = by_core(g, 1)
    g = reduce_rows([g[:, :, i * block : (i + 1) * block] for i in range(row_size)])
    g = by_parity(reduce_columns([g[j] for j in range(col_size)]), 0)[:, None]
    projection_grad = halves(core == 0, g, to_core(g), 1).astype(F32).reshape(-1, block)

    def by_y_and_core(a, axis):
        a = jnp.expand_dims(a, (axis, axis + 1))
        a = halves(y == 0, a, to_y(a), axis)
        return halves(core == 0, a, to_core(a), axis + 1)

    def reduce_part(mine, other, axis):
        if len(mine) < row_size:
            mine, other = ([r for r in jnp.split(a[0], row_size, axis=axis)] for a in (mine, other))
        arrived = [to_core(r) for r in other]
        rows = [shift(total(mine[i], arrived[i]).astype(BF), "row", i) for i in range(1, row_size)]
        g = total(mine[0], arrived[0], *rows).astype(BF)
        return lax.psum_scatter(g, "col", scatter_dimension=0)

    gate_up_parts, down_parts = [], []
    for gate_up, down in grads_two:
        g = reduce_part(*gate_up, 1).reshape(block, 2, sub)
        gate_up_parts.append(by_y_and_core(g, 2))
        down_parts.append(by_y_and_core(reduce_part(*down, 2), 0))
    gate_up_grad = jnp.stack(gate_up_parts, axis=4).astype(F32).reshape(block, 2, -1)
    down_grad = jnp.stack(down_parts, axis=2).astype(F32).reshape(-1, block)

    gains = unrel(jnp.stack([gain_one_term, gain_two_term]))
    for axis, n in (("dp", dp_size), ("row", row_size), ("col", col_size)):
        bit = 1
        while bit < n:
            gains = gains + lax.ppermute(gains, axis, [(i, i ^ bit) for i in range(n)])
            bit *= 2
    attention_gain_grad, feedforward_gain_grad = gains[0], gains[1]
    return (
        unrel(output.astype(BF)),
        unrel(grad_inputs.astype(BF)),
        attention_gain_grad,
        feedforward_gain_grad,
        query_grad,
        key_value_grad,
        projection_grad,
        gate_up_grad,
        down_grad,
    )


def solution(mesh):
    sizes = tuple(mesh.shape[name] for name in ("dp", "row", "col"))
    return jax.shard_map(
        functools.partial(per_device, sizes=sizes),
        mesh=mesh,
        in_specs=(
            P(("dp", "row", "col"), None),
            P(),
            P(),
            P("row", "col"),
            P("row", None, "col"),
            P("col", "row"),
            P("row", None, "col"),
            P("col", "row"),
            P(("dp", "row", "col"), None),
        ),
        out_specs=(
            P(("dp", "row", "col"), None),
            P(("dp", "row", "col"), None),
            P(),
            P(),
            P("row", "col"),
            P("row", None, "col"),
            P("col", "row"),
            P("row", None, "col"),
            P("col", "row"),
        ),
        check_vma=False,
    )
```

```python
import functools
import math

import jax
import jax.numpy as jnp
from jax import lax
from jax.experimental import pallas as pl
from jax.experimental.pallas import tpu as pltpu
from jax.sharding import PartitionSpec as P

QUERY_HEADS = 16
KEY_VALUE_HEADS = 8
HEAD_DIM = 96
SEQUENCE_TOKENS = 1024

eps = 1e-05
rope_base = 100000.0

BF = jnp.bfloat16
F32 = jnp.float32

HALF = HEAD_DIM // 2
LANES = 128
GROUP = 4 * HEAD_DIM
GROUP_LANES = 4 * LANES
BLOCK = 256
SCALE = HEAD_DIM ** (-0.5)
PARTS = 2
QUICK = pl.CostEstimate(flops=1, bytes_accessed=1, transcendentals=0)
SPLIT_MODEL = 768


def dot(a, b):
    return lax.dot_general(a, b, (((1,), (0,)), ((), ())), preferred_element_type=F32)


def dot_nt(a, b):
    return lax.dot_general(a, b, (((1,), (1,)), ((), ())), preferred_element_type=F32)


def dot_tn(a, b):
    return lax.dot_general(a, b, (((0,), (0,)), ((), ())), preferred_element_type=F32)


def scores_t(keys, queries, block):
    s = dot_nt(keys, queries)
    length = s.shape[0]
    key_pos = lax.broadcasted_iota(jnp.int32, s.shape, 0)
    query_pos = lax.broadcasted_iota(jnp.int32, s.shape, 1) + block * BLOCK
    s = jnp.where(key_pos <= query_pos, s, -1e30)
    top = jnp.max(s, axis=0, keepdims=True)
    e = jnp.exp2((s - top) * (SCALE * math.log2(math.e)))
    return e * (1.0 / jnp.sum(e, axis=0, keepdims=True))


def attention_forward_kernel(n1_ref, w_ref, spread_ref, cos_ref, sin_ref, qkv_ref, o_ref):
    w = dot(w_ref[...], spread_ref[...]).astype(BF)
    h = dot(n1_ref[...], w)
    cos, sin = cos_ref[...], sin_ref[...]
    for part in range(4):
        c = h[:, part * LANES : (part + 1) * LANES]
        if part < 3:
            c = c * cos + pltpu.roll(c, LANES // 2, 1) * sin
        qkv_ref[:, part * LANES : (part + 1) * LANES] = c.astype(BF)
    v_t = h[:, 3 * LANES :].T.astype(BF)
    for head in range(2):
        lanes = slice(head * LANES, (head + 1) * LANES)
        for block in range(SEQUENCE_TOKENS // BLOCK):
            rows = slice(block * BLOCK, (block + 1) * BLOCK)
            length = (block + 1) * BLOCK
            p = scores_t(qkv_ref[:length, 2 * LANES : 3 * LANES], qkv_ref[rows, lanes], block)
            o_t = dot(v_t[:, :length], p.astype(BF))
            o_ref[rows, lanes] = o_t.T.astype(BF)


def attention_backward_kernel(qkv_ref, do_ref, gather_ref, cos_ref, sin_ref, out_ref, dk_ref, dv_ref, dq_ref, d_ref):
    cos, sin = cos_ref[...], sin_ref[...]

    def unrotate(c):
        c = c * SCALE
        return (c * cos - pltpu.roll(c, LANES // 2, 1) * sin).astype(BF)

    k_t = qkv_ref[:, 2 * LANES : 3 * LANES].astype(F32).T.astype(BF)
    dk_ref[...] = jnp.zeros_like(dk_ref)
    dv_ref[...] = jnp.zeros_like(dv_ref)
    for head in range(2):
        lanes = slice(head * LANES, (head + 1) * LANES)
        for block in range(SEQUENCE_TOKENS // BLOCK):
            rows = slice(block * BLOCK, (block + 1) * BLOCK)
            length = (block + 1) * BLOCK
            q = qkv_ref[rows, lanes]
            do = do_ref[rows, lanes]
            p = scores_t(qkv_ref[:length, 2 * LANES : 3 * LANES], q, block)
            dp = dot_nt(qkv_ref[:length, 3 * LANES :], do)
            ds = (p * (dp - jnp.sum(p * dp, axis=0, keepdims=True))).astype(BF)
            dv_ref[:length, :] += dot(p.astype(BF), do)
            dk_ref[:length, :] += dot(ds, q)
            dq_ref[rows, :] = dot(k_t[:, :length], ds).T
        d_ref[:, lanes] = unrotate(dq_ref[...])
    d_ref[:, 2 * LANES : 3 * LANES] = unrotate(dk_ref[...])
    d_ref[:, 3 * LANES :] = dv_ref[...].astype(BF)
    out_ref[...] = dot(d_ref[...], gather_ref[...]).astype(BF)


def rotary_tables():
    positions = jnp.arange(SEQUENCE_TOKENS).astype(F32)
    inverse_freq = jnp.exp(jnp.arange(HALF).astype(F32) * (-2.0 * math.log(rope_base) / HEAD_DIM))
    angles = positions[:, None] * inverse_freq[None, :]
    gap = ((0, 0), (0, LANES // 2 - HALF))
    cos, sin = jnp.pad(jnp.cos(angles), gap), jnp.pad(jnp.sin(angles), gap)
    return jnp.concatenate([cos, cos], axis=1), jnp.concatenate([-sin, sin], axis=1)


def spread_matrix():
    src = lax.broadcasted_iota(jnp.int32, (GROUP, GROUP_LANES), 0)
    lane = lax.broadcasted_iota(jnp.int32, (GROUP, GROUP_LANES), 1)
    head, comp = src // HEAD_DIM, src % HEAD_DIM
    place = head * LANES + jnp.where(comp < HALF, comp, comp + LANES // 2 - HALF)
    return (place == lane).astype(BF)


def attention_forward(n1, w, spread, cos, sin):
    tokens, width = n1.shape
    groups = w.shape[1] // GROUP
    whole = lambda a: pl.BlockSpec(a.shape, lambda j: (0, 0))
    return pl.pallas_call(
        attention_forward_kernel,
        grid=(groups,),
        in_specs=[
            whole(n1),
            pl.BlockSpec((width, GROUP), lambda j: (0, j)),
            whole(spread),
            whole(cos),
            whole(sin),
        ],
        out_specs=[
            pl.BlockSpec((tokens, GROUP_LANES), lambda j: (0, j)),
            pl.BlockSpec((tokens, 2 * LANES), lambda j: (0, j)),
        ],
        out_shape=[
            jax.ShapeDtypeStruct((tokens, groups * GROUP_LANES), BF),
            jax.ShapeDtypeStruct((tokens, groups * 2 * LANES), BF),
        ],
        compiler_params=pltpu.CompilerParams(vmem_limit_bytes=48 * 1024 * 1024),
        cost_estimate=QUICK,
        name="attention_forward",
    )(n1, w, spread, cos, sin)


def attention_backward(qkv, do, gather, cos, sin, first, groups):
    tokens = qkv.shape[0]
    whole = lambda a: pl.BlockSpec(a.shape, lambda j: (0, 0))
    return pl.pallas_call(
        attention_backward_kernel,
        grid=(groups,),
        in_specs=[
            pl.BlockSpec((tokens, GROUP_LANES), lambda j: (0, first + j)),
            pl.BlockSpec((tokens, 2 * LANES), lambda j: (0, first + j)),
            whole(gather),
            whole(cos),
            whole(sin),
        ],
        out_specs=pl.BlockSpec((tokens, GROUP), lambda j: (0, j)),
        out_shape=jax.ShapeDtypeStruct((tokens, groups * GROUP), BF),
        scratch_shapes=[
            pltpu.VMEM((tokens, LANES), F32),
            pltpu.VMEM((tokens, LANES), F32),
            pltpu.VMEM((tokens, LANES), F32),
            pltpu.VMEM((tokens, GROUP_LANES), BF),
        ],
        compiler_params=pltpu.CompilerParams(vmem_limit_bytes=48 * 1024 * 1024),
        cost_estimate=QUICK,
        name="attention_backward",
    )(qkv, do, gather, cos, sin)


def feedforward_kernel(col_step, sub, rows_of, n2_ref, cot_ref, *refs):
    *blocks, out_ref, dn2_ref, h_ref, dgu_ref = refs
    sides = [blocks[k : k + rows_of] for k in range(0, len(blocks), rows_of)]
    weights, earlier, grads = sides[:2], sides[2:-2], sides[-2:]
    step, half = pl.program_id(0), pl.num_programs(0) // 2
    width = n2_ref.shape[1] // rows_of
    cut = [slice(i * width, (i + 1) * width) for i in range(rows_of)]

    @pl.when(step == 0)
    def _():
        out_ref[...] = jnp.zeros_like(out_ref)
        dn2_ref[...] = jnp.zeros_like(dn2_ref)

    def rows(ref, first, last):
        return jnp.concatenate([ref[c, first:last] for c in range(col_step)], axis=0)

    def work(whose):
        gate_up = [rows(r, 0, 2 * sub) for r in weights[whose]]
        down = [rows(r, 2 * sub, 3 * sub) for r in weights[whose]]
        dh = sum(dot_nt(cot_ref[:, cut[i]], down[i]) for i in range(rows_of))
        gu = sum(dot_nt(n2_ref[:, cut[i]], gate_up[i]) for i in range(rows_of))
        for c in range(col_step):
            gate, up = (gu[:, (2 * c + k) * sub : (2 * c + k + 1) * sub] for k in range(2))
            sig = jax.nn.sigmoid(gate)
            silu = gate * sig
            lanes = slice(c * sub, (c + 1) * sub)
            part = dh[:, lanes]
            h_ref[:, lanes] = (silu * up).astype(BF)
            dgu_ref[:, 2 * c * sub : (2 * c + 1) * sub] = (part * up * (sig + silu * (1 - sig))).astype(BF)
            dgu_ref[:, (2 * c + 1) * sub : (2 * c + 2) * sub] = (part * silu).astype(BF)
        hidden, dgu = h_ref[...], dgu_ref[...]
        hidden_t, dgu_t = hidden.T, dgu.T
        for i in range(rows_of):
            dn2_ref[:, cut[i]] += dot(dgu, gate_up[i])
            out_ref[:, cut[i]] += dot(hidden, down[i])
            gate_up_grad = dot(dgu_t, n2_ref[:, cut[i]])
            down_grad = dot(hidden_t, cot_ref[:, cut[i]])
            for c in range(col_step):
                new = (gate_up_grad[2 * c * sub : 2 * (c + 1) * sub], down_grad[c * sub : (c + 1) * sub])
                for part, here in zip(new, (slice(2 * sub), slice(2 * sub, None))):
                    if earlier:
                        part = part + earlier[whose][i][c, here].astype(F32)
                    grads[whose][i][c, here] = part.astype(BF)

    pl.when(step < half)(lambda: work(1))
    pl.when(step >= half)(lambda: work(0))


def feedforward(n2, cot, weights, col_step, earlier=()):
    tokens, model = n2.shape
    rows_of = len(weights[0])
    columns, rows, width = weights[0][0].shape
    sub = rows // 3
    half = columns // col_step
    once = lambda a: pl.BlockSpec(a.shape, lambda s: (0, 0), pipeline_mode=pl.Buffered(1))
    place = [lambda s: (jnp.maximum(s - half, 0), 0, 0), lambda s: (jnp.minimum(s, half - 1), 0, 0)]
    flat = [a for side in weights for a in side]
    specs = [pl.BlockSpec((col_step, rows, width), place[whose]) for whose in range(2) for _ in range(rows_of)]
    earlier = [a for side in earlier for a in side]
    total = jax.ShapeDtypeStruct((tokens, model), F32)
    outs = pl.pallas_call(
        functools.partial(feedforward_kernel, col_step, sub, rows_of),
        grid=(2 * half,),
        in_specs=[once(n2), once(cot)] + specs + (specs if earlier else []),
        out_specs=specs + [once(total), once(total)],
        out_shape=[jax.ShapeDtypeStruct(a.shape, BF) for a in flat] + [total, total],
        scratch_shapes=[
            pltpu.VMEM((tokens, col_step * sub), BF),
            pltpu.VMEM((tokens, 2 * col_step * sub), BF),
        ],
        compiler_params=pltpu.CompilerParams(vmem_limit_bytes=60 * 1024 * 1024),
        cost_estimate=QUICK,
        name="feedforward",
    )(n2, cot, *flat, *earlier)
    return [list(outs[:rows_of]), list(outs[rows_of : 2 * rows_of])], outs[2 * rows_of], outs[2 * rows_of + 1]


def place_kernel(*refs):
    parts, (gate_up_ref, down_ref) = refs[:-2], refs[-2:]
    sub, block = parts[0].shape[2] // 3, parts[0].shape[3]
    tiles = 4 * len(parts)
    for y in range(2):
        for core in range(2):
            for k, part in enumerate(parts):
                tile = (2 * y + core) * len(parts) + k
                for half in range(2):
                    piece = part[y, core, half * sub : (half + 1) * sub].astype(F32)
                    gate_up_ref[pl.ds(2 * tile + half, block, stride=2 * tiles), :] = piece.T
                down_ref[tile * sub : (tile + 1) * sub] = part[y, core, 2 * sub :].astype(F32)


def place(parts):
    sub, block = parts[0].shape[2] // 3, parts[0].shape[3]
    tiles = 4 * len(parts)
    gate_up, down = pl.pallas_call(
        place_kernel,
        out_shape=[
            jax.ShapeDtypeStruct((block * tiles * 2, sub), F32),
            jax.ShapeDtypeStruct((tiles * sub, block), F32),
        ],
        compiler_params=pltpu.CompilerParams(vmem_limit_bytes=48 * 1024 * 1024),
        cost_estimate=QUICK,
        name="place",
    )(*parts)
    return gate_up.reshape(block, tiles, 2, sub).transpose(0, 2, 1, 3).reshape(block, 2, -1), down


def place_attention_kernel(*refs):
    cores, (query_ref, pair_ref, projection_ref) = refs[:2], refs[2:]
    block = query_ref.shape[0]
    rows = block // 2
    for core, ref in enumerate(cores):
        here = slice(core * rows, (core + 1) * rows)
        for parity in range(2):
            g = ref[parity, :rows].astype(F32)
            query_ref[here, 2 * parity * HEAD_DIM : 2 * (parity + 1) * HEAD_DIM] = g[:, : 2 * HEAD_DIM]
            g = g.T
            for k in range(2):
                pair_ref[k, parity * HEAD_DIM : (parity + 1) * HEAD_DIM, here] = g[(2 + k) * HEAD_DIM : (3 + k) * HEAD_DIM]
            head = slice((2 * parity + core) * HEAD_DIM, (2 * parity + core + 1) * HEAD_DIM)
            for k in range(block // GROUP):
                piece = ref[parity, rows + k * HEAD_DIM : rows + (k + 1) * HEAD_DIM]
                projection_ref[head, k * GROUP : (k + 1) * GROUP] = piece.astype(F32)


def place_attention(first, second, block):
    folded = block % GROUP != 0
    query, pair, projection = pl.pallas_call(
        place_attention_kernel,
        out_shape=[
            jax.ShapeDtypeStruct((block, 4 * HEAD_DIM), F32),
            jax.ShapeDtypeStruct((2, 2 * HEAD_DIM, block), F32),
            jax.ShapeDtypeStruct((4 * HEAD_DIM, block), F32),
        ],
        compiler_params=pltpu.CompilerParams(vmem_limit_bytes=32 * 1024 * 1024),
        cost_estimate=QUICK,
        name="place_attention",
    )(first, second)
    if folded:
        both = jnp.stack([a[:, block // 2 :].reshape(2, HEAD_DIM, block) for a in (first, second)], axis=1)
        projection = both.astype(F32).reshape(-1, block)
    return query, pair.transpose(2, 0, 1), projection


def inverse_rms(field):
    return lax.rsqrt(jnp.mean(field * field, axis=-1, keepdims=True) + eps)


def norm_back(field, gain, grad):
    r = inverse_rms(field)
    scaled = gain * grad
    inner = jnp.mean(field * scaled, axis=-1, keepdims=True)
    return r * scaled - field * (r * r * r * inner), jnp.sum(grad * field * r, axis=0)


def halves(first_is_mine, mine, other, axis):
    return jnp.where(
        first_is_mine, jnp.concatenate([mine, other], axis), jnp.concatenate([other, mine], axis)
    )


def per_device(
    tokens,
    attention_gain,
    feedforward_gain,
    query_weight,
    key_value_matrix,
    projection_weight,
    gate_up_weight,
    down_weight,
    cotangent,
    *,
    sizes,
):
    dp_size, row_size, col_size = sizes
    x, z, d = lax.axis_index("row"), lax.axis_index("col"), lax.axis_index("dp")
    core, y, parity = d % 2, d // 2, z % 2
    model = tokens.shape[1]
    own = tokens.shape[0]
    block = model // row_size
    hidden_block = down_weight.shape[0]
    sub = hidden_block // 4 // PARTS

    def swap(a, axis, bit):
        n = {"dp": dp_size, "col": col_size}[axis]
        return lax.ppermute(a, axis, [(i, i ^ bit) for i in range(n)])

    def to_core(a):
        return swap(a, "dp", 1)

    def to_y(a):
        return swap(a, "dp", 2)

    def to_pair(a):
        return swap(a, "col", 1)

    def shift(a, axis, by):
        n = {"row": row_size, "col": col_size}[axis]
        return lax.ppermute(a, axis, [(i, (i + by) % n) for i in range(n)])

    def rel(a):
        if row_size == 2:
            return jnp.where(x == 0, a, jnp.concatenate([a[..., block:], a[..., :block]], axis=-1))
        return lax.dynamic_slice_in_dim(jnp.concatenate([a, a], axis=-1), x * block, model, a.ndim - 1)

    def unrel(a):
        if row_size == 2:
            return rel(a)
        return lax.dynamic_slice_in_dim(
            jnp.concatenate([a, a], axis=-1), (row_size - x) % row_size * block, model, a.ndim - 1
        )

    def gather_rows(piece):
        return [piece] + [shift(piece, "row", -i) for i in range(1, row_size)]

    def gather_columns(piece_of):
        return [piece_of(0)] + [shift(piece_of(j & 1), "col", j) for j in range(1, col_size)]

    def pick(a, index, axis):
        return lax.dynamic_index_in_dim(a, index, axis, keepdims=False)

    def merge(rows):
        return rows if len(rows) * SPLIT_MODEL <= model else [jnp.concatenate(rows, axis=2)]

    def by_rows(blocks):
        return list(blocks) if len(blocks) == row_size else jnp.split(blocks[0], row_size, axis=2)

    def reduce_columns(parts, first=0):
        return [shift(part, "col", -j) if j else part for j, part in enumerate(parts, first)]

    def by_core(a, axis):
        mine, other = pick(a, core, axis), pick(a, 1 - core, axis)
        return small(mine, to_core(other))

    def by_parity(arrived):
        return halves(parity == 0, small(*arrived[0::2])[None], small(*arrived[1::2])[None], 0)

    fence = lax.optimization_barrier

    def fold(a):
        if block % GROUP:
            return a.reshape(-1, GROUP)
        return jnp.concatenate([a[:, k : k + GROUP] for k in range(0, block, GROUP)])

    def unfold(a):
        if block % GROUP:
            return a.reshape(a.shape[:-2] + (HEAD_DIM, block))
        return jnp.concatenate([a[..., k : k + HEAD_DIM, :] for k in range(0, a.shape[-2], HEAD_DIM)], axis=-1)

    near, far = slice(1, None, 2), slice(2, None, 2)

    def total(*parts):
        return sum(part.astype(F32) for part in parts)

    def small(*parts):
        return total(*parts).astype(BF)

    def in_sequence(a, other):
        return halves(parity == 0, a, other, 0)

    def rows_of(a, first):
        return lax.dynamic_slice_in_dim(a, first, own, 0)

    query_blocks = query_weight.reshape(block, 2, 2 * HEAD_DIM)
    pair_blocks = key_value_matrix.reshape(block, 2, 2, HEAD_DIM)
    packed = jnp.concatenate([query_blocks, pair_blocks[:, 0], pair_blocks[:, 1]], axis=-1)
    packed = lax.dynamic_slice_in_dim(packed, core * (block // 2), block // 2, 0)
    head_rows = pick(projection_weight.reshape(2, 2, HEAD_DIM, block), core, 1)
    packed = fence(
        [jnp.concatenate([pick(packed, p, 1), fold(pick(head_rows, p, 0))]) for p in (parity, 1 - parity)]
    )
    along = gather_columns(lambda which: packed[which])
    own_packed = gather_rows(packed[0])

    pieces = []
    for part in range(PARTS):
        start = ((2 * y + core) * PARTS + part) * sub
        gate_up = lax.dynamic_slice_in_dim(gate_up_weight, start, sub, 2).transpose(1, 2, 0).reshape(2 * sub, block)
        pieces.append(jnp.concatenate([gate_up, lax.dynamic_slice_in_dim(down_weight, start, sub, 0)]))
    own_rows = gather_rows(jnp.stack(pieces))

    gain_one, gain_two = rel(attention_gain), rel(feedforward_gain)
    inputs = rel(tokens)
    grad_out = rel(cotangent)
    wide_inputs = inputs.astype(F32)
    normed = (wide_inputs * inverse_rms(wide_inputs) * gain_one).astype(BF)
    tables = rotary_tables()
    spread = spread_matrix()
    spread_back = spread.T
    along, own_packed, own_rows, pieces, normed, inputs, grad_out, tables, spread, spread_back = fence(
        (along, own_packed, own_rows, pieces, normed, inputs, grad_out, tables, spread, spread_back)
    )

    normed_other = to_pair(normed)
    got = gather_rows(jnp.stack(along[1:]))
    grad_out_other = to_y(grad_out)
    others = [None, shift(pieces[0], "col", 2), None]
    mine = [jnp.concatenate([own_packed[0][None], got[0]])]
    mine_other = [to_core(mine[0])]
    got, own_packed, normed, normed_other, own_rows, pieces, grad_out, grad_out_other, others, mine, mine_other = fence(
        (got, own_packed, normed, normed_other, own_rows, pieces, grad_out, grad_out_other, others, mine, mine_other)
    )

    mine += [jnp.concatenate([a[None], b]) for a, b in zip(own_packed[1:], got[1:])]
    mine[1:] = fence(mine[1:])
    mine_other += [to_core(a) for a in mine[1:]]
    normed_all = in_sequence(normed, normed_other)
    others = [shift(pieces[0], "col", 1), others[1], shift(pieces[0], "col", 3)]
    late_others = [shift(pieces[1], "col", 1)]
    pairs = [halves(core == 0, a[:, None], b[:, None], 1) for a, b in zip(mine, mine_other)]
    split = block // 2
    weight_qkv = jnp.concatenate([jnp.concatenate([p[j, :, :split] for j in range(col_size)], axis=-1) for p in pairs])
    weight_qkv = weight_qkv.reshape(model, -1)
    heads = jnp.concatenate([unfold(p[:, :, split:]) for p in pairs], axis=-1)
    gap = jnp.zeros(heads.shape[:2] + (LANES // 2 - HALF, model), BF)
    weight_projection = jnp.concatenate(
        [heads[:, :, :HALF], gap, heads[:, :, HALF:], gap], axis=2
    ).reshape(-1, model)
    weight_qkv, weight_projection, normed_all, grad_out, grad_out_other = fence(
        (weight_qkv, weight_projection, normed_all, grad_out, grad_out_other)
    )

    qkv, attended = attention_forward(normed_all, weight_qkv, spread, *tables)
    qkv, attended, others, late_others, grad_out, grad_out_other, weight_projection = fence(
        (qkv, attended, others, late_others, grad_out, grad_out_other, weight_projection)
    )

    sent = dot(rows_of(attended, (1 - parity) * own), weight_projection).astype(BF)
    stacked = jnp.stack(others)
    sent, stacked, attended, weight_projection = fence((sent, stacked, attended, weight_projection))
    arrived = to_pair(sent)
    rest = gather_rows(stacked)
    kept = dot(rows_of(attended, parity * own), weight_projection)
    kept, arrived, rest, pieces, own_rows = fence((kept, arrived, rest, pieces, own_rows))

    middle = inputs.astype(F32) + kept + arrived.astype(F32)
    normed_two = (middle * inverse_rms(middle) * gain_two).astype(BF)
    mine = merge([jnp.concatenate([a[None], b]) for a, b in zip([a[0] for a in own_rows], rest)])
    normed_two, middle, mine = fence((normed_two, middle, mine))
    normed_two_other = to_y(normed_two)
    others = [shift(pieces[1], "col", j) for j in (2, 3)]
    weights = [mine, [to_core(a) for a in mine]]
    weights, normed_two = fence((weights, normed_two))

    rest = [gather_rows(late_others[0])]
    grads, *sums = feedforward(normed_two, grad_out, weights, PARTS)
    grads, sums, rest, others, normed_two_other, weights, middle, late_others = fence(
        (grads, sums, rest, others, normed_two_other, weights, middle, late_others)
    )
    own_sums = [sums]
    stacked = jnp.stack(others)
    early = (
        [jnp.concatenate([own_rows[0][1:], late_others[0][None], stacked])] if row_size * SPLIT_MODEL <= model else []
    )
    stacked, early, own_rows = fence((stacked, early, own_rows))
    rest.append(gather_rows(stacked))
    early_other = [to_core(a) for a in early]
    grads, *sums = feedforward(normed_two_other, grad_out_other, weights, PARTS, grads)
    grads, sums, rest, early, early_other, own_rows = fence((grads, sums, rest, early, early_other, own_rows))
    other_sums = [sums]
    n = len(early)
    late = merge([jnp.concatenate([a[1:], b[None], c]) for a, b, c in zip(own_rows[n:], rest[0][n:], rest[1][n:])])
    mine, other = by_rows(grads[0]), by_rows(grads[1])
    late, other[1:] = fence((late, other[1:]))
    late_other = [to_core(a) for a in late]
    arrived = [to_core(a) for a in other[1:]]
    mine, other[0], late, late_other, arrived = fence((mine, other[0], late, late_other, arrived))
    weights = [early + late, early_other + late_other]
    cut = col_size // 2
    sent = [small(*pair) for pair in zip(mine[1:], arrived)]
    weights, mine[0], other[0], sent, normed_two_other = fence((weights, mine[0], other[0], sent, normed_two_other))
    rows = [shift(a[:cut], "row", i) for i, a in enumerate(sent, 1)]
    arrived = to_core(other[0])
    grads, *sums = feedforward(normed_two_other, grad_out_other, weights, PARTS)
    grads, sums, rows, mine[0], arrived, sent, weights = fence((grads, sums, rows, mine[0], arrived, sent, weights))
    other_sums.append(sums)

    blocks = [small(mine[0][j], arrived[j], *[r[j] for r in rows]) for j in range(cut)]
    sums = small(*[p[1] for p in other_sums])
    sums, blocks, grads, other_sums, own_sums = fence((sums, blocks, grads, other_sums, own_sums))
    grad_two_other = to_y(sums)
    rows = [shift(a[cut:], "row", i) for i, a in enumerate(sent, 1)]
    along = [blocks[0]] + [shift(blocks[j], "col", -j) for j in range(1, cut)]
    grads, *sums = feedforward(normed_two, grad_out, weights, PARTS, grads)
    grads, sums, rows, along, mine[0], arrived, grad_two_other = fence(
        (grads, sums, rows, along, mine[0], arrived, grad_two_other)
    )
    own_sums.append(sums)
    last, other = by_rows(grads[0]), by_rows(grads[1])
    last_rows = [to_core(a) for a in other[1:]]
    kept = total(grad_two_other, *[p[1] for p in own_sums])
    grad_middle, gain_two_term = norm_back(middle, gain_two, kept)
    grad_middle = grad_middle + grad_out.astype(F32)
    branch = grad_middle.astype(BF)
    last_rows, branch, grad_middle, gain_two_term, last, other[0] = fence(
        (last_rows, branch, grad_middle, gain_two_term, last, other[0])
    )
    branch_other = to_pair(branch)
    sent = [small(*pair) for pair in zip(last[1:], last_rows)]
    last_rows = [shift(a, "row", i) for i, a in enumerate(sent, 1)]
    last_core = to_core(other[0])
    out_kept = middle + total(*[p[0] for p in own_sums])
    out_sent = small(*[p[0] for p in other_sums])
    blocks = [small(mine[0][j], arrived[j], *[r[j - cut] for r in rows]) for j in range(cut, col_size)]
    branch, branch_other, last_core, out_kept, out_sent, blocks, grad_middle, gain_two_term = fence(
        (branch, branch_other, last_core, out_kept, out_sent, blocks, grad_middle, gain_two_term)
    )

    along += [shift(blocks[j - cut], "col", -j) for j in range(cut, col_size)]
    branch_all = in_sequence(branch, branch_other)
    grad_attended = dot_nt(branch_all, weight_projection).astype(BF)
    g = dot_tn(attended, branch_all).astype(BF).reshape(col_size, 2, LANES, model)
    projection_halves = jnp.concatenate([g[:, :, :HALF], g[:, :, LANES // 2 : LANES // 2 + HALF]], axis=2)
    projection_halves = [pick(projection_halves, which, 1) for which in (core, 1 - core)]
    projection_other = to_core(projection_halves[1])
    blocks = [small(last[0][j], last_core[j], *[r[j] for r in last_rows]) for j in range(col_size)]

    count = col_size // 2
    wide = count * GROUP
    to_rows = lambda g: [shift(g[i], "row", i) for i in range(1, row_size)]
    qkv_halves = lambda part: dot_tn(normed_all, part).astype(BF).reshape(row_size, 2, block // 2, wide)
    by_halves = lambda g: [pick(g, which, 1) for which in (core, 1 - core)]

    first = attention_backward(qkv, grad_attended, spread_back, *tables, 0, count)
    first, along, projection_halves, projection_other, blocks, grad_attended = fence(
        (first, along, projection_halves, projection_other, blocks, grad_attended)
    )
    last_along = [blocks[0]] + [shift(blocks[j], "col", -j) if j & 1 else blocks[j] for j in range(1, col_size)]
    first_halves = by_halves(qkv_halves(first))
    first_other = to_core(first_halves[1])
    g = small(projection_halves[0], projection_other)
    projection_rows = [g[:, :, i * block : (i + 1) * block] for i in range(row_size)]
    projection_rows[1:] = to_rows(projection_rows)
    second = attention_backward(qkv, grad_attended, spread_back, *tables, count, count)
    second, last_along, first_other, projection_rows, along, first_halves = fence(
        (second, last_along, first_other, projection_rows, along, first_halves)
    )

    product = lambda rows: sum(
        dot_nt(rows(part), weight_qkv[:, k * wide : (k + 1) * wide]) for k, part in enumerate((first, second))
    )
    sent = product(lambda a: rows_of(a, (1 - parity) * own)).astype(BF)
    second_halves = by_halves(qkv_halves(second))
    first_rows = small(first_halves[0], first_other)
    g = small(*projection_rows)
    sent, second, second_halves, first_rows, g, along, out_sent = fence(
        (sent, second, second_halves, first_rows, g, along, out_sent)
    )
    grad_one_other = to_pair(sent)
    first_rows = [first_rows[0]] + to_rows(first_rows)
    second_other = to_core(second_halves[1])
    first_part = small(*along)
    second_halves, second_other, g, first_part = fence((second_halves, second_other, g, first_part))
    second_rows = small(second_halves[0], second_other)
    second_rows = [second_rows[0]] + to_rows(second_rows)
    last_along[far] = [shift(last_along[j], "col", -j) for j in range(2, col_size, 2)]
    first_part_other = to_y(first_part)
    kept = product(lambda a: rows_of(a, parity * own))
    second_rows, first_rows, grad_one_other, kept, first_part, first_part_other, last_along = fence(
        (second_rows, first_rows, grad_one_other, kept, first_part, first_part_other, last_along)
    )

    columns = lambda g, first: reduce_columns([g[:, j * GROUP : (j + 1) * GROUP] for j in range(count)], first)
    blocks = [small(*first_rows), small(*second_rows)]
    last_part = small(*last_along)
    blocks, last_part = fence((blocks, last_part))
    arrived = columns(blocks[1], count) + columns(blocks[0], 0)
    arrived = arrived[count:] + arrived[:count]
    last_part_other = to_y(last_part)
    grad_inputs, gain_one_term = norm_back(inputs.astype(F32), gain_one, kept + grad_one_other.astype(F32))
    grad_inputs = unrel((grad_inputs + grad_middle).astype(BF))
    gains = unrel(jnp.stack([gain_one_term, gain_two_term]))
    first_part = halves(y == 0, first_part[None], first_part_other[None], 0)[:, None]
    first_part_other = to_core(first_part)
    arrived, gains, grad_inputs, first_part, first_part_other, last_part, last_part_other = fence(
        (arrived, gains, grad_inputs, first_part, first_part_other, last_part, last_part_other)
    )
    projection_along = reduce_columns([g[j] for j in range(col_size)])
    out_other = to_y(out_sent)
    gains = gains + swap(gains, "dp", 1)
    gains = gains + swap(gains, "dp", 2)
    last_part = halves(y == 0, last_part[None], last_part_other[None], 0)[:, None]
    arrived = by_parity(arrived)
    gains, last_part, projection_along, arrived, out_other, first_part = fence(
        (gains, last_part, projection_along, arrived, out_other, first_part)
    )

    both = jnp.concatenate([arrived, jnp.stack([fold(p) for p in by_parity(projection_along)])], axis=1)
    both, gains, last_part = fence((both, gains, last_part))
    both_other = to_y(both)
    last_part_other = to_core(last_part)
    for axis, n in (("row", row_size), ("col", col_size)):
        bit = 1
        while bit < n:
            gains = gains + lax.ppermute(gains, axis, [(i, i ^ bit) for i in range(n)])
            bit *= 2
    attention_gain_grad, feedforward_gain_grad = gains[0], gains[1]
    output = unrel((out_kept + out_other.astype(F32)).astype(BF))
    sides = [halves(core == 0, a, b, 1) for a, b in ((first_part, first_part_other), (last_part, last_part_other))]
    gate_up_grad, down_grad = place(sides)
    both, both_other, gate_up_grad, down_grad, gains, output = fence(
        (both, both_other, gate_up_grad, down_grad, gains, output)
    )
    both = small(both, both_other)
    both_other = to_core(both)
    query_grad, key_value_grad, projection_grad = place_attention(
        jnp.where(core == 0, both, both_other), jnp.where(core == 0, both_other, both), block
    )
    return (
        output,
        grad_inputs,
        attention_gain_grad,
        feedforward_gain_grad,
        query_grad,
        key_value_grad,
        projection_grad,
        gate_up_grad,
        down_grad,
    )


def solution(mesh):
    sizes = tuple(mesh.shape[name] for name in ("dp", "row", "col"))
    return jax.shard_map(
        functools.partial(per_device, sizes=sizes),
        mesh=mesh,
        in_specs=(
            P(("dp", "row", "col"), None),
            P(),
            P(),
            P("row", "col"),
            P("row", None, "col"),
            P("col", "row"),
            P("row", None, "col"),
            P("col", "row"),
            P(("dp", "row", "col"), None),
        ),
        out_specs=(
            P(("dp", "row", "col"), None),
            P(("dp", "row", "col"), None),
            P(),
            P(),
            P("row", "col"),
            P("row", None, "col"),
            P("col", "row"),
            P("row", None, "col"),
            P("col", "row"),
        ),
        check_vma=False,
    )
```

```python
import functools
import math

import jax
import jax.numpy as jnp
from jax import lax
from jax.experimental import pallas as pl
from jax.experimental.pallas import tpu as pltpu
from jax.sharding import PartitionSpec as P

QUERY_HEADS = 16
KEY_VALUE_HEADS = 8
HEAD_DIM = 96
SEQUENCE_TOKENS = 1024

eps = 1e-05
rope_base = 100000.0

BF = jnp.bfloat16
F32 = jnp.float32

HALF = HEAD_DIM // 2
LANES = 128
GROUP = 4 * HEAD_DIM
GROUP_LANES = 4 * LANES
BLOCK = 256
SCALE = HEAD_DIM ** (-0.5)
PARTS = 2
QUICK = pl.CostEstimate(flops=1, bytes_accessed=1, transcendentals=0)
SPLIT_MODEL = 768


def dot(a, b):
    return lax.dot_general(a, b, (((1,), (0,)), ((), ())), preferred_element_type=F32)


def dot_nt(a, b):
    return lax.dot_general(a, b, (((1,), (1,)), ((), ())), preferred_element_type=F32)


def dot_tn(a, b):
    return lax.dot_general(a, b, (((0,), (0,)), ((), ())), preferred_element_type=F32)


def scores_t(keys, queries, block):
    s = dot_nt(keys, queries)
    length = s.shape[0]
    key_pos = lax.broadcasted_iota(jnp.int32, s.shape, 0)
    query_pos = lax.broadcasted_iota(jnp.int32, s.shape, 1) + block * BLOCK
    s = jnp.where(key_pos <= query_pos, s, -1e30)
    top = jnp.max(s, axis=0, keepdims=True)
    e = jnp.exp2((s - top) * (SCALE * math.log2(math.e)))
    return e * (1.0 / jnp.sum(e, axis=0, keepdims=True))


def attention_forward_kernel(n1_ref, w_ref, spread_ref, cos_ref, sin_ref, qkv_ref, o_ref):
    w = dot(w_ref[...], spread_ref[...]).astype(BF)
    h = dot(n1_ref[...], w)
    cos, sin = cos_ref[...], sin_ref[...]
    for part in range(4):
        c = h[:, part * LANES : (part + 1) * LANES]
        if part < 3:
            c = c * cos + pltpu.roll(c, LANES // 2, 1) * sin
        qkv_ref[:, part * LANES : (part + 1) * LANES] = c.astype(BF)
    v_t = h[:, 3 * LANES :].T.astype(BF)
    for head in range(2):
        lanes = slice(head * LANES, (head + 1) * LANES)
        for block in range(SEQUENCE_TOKENS // BLOCK):
            rows = slice(block * BLOCK, (block + 1) * BLOCK)
            length = (block + 1) * BLOCK
            p = scores_t(qkv_ref[:length, 2 * LANES : 3 * LANES], qkv_ref[rows, lanes], block)
            o_t = dot(v_t[:, :length], p.astype(BF))
            o_ref[rows, lanes] = o_t.T.astype(BF)


def attention_backward_kernel(qkv_ref, do_ref, gather_ref, cos_ref, sin_ref, out_ref, dk_ref, dv_ref, dq_ref, d_ref):
    cos, sin = cos_ref[...], sin_ref[...]

    def unrotate(c):
        c = c * SCALE
        return (c * cos - pltpu.roll(c, LANES // 2, 1) * sin).astype(BF)

    k_t = qkv_ref[:, 2 * LANES : 3 * LANES].astype(F32).T.astype(BF)
    dk_ref[...] = jnp.zeros_like(dk_ref)
    dv_ref[...] = jnp.zeros_like(dv_ref)
    for head in range(2):
        lanes = slice(head * LANES, (head + 1) * LANES)
        for block in range(SEQUENCE_TOKENS // BLOCK):
            rows = slice(block * BLOCK, (block + 1) * BLOCK)
            length = (block + 1) * BLOCK
            q = qkv_ref[rows, lanes]
            do = do_ref[rows, lanes]
            p = scores_t(qkv_ref[:length, 2 * LANES : 3 * LANES], q, block)
            dp = dot_nt(qkv_ref[:length, 3 * LANES :], do)
            ds = (p * (dp - jnp.sum(p * dp, axis=0, keepdims=True))).astype(BF)
            dv_ref[:length, :] += dot(p.astype(BF), do)
            dk_ref[:length, :] += dot(ds, q)
            dq_ref[rows, :] = dot(k_t[:, :length], ds).T
        d_ref[:, lanes] = unrotate(dq_ref[...])
    d_ref[:, 2 * LANES : 3 * LANES] = unrotate(dk_ref[...])
    d_ref[:, 3 * LANES :] = dv_ref[...].astype(BF)
    out_ref[...] = dot(d_ref[...], gather_ref[...]).astype(BF)


def rotary_tables():
    positions = jnp.arange(SEQUENCE_TOKENS).astype(F32)
    inverse_freq = jnp.exp(jnp.arange(HALF).astype(F32) * (-2.0 * math.log(rope_base) / HEAD_DIM))
    angles = positions[:, None] * inverse_freq[None, :]
    gap = ((0, 0), (0, LANES // 2 - HALF))
    cos, sin = jnp.pad(jnp.cos(angles), gap), jnp.pad(jnp.sin(angles), gap)
    return jnp.concatenate([cos, cos], axis=1), jnp.concatenate([-sin, sin], axis=1)


def spread_matrix():
    src = lax.broadcasted_iota(jnp.int32, (GROUP, GROUP_LANES), 0)
    lane = lax.broadcasted_iota(jnp.int32, (GROUP, GROUP_LANES), 1)
    head, comp = src // HEAD_DIM, src % HEAD_DIM
    place = head * LANES + jnp.where(comp < HALF, comp, comp + LANES // 2 - HALF)
    return (place == lane).astype(BF)


def attention_forward(n1, w, spread, cos, sin):
    tokens, width = n1.shape
    groups = w.shape[1] // GROUP
    whole = lambda a: pl.BlockSpec(a.shape, lambda j: (0, 0))
    return pl.pallas_call(
        attention_forward_kernel,
        grid=(groups,),
        in_specs=[
            whole(n1),
            pl.BlockSpec((width, GROUP), lambda j: (0, j)),
            whole(spread),
            whole(cos),
            whole(sin),
        ],
        out_specs=[
            pl.BlockSpec((tokens, GROUP_LANES), lambda j: (0, j)),
            pl.BlockSpec((tokens, 2 * LANES), lambda j: (0, j)),
        ],
        out_shape=[
            jax.ShapeDtypeStruct((tokens, groups * GROUP_LANES), BF),
            jax.ShapeDtypeStruct((tokens, groups * 2 * LANES), BF),
        ],
        compiler_params=pltpu.CompilerParams(vmem_limit_bytes=48 * 1024 * 1024),
        cost_estimate=QUICK,
        name="attention_forward",
    )(n1, w, spread, cos, sin)


def attention_backward(qkv, do, gather, cos, sin, first, groups):
    tokens = qkv.shape[0]
    whole = lambda a: pl.BlockSpec(a.shape, lambda j: (0, 0))
    return pl.pallas_call(
        attention_backward_kernel,
        grid=(groups,),
        in_specs=[
            pl.BlockSpec((tokens, GROUP_LANES), lambda j: (0, first + j)),
            pl.BlockSpec((tokens, 2 * LANES), lambda j: (0, first + j)),
            whole(gather),
            whole(cos),
            whole(sin),
        ],
        out_specs=pl.BlockSpec((tokens, GROUP), lambda j: (0, j)),
        out_shape=jax.ShapeDtypeStruct((tokens, groups * GROUP), BF),
        scratch_shapes=[
            pltpu.VMEM((tokens, LANES), F32),
            pltpu.VMEM((tokens, LANES), F32),
            pltpu.VMEM((tokens, LANES), F32),
            pltpu.VMEM((tokens, GROUP_LANES), BF),
        ],
        compiler_params=pltpu.CompilerParams(vmem_limit_bytes=48 * 1024 * 1024),
        cost_estimate=QUICK,
        name="attention_backward",
    )(qkv, do, gather, cos, sin)


def feedforward_kernel(col_step, sub, rows_of, n2_ref, cot_ref, *refs):
    *blocks, out_ref, dn2_ref, h_ref, dgu_ref = refs
    sides = [blocks[k : k + rows_of] for k in range(0, len(blocks), rows_of)]
    weights, earlier, grads = sides[:2], sides[2:-2], sides[-2:]
    step, half = pl.program_id(0), pl.num_programs(0) // 2
    width = n2_ref.shape[1] // rows_of
    cut = [slice(i * width, (i + 1) * width) for i in range(rows_of)]

    @pl.when(step == 0)
    def _():
        out_ref[...] = jnp.zeros_like(out_ref)
        dn2_ref[...] = jnp.zeros_like(dn2_ref)

    def rows(ref, first, last):
        return jnp.concatenate([ref[c, first:last] for c in range(col_step)], axis=0)

    def work(whose):
        gate_up = [rows(r, 0, 2 * sub) for r in weights[whose]]
        down = [rows(r, 2 * sub, 3 * sub) for r in weights[whose]]
        dh = sum(dot_nt(cot_ref[:, cut[i]], down[i]) for i in range(rows_of))
        gu = sum(dot_nt(n2_ref[:, cut[i]], gate_up[i]) for i in range(rows_of))
        for c in range(col_step):
            gate, up = (gu[:, (2 * c + k) * sub : (2 * c + k + 1) * sub] for k in range(2))
            sig = jax.nn.sigmoid(gate)
            silu = gate * sig
            lanes = slice(c * sub, (c + 1) * sub)
            part = dh[:, lanes]
            h_ref[:, lanes] = (silu * up).astype(BF)
            dgu_ref[:, 2 * c * sub : (2 * c + 1) * sub] = (part * up * (sig + silu * (1 - sig))).astype(BF)
            dgu_ref[:, (2 * c + 1) * sub : (2 * c + 2) * sub] = (part * silu).astype(BF)
        hidden, dgu = h_ref[...], dgu_ref[...]
        hidden_t, dgu_t = hidden.T, dgu.T
        for i in range(rows_of):
            dn2_ref[:, cut[i]] += dot(dgu, gate_up[i])
            out_ref[:, cut[i]] += dot(hidden, down[i])
            gate_up_grad = dot(dgu_t, n2_ref[:, cut[i]])
            down_grad = dot(hidden_t, cot_ref[:, cut[i]])
            for c in range(col_step):
                new = (gate_up_grad[2 * c * sub : 2 * (c + 1) * sub], down_grad[c * sub : (c + 1) * sub])
                for part, here in zip(new, (slice(2 * sub), slice(2 * sub, None))):
                    if earlier:
                        part = part + earlier[whose][i][c, here].astype(F32)
                    grads[whose][i][c, here] = part.astype(BF)

    pl.when(step < half)(lambda: work(1))
    pl.when(step >= half)(lambda: work(0))


def feedforward(n2, cot, weights, col_step, earlier=()):
    tokens, model = n2.shape
    rows_of = len(weights[0])
    columns, rows, width = weights[0][0].shape
    sub = rows // 3
    half = columns // col_step
    once = lambda a: pl.BlockSpec(a.shape, lambda s: (0, 0), pipeline_mode=pl.Buffered(1))
    place = [lambda s: (jnp.maximum(s - half, 0), 0, 0), lambda s: (jnp.minimum(s, half - 1), 0, 0)]
    flat = [a for side in weights for a in side]
    specs = [pl.BlockSpec((col_step, rows, width), place[whose]) for whose in range(2) for _ in range(rows_of)]
    earlier = [a for side in earlier for a in side]
    total = jax.ShapeDtypeStruct((tokens, model), F32)
    outs = pl.pallas_call(
        functools.partial(feedforward_kernel, col_step, sub, rows_of),
        grid=(2 * half,),
        in_specs=[once(n2), once(cot)] + specs + (specs if earlier else []),
        out_specs=specs + [once(total), once(total)],
        out_shape=[jax.ShapeDtypeStruct(a.shape, BF) for a in flat] + [total, total],
        scratch_shapes=[
            pltpu.VMEM((tokens, col_step * sub), BF),
            pltpu.VMEM((tokens, 2 * col_step * sub), BF),
        ],
        compiler_params=pltpu.CompilerParams(vmem_limit_bytes=60 * 1024 * 1024),
        cost_estimate=QUICK,
        name="feedforward",
    )(n2, cot, *flat, *earlier)
    return [list(outs[:rows_of]), list(outs[rows_of : 2 * rows_of])], outs[2 * rows_of], outs[2 * rows_of + 1]


def place_kernel(*refs):
    cores, (gate_up_ref, down_ref) = refs[:2], refs[2:]
    parts, _, rows, block = cores[0].shape
    sub = rows // 3
    for core, ref in enumerate(cores):
        for y in range(2):
            for k in range(parts):
                tile = (2 * y + core) * parts + k
                for half in range(2):
                    piece = ref[k, y, half * sub : (half + 1) * sub].astype(F32)
                    gate_up_ref[pl.ds(2 * tile + half, block, stride=8 * parts), :] = piece.T
                down_ref[tile * sub : (tile + 1) * sub] = ref[k, y, 2 * sub :].astype(F32)


def place(first, second):
    parts, _, rows, block = first.shape
    sub = rows // 3
    tiles = 4 * parts
    gate_up, down = pl.pallas_call(
        place_kernel,
        out_shape=[
            jax.ShapeDtypeStruct((block * tiles * 2, sub), F32),
            jax.ShapeDtypeStruct((tiles * sub, block), F32),
        ],
        compiler_params=pltpu.CompilerParams(vmem_limit_bytes=48 * 1024 * 1024),
        cost_estimate=QUICK,
        name="place",
    )(first, second)
    return gate_up.reshape(block, tiles, 2, sub).transpose(0, 2, 1, 3).reshape(block, 2, -1), down


def combine_kernel(*refs):
    out_ref = refs[-1]
    *rows, mine, other = refs[:-1]
    qkv = sum(r[...].astype(F32) for r in rows).astype(BF)
    heads = (mine[...].astype(F32) + other[...].astype(F32)).astype(BF)
    split = qkv.shape[0]
    for p in range(2):
        out_ref[p, :split] = qkv[:, p * GROUP : (p + 1) * GROUP]
        for n in range(2 * split // GROUP):
            here = slice(split + n * HEAD_DIM, split + (n + 1) * HEAD_DIM)
            out_ref[p, here] = heads[p, :, n * GROUP : (n + 1) * GROUP]


def combine(rows, arrived, heads, heads_arrived):
    split, block = rows[0].shape[0], heads.shape[2]
    if block % GROUP:
        qkv = sum(r.astype(F32) for r in rows + [arrived])
        heads = heads.astype(F32) + heads_arrived.astype(F32)
        parts = [jnp.concatenate([qkv[:, p * GROUP : (p + 1) * GROUP], heads[p].reshape(-1, GROUP)]) for p in range(2)]
        return jnp.stack(parts).astype(BF)
    return pl.pallas_call(
        combine_kernel,
        out_shape=jax.ShapeDtypeStruct((2, split + HEAD_DIM * block // GROUP, GROUP), BF),
        compiler_params=pltpu.CompilerParams(vmem_limit_bytes=32 * 1024 * 1024),
        cost_estimate=QUICK,
        name="combine",
    )(*rows, arrived, heads, heads_arrived)


def place_attention_kernel(*refs):
    cores, (query_ref, pair_ref, projection_ref) = refs[:2], refs[2:]
    block = query_ref.shape[0]
    rows = block // 2
    for core, ref in enumerate(cores):
        here = slice(core * rows, (core + 1) * rows)
        for parity in range(2):
            g = ref[parity, :rows].astype(F32)
            query_ref[here, 2 * parity * HEAD_DIM : 2 * (parity + 1) * HEAD_DIM] = g[:, : 2 * HEAD_DIM]
            g = g.T
            for k in range(2):
                pair_ref[k, parity * HEAD_DIM : (parity + 1) * HEAD_DIM, here] = g[(2 + k) * HEAD_DIM : (3 + k) * HEAD_DIM]
            head = slice((2 * parity + core) * HEAD_DIM, (2 * parity + core + 1) * HEAD_DIM)
            for k in range(block // GROUP):
                piece = ref[parity, rows + k * HEAD_DIM : rows + (k + 1) * HEAD_DIM]
                projection_ref[head, k * GROUP : (k + 1) * GROUP] = piece.astype(F32)


def place_attention(first, second, block):
    folded = block % GROUP != 0
    query, pair, projection = pl.pallas_call(
        place_attention_kernel,
        out_shape=[
            jax.ShapeDtypeStruct((block, 4 * HEAD_DIM), F32),
            jax.ShapeDtypeStruct((2, 2 * HEAD_DIM, block), F32),
            jax.ShapeDtypeStruct((4 * HEAD_DIM, block), F32),
        ],
        compiler_params=pltpu.CompilerParams(vmem_limit_bytes=32 * 1024 * 1024),
        cost_estimate=QUICK,
        name="place_attention",
    )(first, second)
    if folded:
        both = jnp.stack([a[:, block // 2 :].reshape(2, HEAD_DIM, block) for a in (first, second)], axis=1)
        projection = both.astype(F32).reshape(-1, block)
    return query, pair.transpose(2, 0, 1), projection


def assemble_kernel(groups, core_ref, *refs):
    pieces, (qkv_ref, projection_ref) = refs[:-2], refs[-2:]
    first = core_ref[0] == 0
    blocks = len(pieces) // groups
    rows = qkv_ref.shape[0] // (2 * blocks)
    projection_ref[...] = jnp.zeros_like(projection_ref)
    for i in range(blocks):
        for k in range(groups // 2):
            mine, other = pieces[i * groups + 2 * k], pieces[i * groups + 2 * k + 1]
            for p in range(2):
                a, b = mine[p], other[p]
                group = 2 * k + p
                for core, piece in enumerate((jnp.where(first, a, b), jnp.where(first, b, a))):
                    start = (2 * i + core) * rows
                    qkv_ref[start : start + rows, group * GROUP : (group + 1) * GROUP] = piece[:rows]
                    place = group * 2 * LANES + core * LANES
                    for n in range(2 * rows // GROUP):
                        lanes = slice(2 * i * rows + n * GROUP, 2 * i * rows + (n + 1) * GROUP)
                        head = piece[rows + n * HEAD_DIM : rows + (n + 1) * HEAD_DIM]
                        projection_ref[place : place + HALF, lanes] = head[:HALF]
                        projection_ref[place + LANES // 2 : place + LANES // 2 + HALF, lanes] = head[HALF:]


def assemble(core, pieces, model):
    groups = len(pieces[0])
    flat = [a for row in pieces for a in row]
    return pl.pallas_call(
        functools.partial(assemble_kernel, groups),
        in_specs=[pl.BlockSpec(memory_space=pltpu.SMEM)] + [pl.BlockSpec(memory_space=pltpu.VMEM)] * len(flat),
        out_shape=[
            jax.ShapeDtypeStruct((model, groups * GROUP), BF),
            jax.ShapeDtypeStruct((groups * 2 * LANES, model), BF),
        ],
        compiler_params=pltpu.CompilerParams(vmem_limit_bytes=48 * 1024 * 1024),
        cost_estimate=QUICK,
        name="assemble",
    )(core.astype(jnp.int32)[None], *flat)


def halves_kernel(gap, core_ref, a_ref, b_ref, out_ref):
    g = dot_tn(a_ref[...], b_ref[...]).astype(BF)
    if gap:
        out_ref[0, 0, :HALF] = g[:HALF]
        out_ref[0, 0, HALF:] = g[LANES // 2 : LANES // 2 + HALF]
    else:
        out_ref[0, 0] = g


def gradient_halves(core, a, b, rows, gap=False):
    tokens, width = a.shape
    blocks = width // (2 * rows)
    kept = HEAD_DIM if gap else rows
    columns = b.shape[1]
    return pl.pallas_call(
        functools.partial(halves_kernel, gap),
        grid_spec=pltpu.PrefetchScalarGridSpec(
            num_scalar_prefetch=1,
            grid=(2, blocks),
            in_specs=[
                pl.BlockSpec((tokens, rows), lambda h, i, core: (0, 2 * i + (core[0] + h) % 2)),
                pl.BlockSpec(b.shape, lambda h, i, core: (0, 0)),
            ],
            out_specs=pl.BlockSpec((1, 1, kept, columns), lambda h, i, core: (h, i, 0, 0)),
        ),
        out_shape=jax.ShapeDtypeStruct((2, blocks, kept, columns), BF),
        compiler_params=pltpu.CompilerParams(vmem_limit_bytes=48 * 1024 * 1024),
        cost_estimate=QUICK,
        name="gradient_halves",
    )(core.astype(jnp.int32)[None], a, b)


def inverse_rms(field):
    return lax.rsqrt(jnp.mean(field * field, axis=-1, keepdims=True) + eps)


def norm_back(field, gain, grad):
    r = inverse_rms(field)
    scaled = gain * grad
    inner = jnp.mean(field * scaled, axis=-1, keepdims=True)
    return r * scaled - field * (r * r * r * inner), jnp.sum(grad * field * r, axis=0)


def halves(first_is_mine, mine, other, axis):
    return jnp.where(
        first_is_mine, jnp.concatenate([mine, other], axis), jnp.concatenate([other, mine], axis)
    )


def per_device(
    tokens,
    attention_gain,
    feedforward_gain,
    query_weight,
    key_value_matrix,
    projection_weight,
    gate_up_weight,
    down_weight,
    cotangent,
    *,
    sizes,
):
    dp_size, row_size, col_size = sizes
    x, z, d = lax.axis_index("row"), lax.axis_index("col"), lax.axis_index("dp")
    core, y, parity = d % 2, d // 2, z % 2
    model = tokens.shape[1]
    own = tokens.shape[0]
    block = model // row_size
    hidden_block = down_weight.shape[0]
    sub = hidden_block // 4 // PARTS

    def swap(a, axis, bit):
        n = {"dp": dp_size, "col": col_size}[axis]
        return lax.ppermute(a, axis, [(i, i ^ bit) for i in range(n)])

    def to_core(a):
        return swap(a, "dp", 1)

    def to_y(a):
        return swap(a, "dp", 2)

    def to_pair(a):
        return swap(a, "col", 1)

    def shift(a, axis, by):
        n = {"row": row_size, "col": col_size}[axis]
        return lax.ppermute(a, axis, [(i, (i + by) % n) for i in range(n)])

    def rel(a):
        if row_size == 2:
            return jnp.where(x == 0, a, jnp.concatenate([a[..., block:], a[..., :block]], axis=-1))
        return lax.dynamic_slice_in_dim(jnp.concatenate([a, a], axis=-1), x * block, model, a.ndim - 1)

    def unrel(a):
        if row_size == 2:
            return rel(a)
        return lax.dynamic_slice_in_dim(
            jnp.concatenate([a, a], axis=-1), (row_size - x) % row_size * block, model, a.ndim - 1
        )

    def gather_rows(piece):
        return [piece] + [shift(piece, "row", -i) for i in range(1, row_size)]

    def pick(a, index, axis):
        return lax.dynamic_index_in_dim(a, index, axis, keepdims=False)

    def merge(rows):
        return rows if len(rows) * SPLIT_MODEL <= model else [jnp.concatenate(rows, axis=2)]

    def by_rows(blocks):
        return list(blocks) if len(blocks) == row_size else jnp.split(blocks[0], row_size, axis=2)

    fence = lax.optimization_barrier

    def fold(a):
        if block % GROUP:
            return a.reshape(-1, GROUP)
        return jnp.concatenate([a[:, k : k + GROUP] for k in range(0, block, GROUP)])

    def unfold(a):
        if block % GROUP:
            return a.reshape(a.shape[:-2] + (HEAD_DIM, block))
        return jnp.concatenate([a[..., k : k + HEAD_DIM, :] for k in range(0, a.shape[-2], HEAD_DIM)], axis=-1)


    def total(*parts):
        return sum(part.astype(F32) for part in parts)

    def small(*parts):
        return total(*parts).astype(BF)

    def in_sequence(a, other):
        return halves(parity == 0, a, other, 0)

    def rows_of(a, first):
        return lax.dynamic_slice_in_dim(a, first, own, 0)

    query_blocks = query_weight.reshape(block, 2, 2 * HEAD_DIM)
    pair_blocks = key_value_matrix.reshape(block, 2, 2, HEAD_DIM)
    packed = jnp.concatenate([query_blocks, pair_blocks[:, 0], pair_blocks[:, 1]], axis=-1)
    packed = lax.dynamic_slice_in_dim(packed, core * (block // 2), block // 2, 0)
    head_rows = pick(projection_weight.reshape(2, 2, HEAD_DIM, block), core, 1)
    packed = jnp.stack([jnp.concatenate([packed[:, p], fold(head_rows[p])]) for p in range(2)])
    packed, tokens, cotangent, gate_up_weight, down_weight = fence(
        (packed, tokens, cotangent, gate_up_weight, down_weight)
    )
    far_packed = shift(packed, "col", 2)
    own_packed = gather_rows(packed)

    pieces = []
    for part in range(PARTS):
        start = ((2 * y + core) * PARTS + part) * sub
        gate_up = lax.dynamic_slice_in_dim(gate_up_weight, start, sub, 2).transpose(1, 2, 0).reshape(2 * sub, block)
        pieces.append(jnp.concatenate([gate_up, lax.dynamic_slice_in_dim(down_weight, start, sub, 0)]))
    own_rows = gather_rows(jnp.stack(pieces))
    grad_out = rel(cotangent)
    grad_out_other = to_y(grad_out)
    gain_one, gain_two = rel(attention_gain), rel(feedforward_gain)
    inputs = rel(tokens)
    wide_inputs = inputs.astype(F32)
    normed = (wide_inputs * inverse_rms(wide_inputs) * gain_one).astype(BF)
    normed_other = to_pair(normed)
    tables = rotary_tables()
    spread = spread_matrix()
    spread_back = spread.T
    far_packed, own_packed, own_rows, pieces, grad_out, grad_out_other, inputs, normed, normed_other, tables = fence(
        (far_packed, own_packed, own_rows, pieces, grad_out, grad_out_other, inputs, normed, normed_other, tables)
    )

    far_rows = gather_rows(far_packed)
    own_cores = [to_core(a) for a in own_packed]
    others = [shift(pieces[0], "col", 1)]
    late_others = [shift(pieces[1], "col", 1)]
    normed_all = in_sequence(normed, normed_other)
    far_rows, own_cores, own_packed, others, late_others, normed_all, spread, spread_back = fence(
        (far_rows, own_cores, own_packed, others, late_others, normed_all, spread, spread_back)
    )
    far_cores = [to_core(a) for a in far_rows]
    others += [shift(pieces[0], "col", j) for j in range(2, col_size)]
    split = block // 2
    if split % LANES == 0:
        rows = [list(parts) for parts in zip(far_rows, far_cores, own_packed, own_cores)]
        weight_qkv, weight_projection = assemble(core, rows, model)
    else:
        pick_core = lambda a, b: halves(core == 0, a[:, None], b[:, None], 1)
        pairs = [
            jnp.concatenate([pick_core(*far), pick_core(*mine)])
            for far, mine in zip(zip(far_rows, far_cores), zip(own_packed, own_cores))
        ]
        weight_qkv = jnp.concatenate([jnp.concatenate([p[j, :, :split] for j in range(col_size)], axis=-1) for p in pairs])
        weight_qkv = weight_qkv.reshape(model, -1)
        heads = jnp.concatenate([unfold(p[:, :, split:]) for p in pairs], axis=-1)
        gap = jnp.zeros(heads.shape[:2] + (LANES // 2 - HALF, model), BF)
        weight_projection = jnp.concatenate(
            [heads[:, :, :HALF], gap, heads[:, :, HALF:], gap], axis=2
        ).reshape(-1, model)
    weight_qkv, weight_projection = fence((weight_qkv, weight_projection))

    qkv, attended = attention_forward(normed_all, weight_qkv, spread, *tables)
    qkv, attended, others, late_others, grad_out, grad_out_other, weight_projection = fence(
        (qkv, attended, others, late_others, grad_out, grad_out_other, weight_projection)
    )

    sent = dot(rows_of(attended, (1 - parity) * own), weight_projection).astype(BF)
    stacked = jnp.stack(others)
    sent, stacked, attended, weight_projection = fence((sent, stacked, attended, weight_projection))
    arrived = to_pair(sent)
    rest = gather_rows(stacked)
    fine = row_size * SPLIT_MODEL <= model
    own_first = [a[0] for a in own_rows]
    kept = dot(rows_of(attended, parity * own), weight_projection)
    kept, stacked = fence((kept, stacked))
    mine = [jnp.concatenate([own_first[0][None], stacked])] if fine else []
    mine_other = [to_core(a) for a in mine]
    kept, arrived, rest, mine, mine_other, pieces, own_rows = fence(
        (kept, arrived, rest, mine, mine_other, pieces, own_rows)
    )

    middle = inputs.astype(F32) + kept + arrived.astype(F32)
    normed_two = (middle * inverse_rms(middle) * gain_two).astype(BF)
    n = len(mine)
    late = merge([jnp.concatenate([a[None], b]) for a, b in zip(own_first[n:], rest[n:])])
    normed_two, middle, late = fence((normed_two, middle, late))
    normed_two_other = to_y(normed_two)
    weights = [mine + late, mine_other + [to_core(a) for a in late]]
    others = [shift(pieces[1], "col", j) for j in (2, 3)]
    weights, normed_two = fence((weights, normed_two))

    rest = [gather_rows(late_others[0])]
    grads, *sums = feedforward(normed_two, grad_out, weights, PARTS)
    grads, sums, rest, others, normed_two_other, weights, middle, late_others = fence(
        (grads, sums, rest, others, normed_two_other, weights, middle, late_others)
    )
    own_sums = [sums]
    stacked = jnp.stack(others)
    early = (
        [jnp.concatenate([own_rows[0][1:], late_others[0][None], stacked])] if row_size * SPLIT_MODEL <= model else []
    )
    stacked, early, own_rows = fence((stacked, early, own_rows))
    rest.append(gather_rows(stacked))
    early_other = [to_core(a) for a in early]
    grads, *sums = feedforward(normed_two_other, grad_out_other, weights, PARTS, grads)
    grads, sums, rest, early, early_other, own_rows = fence((grads, sums, rest, early, early_other, own_rows))
    other_sums = [sums]
    n = len(early)
    late = merge([jnp.concatenate([a[1:], b[None], c]) for a, b, c in zip(own_rows[n:], rest[0][n:], rest[1][n:])])
    mine, other = by_rows(grads[0]), by_rows(grads[1])
    late, other[1:] = fence((late, other[1:]))
    late_other = [to_core(a) for a in late]
    arrived = [to_core(a) for a in other[1:]]
    mine, other[0], late, late_other, arrived = fence((mine, other[0], late, late_other, arrived))
    weights = [early + late, early_other + late_other]
    middle_columns = lambda a: a[1:3]
    outer_columns = lambda a: jnp.stack([a[0], a[3]])
    sent = [[small(cut(a), cut(b)) for a, b in zip(mine[1:], arrived)] for cut in (middle_columns, outer_columns)]
    weights, mine[0], other[0], sent, normed_two_other = fence((weights, mine[0], other[0], sent, normed_two_other))
    rows = [shift(a, "row", i) for i, a in enumerate(sent[0], 1)]
    arrived = to_core(other[0])
    grads, *sums = feedforward(normed_two_other, grad_out_other, weights, PARTS)
    grads, sums, rows, mine[0], arrived, sent, weights = fence((grads, sums, rows, mine[0], arrived, sent, weights))
    other_sums.append(sums)

    blocks = [small(mine[0][j], arrived[j], *[r[j - 1] for r in rows]) for j in (1, 2)]
    sums = small(*[p[1] for p in other_sums])
    sums, blocks, grads, other_sums, own_sums = fence((sums, blocks, grads, other_sums, own_sums))
    grad_two_other = to_y(sums)
    rows = [shift(a, "row", i) for i, a in enumerate(sent[1], 1)]
    along = [shift(blocks[1], "col", -2)]
    grads, *sums = feedforward(normed_two, grad_out, weights, PARTS, grads)
    grads, sums, rows, along, blocks, mine[0], arrived, grad_two_other = fence(
        (grads, sums, rows, along, blocks, mine[0], arrived, grad_two_other)
    )
    along.append(shift(blocks[0], "col", -1))
    own_sums.append(sums)
    last, other = by_rows(grads[0]), by_rows(grads[1])
    last_rows = [to_core(a) for a in other[1:]]
    kept = total(grad_two_other, *[p[1] for p in own_sums])
    grad_middle, gain_two_term = norm_back(middle, gain_two, kept)
    grad_middle = grad_middle + grad_out.astype(F32)
    branch = grad_middle.astype(BF)
    last_rows, branch, grad_middle, gain_two_term, last, other[0], along = fence(
        (last_rows, branch, grad_middle, gain_two_term, last, other[0], along)
    )
    branch_other = to_pair(branch)
    sent = [[small(cut(a), cut(b)) for a, b in zip(last[1:], last_rows)] for cut in (middle_columns, outer_columns)]
    last_rows = [shift(a, "row", i) for i, a in enumerate(sent[0], 1)]
    last_core = to_core(other[0])
    out_kept = middle + total(*[p[0] for p in own_sums])
    out_sent = small(*[p[0] for p in other_sums])
    blocks = [small(mine[0][j], arrived[j], *[r[j // 3] for r in rows]) for j in (0, 3)]
    branch, branch_other, last_core, last_rows, sent, out_kept, out_sent, blocks, grad_middle, gain_two_term = fence(
        (branch, branch_other, last_core, last_rows, sent, out_kept, out_sent, blocks, grad_middle, gain_two_term)
    )

    along += [blocks[0], shift(blocks[1], "col", -3)]
    out_other = to_y(out_sent)
    outer_rows = [shift(a, "row", i) for i, a in enumerate(sent[1], 1)]
    branch_all = in_sequence(branch, branch_other)
    grad_attended = dot_nt(branch_all, weight_projection).astype(BF)
    count = col_size // 2
    wide = count * GROUP
    to_rows = lambda g: [shift(g[i], "row", i) for i in range(1, row_size)]

    def qkv_halves(part):
        if split % LANES == 0:
            return gradient_halves(core, normed_all, part, split)
        g = dot_tn(normed_all, part).astype(BF).reshape(row_size, 2, split, wide)
        return jnp.stack([pick(g, core, 1), pick(g, 1 - core, 1)])

    first = attention_backward(qkv, grad_attended, spread_back, *tables, 0, count)
    first, along, outer_rows, grad_attended, branch_all = fence((first, along, outer_rows, grad_attended, branch_all))
    rows = [[m[0] for m in outer_rows], [m[0] for m in last_rows], [m[1] for m in last_rows], [m[1] for m in outer_rows]]
    blocks = [small(last[0][j], last_core[j], *rows[j]) for j in range(col_size)]
    blocks, grad_attended, first, branch_all = fence((blocks, grad_attended, first, branch_all))
    last_along = [blocks[0]] + [shift(blocks[j], "col", -j) if j & 1 else blocks[j] for j in range(1, col_size)]
    projection_halves = gradient_halves(core, attended, branch_all, LANES, True)
    first_halves = qkv_halves(first)
    second = attention_backward(qkv, grad_attended, spread_back, *tables, count, count)
    second, last_along, along, first_halves, projection_halves, out_other = fence(
        (second, last_along, along, first_halves, projection_halves, out_other)
    )

    product = lambda rows: sum(
        dot_nt(rows(part), weight_qkv[:, k * wide : (k + 1) * wide]) for k, part in enumerate((first, second))
    )
    first_other, projection_other = to_core(first_halves[1]), to_core(projection_halves[1])
    sent = product(lambda a: rows_of(a, (1 - parity) * own)).astype(BF)
    second_halves = qkv_halves(second)
    first_part = small(*along)
    sent, second_halves, first_part, last_along, first_other, projection_other, first_halves, projection_halves = fence(
        (sent, second_halves, first_part, last_along, first_other, projection_other, first_halves, projection_halves)
    )
    half = own // 2
    grad_one_other = [to_pair(sent[:half])]
    last_along[2] = shift(last_along[2], "col", -2)
    first_rows = small(first_halves[0], first_other)
    g = small(projection_halves[0], projection_other)
    sent, first_rows, g, second_halves = fence((sent, first_rows, g, second_halves))
    first_rows = [first_rows[0]] + to_rows(first_rows)
    projection_rows = [g[:, :, i * block : (i + 1) * block] for i in range(row_size)]
    projection_rows[1:] = to_rows(projection_rows)
    second_other = to_core(second_halves[1])
    kept = product(lambda a: rows_of(a, parity * own))
    sent, grad_one_other, last_along, first_rows, projection_rows, second_halves, second_other, first_part, kept = fence(
        (sent, grad_one_other, last_along, first_rows, projection_rows, second_halves, second_other, first_part, kept)
    )

    second_rows = small(second_halves[0], second_other)
    first_rows = small(*first_rows)
    g = small(*projection_rows)
    both_parts = jnp.stack([first_part, small(*last_along)])
    second_rows, first_rows, both_parts, g = fence((second_rows, first_rows, both_parts, g))
    second_rows = [second_rows[0]] + to_rows(second_rows)
    first_rows = shift(first_rows, "col", 2)
    projection_far = shift(g[:2], "col", 2)
    grad_one_other.append(to_pair(sent[half:]))
    both_parts_other = to_y(both_parts)
    second_rows, first_rows, projection_far, grad_one_other, both_parts, both_parts_other, g = fence(
        (second_rows, first_rows, projection_far, grad_one_other, both_parts, both_parts_other, g)
    )

    both = combine(second_rows, first_rows, g[2:], projection_far)
    both, both_parts, both_parts_other, grad_one_other = fence((both, both_parts, both_parts_other, grad_one_other))
    both_other = to_y(both)
    both_parts = halves(y == 0, both_parts[:, None], both_parts_other[:, None], 1)
    both_parts_core = to_core(both_parts)
    arrived = jnp.concatenate(grad_one_other).astype(F32)
    grad_inputs, gain_one_term = norm_back(inputs.astype(F32), gain_one, kept + arrived)
    grad_inputs = unrel((grad_inputs + grad_middle).astype(BF))
    gains = unrel(jnp.stack([gain_one_term, gain_two_term]))
    for axis, n in (("row", row_size), ("col", col_size)):
        bit = 1
        while bit < n:
            gains = gains + lax.ppermute(gains, axis, [(i, i ^ bit) for i in range(n)])
            bit *= 2
    gains = gains + swap(gains, "dp", 1)
    gate_up_grad, down_grad = place(
        jnp.where(core == 0, both_parts, both_parts_core), jnp.where(core == 0, both_parts_core, both_parts)
    )
    output = unrel((out_kept + out_other.astype(F32)).astype(BF))
    both, both_other, gate_up_grad, down_grad, gains, output, grad_inputs = fence(
        (both, both_other, gate_up_grad, down_grad, gains, output, grad_inputs)
    )
    both = small(both, both_other)
    both_other = to_core(both)
    gains = gains + swap(gains, "dp", 2)
    attention_gain_grad, feedforward_gain_grad = gains[0], gains[1]
    query_grad, key_value_grad, projection_grad = place_attention(
        jnp.where(core == 0, both, both_other), jnp.where(core == 0, both_other, both), block
    )
    return (
        output,
        grad_inputs,
        attention_gain_grad,
        feedforward_gain_grad,
        query_grad,
        key_value_grad,
        projection_grad,
        gate_up_grad,
        down_grad,
    )


def solution(mesh):
    sizes = tuple(mesh.shape[name] for name in ("dp", "row", "col"))
    return jax.shard_map(
        functools.partial(per_device, sizes=sizes),
        mesh=mesh,
        in_specs=(
            P(("dp", "row", "col"), None),
            P(),
            P(),
            P("row", "col"),
            P("row", None, "col"),
            P("col", "row"),
            P("row", None, "col"),
            P("col", "row"),
            P(("dp", "row", "col"), None),
        ),
        out_specs=(
            P(("dp", "row", "col"), None),
            P(("dp", "row", "col"), None),
            P(),
            P(),
            P("row", "col"),
            P("row", None, "col"),
            P("col", "row"),
            P("row", None, "col"),
            P("col", "row"),
        ),
        check_vma=False,
    )
```

```python
import functools
import math

import jax
import jax.numpy as jnp
from jax import lax
from jax.experimental import pallas as pl
from jax.experimental.pallas import tpu as pltpu
from jax.sharding import PartitionSpec as P

QUERY_HEADS = 16
KEY_VALUE_HEADS = 8
HEAD_DIM = 96
SEQUENCE_TOKENS = 1024

eps = 1e-05
rope_base = 100000.0

BF = jnp.bfloat16
F32 = jnp.float32

HALF = HEAD_DIM // 2
LANES = 128
GROUP = 4 * HEAD_DIM
GROUP_LANES = 4 * LANES
BLOCK = 256
SCALE = HEAD_DIM ** (-0.5)
PARTS = 2
QUICK = pl.CostEstimate(flops=1, bytes_accessed=1, transcendentals=0)
SPLIT_MODEL = 768


def dot(a, b):
    return lax.dot_general(a, b, (((1,), (0,)), ((), ())), preferred_element_type=F32)


def dot_nt(a, b):
    return lax.dot_general(a, b, (((1,), (1,)), ((), ())), preferred_element_type=F32)


def dot_tn(a, b):
    return lax.dot_general(a, b, (((0,), (0,)), ((), ())), preferred_element_type=F32)


def exponentials_t(keys, queries, block):
    s = dot_nt(keys, queries)
    here = s[block * BLOCK :]
    later = lax.broadcasted_iota(jnp.int32, here.shape, 0) > lax.broadcasted_iota(jnp.int32, here.shape, 1)
    here = jnp.where(later, -1e30, here)
    s = jnp.concatenate([s[: block * BLOCK], here], axis=0) if block else here
    top = jnp.max(s, axis=0, keepdims=True)
    e = jnp.exp2((s - top) * (SCALE * math.log2(math.e)))
    return e, 1.0 / jnp.sum(e, axis=0, keepdims=True)


def attention_forward_kernel(n1_ref, w_ref, spread_ref, cos_ref, sin_ref, qkv_ref, o_ref):
    w = dot(w_ref[...], spread_ref[...]).astype(BF)
    h = dot(n1_ref[...], w)
    cos, sin = cos_ref[...], sin_ref[...]
    for part in range(4):
        c = h[:, part * LANES : (part + 1) * LANES]
        if part < 3:
            c = c * cos + pltpu.roll(c, LANES // 2, 1) * sin
        qkv_ref[:, part * LANES : (part + 1) * LANES] = c.astype(BF)
    v_t = h[:, 3 * LANES :].T.astype(BF)
    for head in range(2):
        lanes = slice(head * LANES, (head + 1) * LANES)
        for block in range(SEQUENCE_TOKENS // BLOCK):
            rows = slice(block * BLOCK, (block + 1) * BLOCK)
            length = (block + 1) * BLOCK
            e, inverse = exponentials_t(qkv_ref[:length, 2 * LANES : 3 * LANES], qkv_ref[rows, lanes], block)
            o_t = dot(v_t[:, :length], e.astype(BF)) * inverse
            o_ref[rows, lanes] = o_t.T.astype(BF)


def attention_backward_kernel(qkv_ref, do_ref, gather_ref, cos_ref, sin_ref, out_ref, dk_ref, dv_ref, dq_ref, d_ref):
    cos, sin = cos_ref[...], sin_ref[...]

    def unrotate(c):
        c = c * SCALE
        return (c * cos - pltpu.roll(c, LANES // 2, 1) * sin).astype(BF)

    k_t = qkv_ref[:, 2 * LANES : 3 * LANES].astype(F32).T.astype(BF)
    dk_ref[...] = jnp.zeros_like(dk_ref)
    dv_ref[...] = jnp.zeros_like(dv_ref)
    for head in range(2):
        lanes = slice(head * LANES, (head + 1) * LANES)
        for block in range(SEQUENCE_TOKENS // BLOCK):
            rows = slice(block * BLOCK, (block + 1) * BLOCK)
            length = (block + 1) * BLOCK
            q = qkv_ref[rows, lanes]
            do = do_ref[rows, lanes]
            e, inverse = exponentials_t(qkv_ref[:length, 2 * LANES : 3 * LANES], q, block)
            p = e * inverse
            dp = dot_nt(qkv_ref[:length, 3 * LANES :], do)
            ds = (p * (dp - jnp.sum(p * dp, axis=0, keepdims=True))).astype(BF)
            dv_ref[:length, :] += dot(p.astype(BF), do)
            dk_ref[:length, :] += dot(ds, q)
            dq_ref[rows, :] = dot(k_t[:, :length], ds).T
        d_ref[:, lanes] = unrotate(dq_ref[...])
    d_ref[:, 2 * LANES : 3 * LANES] = unrotate(dk_ref[...])
    d_ref[:, 3 * LANES :] = dv_ref[...].astype(BF)
    out_ref[...] = dot(d_ref[...], gather_ref[...]).astype(BF)


def rotary_tables():
    positions = jnp.arange(SEQUENCE_TOKENS).astype(F32)
    inverse_freq = jnp.exp(jnp.arange(HALF).astype(F32) * (-2.0 * math.log(rope_base) / HEAD_DIM))
    angles = positions[:, None] * inverse_freq[None, :]
    gap = ((0, 0), (0, LANES // 2 - HALF))
    cos, sin = jnp.pad(jnp.cos(angles), gap), jnp.pad(jnp.sin(angles), gap)
    return jnp.concatenate([cos, cos], axis=1), jnp.concatenate([-sin, sin], axis=1)


def spread_matrix():
    src = lax.broadcasted_iota(jnp.int32, (GROUP, GROUP_LANES), 0)
    lane = lax.broadcasted_iota(jnp.int32, (GROUP, GROUP_LANES), 1)
    head, comp = src // HEAD_DIM, src % HEAD_DIM
    place = head * LANES + jnp.where(comp < HALF, comp, comp + LANES // 2 - HALF)
    return (place == lane).astype(BF)


def attention_forward(n1, w, spread, cos, sin):
    tokens, width = n1.shape
    groups = w.shape[1] // GROUP
    whole = lambda a: pl.BlockSpec(a.shape, lambda j: (0, 0))
    return pl.pallas_call(
        attention_forward_kernel,
        grid=(groups,),
        in_specs=[
            whole(n1),
            pl.BlockSpec((width, GROUP), lambda j: (0, j)),
            whole(spread),
            whole(cos),
            whole(sin),
        ],
        out_specs=[
            pl.BlockSpec((tokens, GROUP_LANES), lambda j: (0, j)),
            pl.BlockSpec((tokens, 2 * LANES), lambda j: (0, j)),
        ],
        out_shape=[
            jax.ShapeDtypeStruct((tokens, groups * GROUP_LANES), BF),
            jax.ShapeDtypeStruct((tokens, groups * 2 * LANES), BF),
        ],
        compiler_params=pltpu.CompilerParams(vmem_limit_bytes=48 * 1024 * 1024),
        cost_estimate=QUICK,
        name="attention_forward",
    )(n1, w, spread, cos, sin)


def attention_backward(qkv, do, gather, cos, sin, first, groups):
    tokens = qkv.shape[0]
    whole = lambda a: pl.BlockSpec(a.shape, lambda j: (0, 0))
    return pl.pallas_call(
        attention_backward_kernel,
        grid=(groups,),
        in_specs=[
            pl.BlockSpec((tokens, GROUP_LANES), lambda j: (0, first + j)),
            pl.BlockSpec((tokens, 2 * LANES), lambda j: (0, first + j)),
            whole(gather),
            whole(cos),
            whole(sin),
        ],
        out_specs=pl.BlockSpec((tokens, GROUP), lambda j: (0, j)),
        out_shape=jax.ShapeDtypeStruct((tokens, groups * GROUP), BF),
        scratch_shapes=[
            pltpu.VMEM((tokens, LANES), F32),
            pltpu.VMEM((tokens, LANES), F32),
            pltpu.VMEM((tokens, LANES), F32),
            pltpu.VMEM((tokens, GROUP_LANES), BF),
        ],
        compiler_params=pltpu.CompilerParams(vmem_limit_bytes=48 * 1024 * 1024),
        cost_estimate=QUICK,
        name="attention_backward",
    )(qkv, do, gather, cos, sin)


def feedforward_kernel(col_step, sub, rows_of, n2_ref, cot_ref, *refs):
    *blocks, out_bf_ref, dn2_bf_ref, out_ref, dn2_ref, h_ref, dgu_ref = refs
    sides = [blocks[k : k + rows_of] for k in range(0, len(blocks), rows_of)]
    weights, earlier, grads = sides[:2], sides[2:-2], sides[-2:]
    step, half = pl.program_id(0), pl.num_programs(0) // 2
    width = n2_ref.shape[1] // rows_of
    cut = [slice(i * width, (i + 1) * width) for i in range(rows_of)]

    @pl.when(step == 0)
    def _():
        out_ref[...] = jnp.zeros_like(out_ref)
        dn2_ref[...] = jnp.zeros_like(dn2_ref)

    def rows(ref, first, last):
        return jnp.concatenate([ref[c, first:last] for c in range(col_step)], axis=0)

    def work(whose):
        gate_up = [rows(r, 0, 2 * sub) for r in weights[whose]]
        down = [rows(r, 2 * sub, 3 * sub) for r in weights[whose]]
        dh = sum(dot_nt(cot_ref[:, cut[i]], down[i]) for i in range(rows_of))
        gu = sum(dot_nt(n2_ref[:, cut[i]], gate_up[i]) for i in range(rows_of))
        for c in range(col_step):
            gate, up = (gu[:, (2 * c + k) * sub : (2 * c + k + 1) * sub] for k in range(2))
            sig = jax.nn.sigmoid(gate)
            silu = gate * sig
            lanes = slice(c * sub, (c + 1) * sub)
            part = dh[:, lanes]
            h_ref[:, lanes] = (silu * up).astype(BF)
            dgu_ref[:, 2 * c * sub : (2 * c + 1) * sub] = (part * up * (sig + silu * (1 - sig))).astype(BF)
            dgu_ref[:, (2 * c + 1) * sub : (2 * c + 2) * sub] = (part * silu).astype(BF)
        hidden, dgu = h_ref[...], dgu_ref[...]
        hidden_t, dgu_t = hidden.T, dgu.T
        for i in range(rows_of):
            dn2_ref[:, cut[i]] += dot(dgu, gate_up[i])
            out_ref[:, cut[i]] += dot(hidden, down[i])
            gate_up_grad = dot(dgu_t, n2_ref[:, cut[i]])
            down_grad = dot(hidden_t, cot_ref[:, cut[i]])
            for c in range(col_step):
                new = (gate_up_grad[2 * c * sub : 2 * (c + 1) * sub], down_grad[c * sub : (c + 1) * sub])
                for part, here in zip(new, (slice(2 * sub), slice(2 * sub, None))):
                    if earlier:
                        part = part + earlier[whose][i][c, here].astype(F32)
                    grads[whose][i][c, here] = part.astype(BF)

    pl.when(step < half)(lambda: work(1))
    pl.when(step >= half)(lambda: work(0))

    @pl.when(step == 2 * half - 1)
    def _():
        out_bf_ref[...] = out_ref[...].astype(BF)
        dn2_bf_ref[...] = dn2_ref[...].astype(BF)


def feedforward(n2, cot, weights, col_step, earlier=()):
    tokens, model = n2.shape
    rows_of = len(weights[0])
    columns, rows, width = weights[0][0].shape
    sub = rows // 3
    half = columns // col_step
    once = lambda a: pl.BlockSpec(a.shape, lambda s: (0, 0), pipeline_mode=pl.Buffered(1))
    place = [lambda s: (jnp.maximum(s - half, 0), 0, 0), lambda s: (jnp.minimum(s, half - 1), 0, 0)]
    flat = [a for side in weights for a in side]
    specs = [pl.BlockSpec((col_step, rows, width), place[whose]) for whose in range(2) for _ in range(rows_of)]
    earlier = [a for side in earlier for a in side]
    total = jax.ShapeDtypeStruct((tokens, model), BF)
    outs = pl.pallas_call(
        functools.partial(feedforward_kernel, col_step, sub, rows_of),
        grid=(2 * half,),
        in_specs=[once(n2), once(cot)] + specs + (specs if earlier else []),
        out_specs=specs + [once(total), once(total)],
        out_shape=[jax.ShapeDtypeStruct(a.shape, BF) for a in flat] + [total, total],
        scratch_shapes=[
            pltpu.VMEM((tokens, model), F32),
            pltpu.VMEM((tokens, model), F32),
            pltpu.VMEM((tokens, col_step * sub), BF),
            pltpu.VMEM((tokens, 2 * col_step * sub), BF),
        ],
        compiler_params=pltpu.CompilerParams(vmem_limit_bytes=60 * 1024 * 1024),
        cost_estimate=QUICK,
        name="feedforward",
    )(n2, cot, *flat, *earlier)
    return [list(outs[:rows_of]), list(outs[rows_of : 2 * rows_of])], outs[2 * rows_of], outs[2 * rows_of + 1]


def place_kernel(*refs):
    cores, (gate_up_ref, down_ref) = refs[:2], refs[2:]
    parts, _, rows, block = cores[0].shape
    sub = rows // 3
    for core, ref in enumerate(cores):
        for y in range(2):
            for k in range(parts):
                tile = (2 * y + core) * parts + k
                for half in range(2):
                    piece = ref[k, y, half * sub : (half + 1) * sub].astype(F32)
                    gate_up_ref[pl.ds(2 * tile + half, block, stride=8 * parts), :] = piece.T
                down_ref[tile * sub : (tile + 1) * sub] = ref[k, y, 2 * sub :].astype(F32)


def place(first, second):
    parts, _, rows, block = first.shape
    sub = rows // 3
    tiles = 4 * parts
    gate_up, down = pl.pallas_call(
        place_kernel,
        out_shape=[
            jax.ShapeDtypeStruct((block * tiles * 2, sub), F32),
            jax.ShapeDtypeStruct((tiles * sub, block), F32),
        ],
        compiler_params=pltpu.CompilerParams(vmem_limit_bytes=48 * 1024 * 1024),
        cost_estimate=QUICK,
        name="place",
    )(first, second)
    return gate_up.reshape(block, tiles, 2, sub).transpose(0, 2, 1, 3).reshape(block, 2, -1), down


def combine_kernel(*refs):
    out_ref = refs[-1]
    *rows, mine, other = refs[:-1]
    qkv = sum(r[...].astype(F32) for r in rows).astype(BF)
    heads = (mine[...].astype(F32) + other[...].astype(F32)).astype(BF)
    split = qkv.shape[0]
    for p in range(2):
        out_ref[p, :split] = qkv[:, p * GROUP : (p + 1) * GROUP]
        for n in range(2 * split // GROUP):
            here = slice(split + n * HEAD_DIM, split + (n + 1) * HEAD_DIM)
            out_ref[p, here] = heads[p, :, n * GROUP : (n + 1) * GROUP]


def combine(rows, arrived, heads, heads_arrived):
    split, block = rows[0].shape[0], heads.shape[2]
    if block % GROUP:
        qkv = sum(r.astype(F32) for r in rows + [arrived])
        heads = heads.astype(F32) + heads_arrived.astype(F32)
        parts = [jnp.concatenate([qkv[:, p * GROUP : (p + 1) * GROUP], heads[p].reshape(-1, GROUP)]) for p in range(2)]
        return jnp.stack(parts).astype(BF)
    return pl.pallas_call(
        combine_kernel,
        out_shape=jax.ShapeDtypeStruct((2, split + HEAD_DIM * block // GROUP, GROUP), BF),
        compiler_params=pltpu.CompilerParams(vmem_limit_bytes=32 * 1024 * 1024),
        cost_estimate=QUICK,
        name="combine",
    )(*rows, arrived, heads, heads_arrived)


def place_attention_kernel(*refs):
    cores, (query_ref, pair_ref, projection_ref) = refs[:2], refs[2:]
    block = query_ref.shape[0]
    rows = block // 2
    for core, ref in enumerate(cores):
        here = slice(core * rows, (core + 1) * rows)
        for parity in range(2):
            g = ref[parity, :rows].astype(F32)
            query_ref[here, 2 * parity * HEAD_DIM : 2 * (parity + 1) * HEAD_DIM] = g[:, : 2 * HEAD_DIM]
            g = g.T
            for k in range(2):
                pair_ref[k, parity * HEAD_DIM : (parity + 1) * HEAD_DIM, here] = g[(2 + k) * HEAD_DIM : (3 + k) * HEAD_DIM]
            head = slice((2 * parity + core) * HEAD_DIM, (2 * parity + core + 1) * HEAD_DIM)
            for k in range(block // GROUP):
                piece = ref[parity, rows + k * HEAD_DIM : rows + (k + 1) * HEAD_DIM]
                projection_ref[head, k * GROUP : (k + 1) * GROUP] = piece.astype(F32)


def place_attention(first, second, block):
    folded = block % GROUP != 0
    query, pair, projection = pl.pallas_call(
        place_attention_kernel,
        out_shape=[
            jax.ShapeDtypeStruct((block, 4 * HEAD_DIM), F32),
            jax.ShapeDtypeStruct((2, 2 * HEAD_DIM, block), F32),
            jax.ShapeDtypeStruct((4 * HEAD_DIM, block), F32),
        ],
        compiler_params=pltpu.CompilerParams(vmem_limit_bytes=32 * 1024 * 1024),
        cost_estimate=QUICK,
        name="place_attention",
    )(first, second)
    if folded:
        both = jnp.stack([a[:, block // 2 :].reshape(2, HEAD_DIM, block) for a in (first, second)], axis=1)
        projection = both.astype(F32).reshape(-1, block)
    return query, pair.transpose(2, 0, 1), projection


def assemble_kernel(groups, core_ref, *refs):
    pieces, (qkv_ref, projection_ref) = refs[:-2], refs[-2:]
    first = core_ref[0] == 0
    blocks = len(pieces) // groups
    rows = qkv_ref.shape[0] // (2 * blocks)
    projection_ref[...] = jnp.zeros_like(projection_ref)
    for i in range(blocks):
        for k in range(groups // 2):
            mine, other = pieces[i * groups + 2 * k], pieces[i * groups + 2 * k + 1]
            for p in range(2):
                a, b = mine[p], other[p]
                group = 2 * k + p
                for core, piece in enumerate((jnp.where(first, a, b), jnp.where(first, b, a))):
                    start = (2 * i + core) * rows
                    qkv_ref[start : start + rows, group * GROUP : (group + 1) * GROUP] = piece[:rows]
                    place = group * 2 * LANES + core * LANES
                    for n in range(2 * rows // GROUP):
                        lanes = slice(2 * i * rows + n * GROUP, 2 * i * rows + (n + 1) * GROUP)
                        head = piece[rows + n * HEAD_DIM : rows + (n + 1) * HEAD_DIM]
                        projection_ref[place : place + HALF, lanes] = head[:HALF]
                        projection_ref[place + LANES // 2 : place + LANES // 2 + HALF, lanes] = head[HALF:]


def assemble(core, pieces, model):
    groups = len(pieces[0])
    flat = [a for row in pieces for a in row]
    return pl.pallas_call(
        functools.partial(assemble_kernel, groups),
        in_specs=[pl.BlockSpec(memory_space=pltpu.SMEM)] + [pl.BlockSpec(memory_space=pltpu.VMEM)] * len(flat),
        out_shape=[
            jax.ShapeDtypeStruct((model, groups * GROUP), BF),
            jax.ShapeDtypeStruct((groups * 2 * LANES, model), BF),
        ],
        compiler_params=pltpu.CompilerParams(vmem_limit_bytes=48 * 1024 * 1024),
        cost_estimate=QUICK,
        name="assemble",
    )(core.astype(jnp.int32)[None], *flat)


def halves_kernel(gap, core_ref, a_ref, b_ref, out_ref):
    g = dot_tn(a_ref[...], b_ref[...]).astype(BF)
    if gap:
        out_ref[0, 0, :HALF] = g[:HALF]
        out_ref[0, 0, HALF:] = g[LANES // 2 : LANES // 2 + HALF]
    else:
        out_ref[0, 0] = g


def gradient_halves(core, a, b, rows, gap=False):
    tokens, width = a.shape
    blocks = width // (2 * rows)
    kept = HEAD_DIM if gap else rows
    columns = b.shape[1]
    return pl.pallas_call(
        functools.partial(halves_kernel, gap),
        grid_spec=pltpu.PrefetchScalarGridSpec(
            num_scalar_prefetch=1,
            grid=(2, blocks),
            in_specs=[
                pl.BlockSpec((tokens, rows), lambda h, i, core: (0, 2 * i + (core[0] + h) % 2)),
                pl.BlockSpec(b.shape, lambda h, i, core: (0, 0)),
            ],
            out_specs=pl.BlockSpec((1, 1, kept, columns), lambda h, i, core: (h, i, 0, 0)),
        ),
        out_shape=jax.ShapeDtypeStruct((2, blocks, kept, columns), BF),
        compiler_params=pltpu.CompilerParams(vmem_limit_bytes=48 * 1024 * 1024),
        cost_estimate=QUICK,
        name="gradient_halves",
    )(core.astype(jnp.int32)[None], a, b)


def inverse_rms(field):
    return lax.rsqrt(jnp.mean(field * field, axis=-1, keepdims=True) + eps)


def norm_back(field, gain, grad):
    r = inverse_rms(field)
    scaled = gain * grad
    inner = jnp.mean(field * scaled, axis=-1, keepdims=True)
    return r * scaled - field * (r * r * r * inner), jnp.sum(grad * field * r, axis=0)


def norm_back_kernel(field_ref, gain_ref, skip_ref, *refs):
    *terms, out_ref, rounded_ref, gain_grad_ref = refs
    field = field_ref[...]
    grad = sum(t[...].astype(F32) for t in terms)
    r = inverse_rms(field)
    scaled = gain_ref[...] * grad
    inner = jnp.mean(field * scaled, axis=-1, keepdims=True)
    out = skip_ref[...].astype(F32) + r * scaled - field * (r * r * r * inner)
    out_ref[...] = out
    rounded_ref[...] = out.astype(BF)

    @pl.when(pl.program_id(0) == 0)
    def _():
        gain_grad_ref[...] = jnp.zeros_like(gain_grad_ref)

    gain_grad_ref[...] += jnp.sum(grad * (field * r), axis=0, keepdims=True)


def norm_back_rows(field, gain, skip, terms):
    tokens, model = field.shape
    rows = 128
    block = pl.BlockSpec((rows, model), lambda i: (i, 0))
    line = pl.BlockSpec((1, model), lambda i: (0, 0))
    out, rounded, gain_grad = pl.pallas_call(
        norm_back_kernel,
        grid=(tokens // rows,),
        in_specs=[block, line, block] + [block] * len(terms),
        out_specs=[block, block, line],
        out_shape=[
            jax.ShapeDtypeStruct(field.shape, F32),
            jax.ShapeDtypeStruct(field.shape, BF),
            jax.ShapeDtypeStruct((1, model), F32),
        ],
        compiler_params=pltpu.CompilerParams(vmem_limit_bytes=60 * 1024 * 1024),
        cost_estimate=QUICK,
        name="norm_back",
    )(field, gain[None], skip, *terms)
    return out, rounded, gain_grad[0]


def halves(first_is_mine, mine, other, axis):
    return jnp.where(
        first_is_mine, jnp.concatenate([mine, other], axis), jnp.concatenate([other, mine], axis)
    )


def per_device(
    tokens,
    attention_gain,
    feedforward_gain,
    query_weight,
    key_value_matrix,
    projection_weight,
    gate_up_weight,
    down_weight,
    cotangent,
    *,
    sizes,
):
    dp_size, row_size, col_size = sizes
    x, z, d = lax.axis_index("row"), lax.axis_index("col"), lax.axis_index("dp")
    core, y, parity = d % 2, d // 2, z % 2
    model = tokens.shape[1]
    own = tokens.shape[0]
    block = model // row_size
    hidden_block = down_weight.shape[0]
    sub = hidden_block // 4 // PARTS

    def swap(a, axis, bit):
        n = {"dp": dp_size, "col": col_size}[axis]
        return lax.ppermute(a, axis, [(i, i ^ bit) for i in range(n)])

    def to_core(a):
        return swap(a, "dp", 1)

    def to_y(a):
        return swap(a, "dp", 2)

    def to_pair(a):
        return swap(a, "col", 1)

    def shift(a, axis, by):
        n = {"row": row_size, "col": col_size}[axis]
        return lax.ppermute(a, axis, [(i, (i + by) % n) for i in range(n)])

    def rel(a):
        if row_size == 2:
            return jnp.where(x == 0, a, jnp.concatenate([a[..., block:], a[..., :block]], axis=-1))
        return lax.dynamic_slice_in_dim(jnp.concatenate([a, a], axis=-1), x * block, model, a.ndim - 1)

    def unrel(a):
        if row_size == 2:
            return rel(a)
        return lax.dynamic_slice_in_dim(
            jnp.concatenate([a, a], axis=-1), (row_size - x) % row_size * block, model, a.ndim - 1
        )

    def gather_rows(piece):
        return [piece] + [shift(piece, "row", -i) for i in range(1, row_size)]

    def pick(a, index, axis):
        return lax.dynamic_index_in_dim(a, index, axis, keepdims=False)

    def merge(rows):
        return rows if len(rows) * SPLIT_MODEL <= model else [jnp.concatenate(rows, axis=2)]

    def by_rows(blocks):
        return list(blocks) if len(blocks) == row_size else jnp.split(blocks[0], row_size, axis=2)

    fence = lax.optimization_barrier

    def fold(a):
        if block % GROUP:
            return a.reshape(-1, GROUP)
        return jnp.concatenate([a[:, k : k + GROUP] for k in range(0, block, GROUP)])

    def unfold(a):
        if block % GROUP:
            return a.reshape(a.shape[:-2] + (HEAD_DIM, block))
        return jnp.concatenate([a[..., k : k + HEAD_DIM, :] for k in range(0, a.shape[-2], HEAD_DIM)], axis=-1)


    def total(*parts):
        return sum(part.astype(F32) for part in parts)

    def small(*parts):
        return total(*parts).astype(BF)

    def in_sequence(a, other):
        return halves(parity == 0, a, other, 0)

    def rows_of(a, first):
        return lax.dynamic_slice_in_dim(a, first, own, 0)

    query_blocks = query_weight.reshape(block, 2, 2 * HEAD_DIM)
    pair_blocks = key_value_matrix.reshape(block, 2, 2, HEAD_DIM)
    packed = jnp.concatenate([query_blocks, pair_blocks[:, 0], pair_blocks[:, 1]], axis=-1)
    packed = lax.dynamic_slice_in_dim(packed, core * (block // 2), block // 2, 0)
    head_rows = pick(projection_weight.reshape(2, 2, HEAD_DIM, block), core, 1)
    packed = jnp.stack([jnp.concatenate([packed[:, p], fold(head_rows[p])]) for p in range(2)])
    packed, tokens, cotangent, gate_up_weight, down_weight = fence(
        (packed, tokens, cotangent, gate_up_weight, down_weight)
    )
    far_packed = shift(packed, "col", 2)
    own_packed = gather_rows(packed)

    pieces = []
    for part in range(PARTS):
        start = ((2 * y + core) * PARTS + part) * sub
        gate_up = lax.dynamic_slice_in_dim(gate_up_weight, start, sub, 2).transpose(1, 2, 0).reshape(2 * sub, block)
        pieces.append(jnp.concatenate([gate_up, lax.dynamic_slice_in_dim(down_weight, start, sub, 0)]))
    gain_one, gain_two = rel(attention_gain), rel(feedforward_gain)
    inputs = rel(tokens)
    wide_inputs = inputs.astype(F32)
    normed = (wide_inputs * inverse_rms(wide_inputs) * gain_one).astype(BF)
    normed_other = to_pair(normed)
    tables = rotary_tables()
    spread = spread_matrix()
    spread_back = spread.T
    far_packed, own_packed, pieces, inputs, normed, normed_other, tables = fence(
        (far_packed, own_packed, pieces, inputs, normed, normed_other, tables)
    )

    far_rows = gather_rows(far_packed)
    own_cores = [to_core(a) for a in own_packed]
    others = [shift(pieces[0], "col", 1)]
    late_others = [shift(pieces[1], "col", 1)]
    normed_all = in_sequence(normed, normed_other)
    grad_out = rel(cotangent)
    far_rows, own_cores, own_packed, others, late_others, normed_all, spread, spread_back, grad_out, pieces = fence(
        (far_rows, own_cores, own_packed, others, late_others, normed_all, spread, spread_back, grad_out, pieces)
    )
    own_rows = gather_rows(jnp.stack(pieces))
    rest_near = gather_rows(others[0])
    far_cores = [to_core(a) for a in far_rows]
    others += [shift(pieces[0], "col", j) for j in range(2, col_size)]
    split = block // 2
    if split % LANES == 0:
        rows = [list(parts) for parts in zip(far_rows, far_cores, own_packed, own_cores)]
        weight_qkv, weight_projection = assemble(core, rows, model)
    else:
        pick_core = lambda a, b: halves(core == 0, a[:, None], b[:, None], 1)
        pairs = [
            jnp.concatenate([pick_core(*far), pick_core(*mine)])
            for far, mine in zip(zip(far_rows, far_cores), zip(own_packed, own_cores))
        ]
        weight_qkv = jnp.concatenate([jnp.concatenate([p[j, :, :split] for j in range(col_size)], axis=-1) for p in pairs])
        weight_qkv = weight_qkv.reshape(model, -1)
        heads = jnp.concatenate([unfold(p[:, :, split:]) for p in pairs], axis=-1)
        gap = jnp.zeros(heads.shape[:2] + (LANES // 2 - HALF, model), BF)
        weight_projection = jnp.concatenate(
            [heads[:, :, :HALF], gap, heads[:, :, HALF:], gap], axis=2
        ).reshape(-1, model)
    weight_qkv, weight_projection = fence((weight_qkv, weight_projection))

    qkv, attended = attention_forward(normed_all, weight_qkv, spread, *tables)
    qkv, attended, others, late_others, own_rows, grad_out, weight_projection, rest_near = fence(
        (qkv, attended, others, late_others, own_rows, grad_out, weight_projection, rest_near)
    )

    sent = dot(rows_of(attended, (1 - parity) * own), weight_projection).astype(BF)
    stacked = jnp.stack(others[1:])
    sent, stacked, attended, weight_projection = fence((sent, stacked, attended, weight_projection))
    arrived = to_pair(sent)
    rest = gather_rows(stacked)
    grad_out_other = to_y(grad_out)
    fine = row_size * SPLIT_MODEL <= model
    own_first = [a[0] for a in own_rows]
    kept = dot(rows_of(attended, parity * own), weight_projection)
    kept, stacked = fence((kept, stacked))
    mine = [jnp.concatenate([own_first[0][None], rest_near[0][None], stacked])] if fine else []
    mine_other = [to_core(a) for a in mine]
    kept, arrived, rest, mine, mine_other, pieces, own_rows, grad_out, grad_out_other = fence(
        (kept, arrived, rest, mine, mine_other, pieces, own_rows, grad_out, grad_out_other)
    )

    middle = inputs.astype(F32) + kept + arrived.astype(F32)
    normed_two = (middle * inverse_rms(middle) * gain_two).astype(BF)
    n = len(mine)
    late = merge([jnp.concatenate([a[None], b[None], c]) for a, b, c in zip(own_first[n:], rest_near[n:], rest[n:])])
    normed_two, middle, late = fence((normed_two, middle, late))
    normed_two_other = to_y(normed_two)
    weights = [mine + late, mine_other + [to_core(a) for a in late]]
    others = [shift(pieces[1], "col", j) for j in (2, 3)]
    weights, normed_two = fence((weights, normed_two))

    rest = [gather_rows(late_others[0])]
    grads, *sums = feedforward(normed_two, grad_out, weights, PARTS)
    grads, sums, rest, others, normed_two_other, weights, middle, late_others = fence(
        (grads, sums, rest, others, normed_two_other, weights, middle, late_others)
    )
    own_sums = [sums]
    stacked = jnp.stack(others)
    early = (
        [jnp.concatenate([own_rows[0][1:], late_others[0][None], stacked])] if row_size * SPLIT_MODEL <= model else []
    )
    stacked, early, own_rows = fence((stacked, early, own_rows))
    rest.append(gather_rows(stacked))
    early_other = [to_core(a) for a in early]
    grads, *sums = feedforward(normed_two_other, grad_out_other, weights, PARTS, grads)
    grads, sums, rest, early, early_other, own_rows = fence((grads, sums, rest, early, early_other, own_rows))
    other_sums = [sums]
    n = len(early)
    late = merge([jnp.concatenate([a[1:], b[None], c]) for a, b, c in zip(own_rows[n:], rest[0][n:], rest[1][n:])])
    mine, other = by_rows(grads[0]), by_rows(grads[1])
    late, other[1:] = fence((late, other[1:]))
    late_other = [to_core(a) for a in late]
    arrived = [to_core(a) for a in other[1:]]
    mine, other[0], late, late_other, arrived = fence((mine, other[0], late, late_other, arrived))
    weights = [early + late, early_other + late_other]
    middle_columns = lambda a: a[1:3]
    outer_columns = lambda a: jnp.stack([a[0], a[3]])
    sent = [[small(cut(a), cut(b)) for a, b in zip(mine[1:], arrived)] for cut in (middle_columns, outer_columns)]
    weights, mine[0], other[0], sent, normed_two_other = fence((weights, mine[0], other[0], sent, normed_two_other))
    rows = [shift(a, "row", i) for i, a in enumerate(sent[0], 1)]
    arrived = to_core(other[0])
    grads, *sums = feedforward(normed_two_other, grad_out_other, weights, PARTS)
    grads, sums, rows, mine[0], arrived, sent, weights = fence((grads, sums, rows, mine[0], arrived, sent, weights))
    other_sums.append(sums)

    blocks = [small(mine[0][j], arrived[j], *[r[j - 1] for r in rows]) for j in (1, 2)]
    sums = small(*[p[1] for p in other_sums])
    sums, blocks, grads, other_sums, own_sums = fence((sums, blocks, grads, other_sums, own_sums))
    grad_two_other = to_y(sums)
    rows = [shift(a, "row", i) for i, a in enumerate(sent[1], 1)]
    along = [shift(blocks[1], "col", -2)]
    grads, *sums = feedforward(normed_two, grad_out, weights, PARTS, grads)
    grads, sums, rows, along, blocks, mine[0], arrived, grad_two_other = fence(
        (grads, sums, rows, along, blocks, mine[0], arrived, grad_two_other)
    )
    near_block = blocks[0]
    own_sums.append(sums)
    last, other = by_rows(grads[0]), by_rows(grads[1])
    last_rows = [to_core(a) for a in other[1:]]
    terms = [grad_two_other] + [p[1] for p in own_sums]
    grad_middle, branch, gain_two_term = norm_back_rows(middle, gain_two, grad_out, terms)
    last_rows, branch, grad_middle, gain_two_term, last, other[0] = fence(
        (last_rows, branch, grad_middle, gain_two_term, last, other[0])
    )
    branch_other = to_pair(branch)
    sent = [[small(cut(a), cut(b)) for a, b in zip(last[1:], last_rows)] for cut in (middle_columns, outer_columns)]
    last_rows = [shift(a, "row", i) for i, a in enumerate(sent[0], 1)]
    last_core = to_core(other[0])
    blocks = [small(mine[0][j], arrived[j], *[r[j // 3] for r in rows]) for j in (0, 3)]
    blocks.append(near_block)
    branch, branch_other, last_core, last_rows, sent, own_sums, other_sums, blocks, grad_middle, gain_two_term = fence(
        (branch, branch_other, last_core, last_rows, sent, own_sums, other_sums, blocks, grad_middle, gain_two_term)
    )

    along += [blocks[0], shift(blocks[1], "col", -3), shift(blocks[2], "col", -1)]
    out_other = to_y(small(*[p[0] for p in other_sums]))
    outer_rows = [shift(a, "row", i) for i, a in enumerate(sent[1], 1)]
    branch_all = in_sequence(branch, branch_other)
    grad_attended = dot_nt(branch_all, weight_projection).astype(BF)
    count = col_size // 2
    wide = count * GROUP
    to_rows = lambda g: [shift(g[i], "row", i) for i in range(1, row_size)]

    def qkv_halves(part):
        if split % LANES == 0:
            return gradient_halves(core, normed_all, part, split)
        g = dot_tn(normed_all, part).astype(BF).reshape(row_size, 2, split, wide)
        return jnp.stack([pick(g, core, 1), pick(g, 1 - core, 1)])

    first = attention_backward(qkv, grad_attended, spread_back, *tables, 0, count)
    first, along, outer_rows, grad_attended, branch_all = fence((first, along, outer_rows, grad_attended, branch_all))
    rows = [[m[0] for m in outer_rows], [m[0] for m in last_rows], [m[1] for m in last_rows], [m[1] for m in outer_rows]]
    blocks = [small(last[0][j], last_core[j], *rows[j]) for j in range(col_size)]
    blocks, grad_attended, first, branch_all = fence((blocks, grad_attended, first, branch_all))
    last_along = [blocks[0]] + [shift(blocks[j], "col", -j) if j & 1 else blocks[j] for j in range(1, col_size)]
    projection_halves = gradient_halves(core, attended, branch_all, LANES, True)
    first_halves = qkv_halves(first)
    second = attention_backward(qkv, grad_attended, spread_back, *tables, count, count)
    second, last_along, along, first_halves, projection_halves, out_other = fence(
        (second, last_along, along, first_halves, projection_halves, out_other)
    )

    product = lambda rows: sum(
        dot_nt(rows(part), weight_qkv[:, k * wide : (k + 1) * wide]) for k, part in enumerate((first, second))
    )
    first_other, projection_other = to_core(first_halves[1]), to_core(projection_halves[1])
    sent = product(lambda a: rows_of(a, (1 - parity) * own)).astype(BF)
    second_halves = qkv_halves(second)
    first_part = small(*along)
    sent, second_halves, first_part, last_along, first_other, projection_other, first_halves, projection_halves = fence(
        (sent, second_halves, first_part, last_along, first_other, projection_other, first_halves, projection_halves)
    )
    half = own // 2
    grad_one_other = [to_pair(sent[:half])]
    last_along[2] = shift(last_along[2], "col", -2)
    first_rows = small(first_halves[0], first_other)
    g = small(projection_halves[0], projection_other)
    sent, first_rows, g, second_halves, own_sums = fence((sent, first_rows, g, second_halves, own_sums))
    out_kept = middle + total(*[p[0] for p in own_sums])
    first_rows = [first_rows[0]] + to_rows(first_rows)
    projection_rows = [g[:, :, i * block : (i + 1) * block] for i in range(row_size)]
    projection_rows[1:] = to_rows(projection_rows)
    second_other = to_core(second_halves[1])
    kept = product(lambda a: rows_of(a, parity * own))
    sent, grad_one_other, last_along, first_rows, projection_rows, second_halves, second_other, first_part, kept, out_kept = fence(
        (sent, grad_one_other, last_along, first_rows, projection_rows, second_halves, second_other, first_part, kept, out_kept)
    )

    second_rows = small(second_halves[0], second_other)
    first_rows = small(*first_rows)
    g = small(*projection_rows)
    both_parts = jnp.stack([first_part, small(*last_along)])
    second_rows, first_rows, both_parts, g = fence((second_rows, first_rows, both_parts, g))
    second_rows = [second_rows[0]] + to_rows(second_rows)
    first_rows = shift(first_rows, "col", 2)
    projection_far = shift(g[:2], "col", 2)
    grad_one_other.append(to_pair(sent[half:]))
    both_parts_other = to_y(both_parts)
    second_rows, first_rows, projection_far, grad_one_other, both_parts, both_parts_other, g = fence(
        (second_rows, first_rows, projection_far, grad_one_other, both_parts, both_parts_other, g)
    )

    both = combine(second_rows, first_rows, g[2:], projection_far)
    both, both_parts, both_parts_other, grad_one_other = fence((both, both_parts, both_parts_other, grad_one_other))
    both_other = to_y(both)
    both_parts = halves(y == 0, both_parts[:, None], both_parts_other[:, None], 1)
    both_parts_core = to_core(both_parts)
    arrived = jnp.concatenate(grad_one_other).astype(F32)
    grad_inputs, gain_one_term = norm_back(inputs.astype(F32), gain_one, kept + arrived)
    grad_inputs = unrel((grad_inputs + grad_middle).astype(BF))
    gains = unrel(jnp.stack([gain_one_term, gain_two_term]))
    for axis, n in (("row", row_size), ("col", col_size)):
        bit = 1
        while bit < n:
            gains = gains + lax.ppermute(gains, axis, [(i, i ^ bit) for i in range(n)])
            bit *= 2
    gains = gains + swap(gains, "dp", 1)
    gate_up_grad, down_grad = place(
        jnp.where(core == 0, both_parts, both_parts_core), jnp.where(core == 0, both_parts_core, both_parts)
    )
    output = unrel((out_kept + out_other.astype(F32)).astype(BF))
    both, both_other, gate_up_grad, down_grad, gains, output, grad_inputs = fence(
        (both, both_other, gate_up_grad, down_grad, gains, output, grad_inputs)
    )
    both = small(both, both_other)
    both_other = to_core(both)
    gains = gains + swap(gains, "dp", 2)
    attention_gain_grad, feedforward_gain_grad = gains[0], gains[1]
    query_grad, key_value_grad, projection_grad = place_attention(
        jnp.where(core == 0, both, both_other), jnp.where(core == 0, both_other, both), block
    )
    return (
        output,
        grad_inputs,
        attention_gain_grad,
        feedforward_gain_grad,
        query_grad,
        key_value_grad,
        projection_grad,
        gate_up_grad,
        down_grad,
    )


def solution(mesh):
    sizes = tuple(mesh.shape[name] for name in ("dp", "row", "col"))
    return jax.shard_map(
        functools.partial(per_device, sizes=sizes),
        mesh=mesh,
        in_specs=(
            P(("dp", "row", "col"), None),
            P(),
            P(),
            P("row", "col"),
            P("row", None, "col"),
            P("col", "row"),
            P("row", None, "col"),
            P("col", "row"),
            P(("dp", "row", "col"), None),
        ),
        out_specs=(
            P(("dp", "row", "col"), None),
            P(("dp", "row", "col"), None),
            P(),
            P(),
            P("row", "col"),
            P("row", None, "col"),
            P("col", "row"),
            P("row", None, "col"),
            P("col", "row"),
        ),
        check_vma=False,
    )
```

```python
import functools
import math

import jax
import jax.numpy as jnp
from jax import lax
from jax.experimental import pallas as pl
from jax.experimental.pallas import tpu as pltpu
from jax.sharding import PartitionSpec as P

QUERY_HEADS = 16
KEY_VALUE_HEADS = 8
HEAD_DIM = 96
SEQUENCE_TOKENS = 1024

eps = 1e-05
rope_base = 100000.0

BF = jnp.bfloat16
F32 = jnp.float32

HALF = HEAD_DIM // 2
LANES = 128
GROUP = 4 * HEAD_DIM
GROUP_LANES = 4 * LANES
BLOCK = 256
SCALE = HEAD_DIM ** (-0.5)
PARTS = 2
QUICK = pl.CostEstimate(flops=1, bytes_accessed=1, transcendentals=0)
SPLIT_MODEL = 768


def dot(a, b):
    return lax.dot_general(a, b, (((1,), (0,)), ((), ())), preferred_element_type=F32)


def dot_nt(a, b):
    return lax.dot_general(a, b, (((1,), (1,)), ((), ())), preferred_element_type=F32)


def dot_tn(a, b):
    return lax.dot_general(a, b, (((0,), (0,)), ((), ())), preferred_element_type=F32)


def exponentials_t(keys, queries, block):
    s = dot_nt(keys, queries)
    here = s[block * BLOCK :]
    later = lax.broadcasted_iota(jnp.int32, here.shape, 0) > lax.broadcasted_iota(jnp.int32, here.shape, 1)
    here = jnp.where(later, -1e30, here)
    s = jnp.concatenate([s[: block * BLOCK], here], axis=0) if block else here
    top = jnp.max(s, axis=0, keepdims=True)
    e = jnp.exp2((s - top) * (SCALE * math.log2(math.e)))
    return e, 1.0 / jnp.sum(e, axis=0, keepdims=True)


def attention_forward_kernel(n1_ref, w_ref, spread_ref, cos_ref, sin_ref, qkv_ref, o_ref):
    w = dot(w_ref[...], spread_ref[...]).astype(BF)
    h = dot(n1_ref[...], w)
    cos, sin = cos_ref[...], sin_ref[...]
    for part in range(4):
        c = h[:, part * LANES : (part + 1) * LANES]
        if part < 3:
            c = c * cos + pltpu.roll(c, LANES // 2, 1) * sin
        qkv_ref[:, part * LANES : (part + 1) * LANES] = c.astype(BF)
    v_t = h[:, 3 * LANES :].T.astype(BF)
    for head in range(2):
        lanes = slice(head * LANES, (head + 1) * LANES)
        for block in range(SEQUENCE_TOKENS // BLOCK):
            rows = slice(block * BLOCK, (block + 1) * BLOCK)
            length = (block + 1) * BLOCK
            e, inverse = exponentials_t(qkv_ref[:length, 2 * LANES : 3 * LANES], qkv_ref[rows, lanes], block)
            o_t = dot(v_t[:, :length], e.astype(BF)) * inverse
            o_ref[rows, lanes] = o_t.T.astype(BF)


def attention_backward_kernel(qkv_ref, do_ref, gather_ref, cos_ref, sin_ref, out_ref, dk_ref, dv_ref, dq_ref, d_ref):
    cos, sin = cos_ref[...], sin_ref[...]

    def unrotate(c):
        c = c * SCALE
        return (c * cos - pltpu.roll(c, LANES // 2, 1) * sin).astype(BF)

    k_t = qkv_ref[:, 2 * LANES : 3 * LANES].astype(F32).T.astype(BF)
    dk_ref[...] = jnp.zeros_like(dk_ref)
    dv_ref[...] = jnp.zeros_like(dv_ref)
    for head in range(2):
        lanes = slice(head * LANES, (head + 1) * LANES)
        for block in range(SEQUENCE_TOKENS // BLOCK):
            rows = slice(block * BLOCK, (block + 1) * BLOCK)
            length = (block + 1) * BLOCK
            q = qkv_ref[rows, lanes]
            do = do_ref[rows, lanes]
            e, inverse = exponentials_t(qkv_ref[:length, 2 * LANES : 3 * LANES], q, block)
            p = e * inverse
            dp = dot_nt(qkv_ref[:length, 3 * LANES :], do)
            ds = (p * (dp - jnp.sum(p * dp, axis=0, keepdims=True))).astype(BF)
            dv_ref[:length, :] += dot(p.astype(BF), do)
            dk_ref[:length, :] += dot(ds, q)
            dq_ref[rows, :] = dot(k_t[:, :length], ds).T
        d_ref[:, lanes] = unrotate(dq_ref[...])
    d_ref[:, 2 * LANES : 3 * LANES] = unrotate(dk_ref[...])
    d_ref[:, 3 * LANES :] = dv_ref[...].astype(BF)
    out_ref[...] = dot(d_ref[...], gather_ref[...]).astype(BF)


def rotary_tables():
    positions = jnp.arange(SEQUENCE_TOKENS).astype(F32)
    inverse_freq = jnp.exp(jnp.arange(HALF).astype(F32) * (-2.0 * math.log(rope_base) / HEAD_DIM))
    angles = positions[:, None] * inverse_freq[None, :]
    gap = ((0, 0), (0, LANES // 2 - HALF))
    cos, sin = jnp.pad(jnp.cos(angles), gap), jnp.pad(jnp.sin(angles), gap)
    return jnp.concatenate([cos, cos], axis=1), jnp.concatenate([-sin, sin], axis=1)


def spread_matrix():
    src = lax.broadcasted_iota(jnp.int32, (GROUP, GROUP_LANES), 0)
    lane = lax.broadcasted_iota(jnp.int32, (GROUP, GROUP_LANES), 1)
    head, comp = src // HEAD_DIM, src % HEAD_DIM
    place = head * LANES + jnp.where(comp < HALF, comp, comp + LANES // 2 - HALF)
    return (place == lane).astype(BF)


def attention_forward(n1, w, spread, cos, sin):
    tokens, width = n1.shape
    groups = w.shape[1] // GROUP
    whole = lambda a: pl.BlockSpec(a.shape, lambda j: (0, 0))
    return pl.pallas_call(
        attention_forward_kernel,
        grid=(groups,),
        in_specs=[
            whole(n1),
            pl.BlockSpec((width, GROUP), lambda j: (0, j)),
            whole(spread),
            whole(cos),
            whole(sin),
        ],
        out_specs=[
            pl.BlockSpec((tokens, GROUP_LANES), lambda j: (0, j)),
            pl.BlockSpec((tokens, 2 * LANES), lambda j: (0, j)),
        ],
        out_shape=[
            jax.ShapeDtypeStruct((tokens, groups * GROUP_LANES), BF),
            jax.ShapeDtypeStruct((tokens, groups * 2 * LANES), BF),
        ],
        compiler_params=pltpu.CompilerParams(vmem_limit_bytes=48 * 1024 * 1024),
        cost_estimate=QUICK,
        name="attention_forward",
    )(n1, w, spread, cos, sin)


def attention_backward(qkv, do, gather, cos, sin, first, groups):
    tokens = qkv.shape[0]
    whole = lambda a: pl.BlockSpec(a.shape, lambda j: (0, 0))
    return pl.pallas_call(
        attention_backward_kernel,
        grid=(groups,),
        in_specs=[
            pl.BlockSpec((tokens, GROUP_LANES), lambda j: (0, first + j)),
            pl.BlockSpec((tokens, 2 * LANES), lambda j: (0, first + j)),
            whole(gather),
            whole(cos),
            whole(sin),
        ],
        out_specs=pl.BlockSpec((tokens, GROUP), lambda j: (0, j)),
        out_shape=jax.ShapeDtypeStruct((tokens, groups * GROUP), BF),
        scratch_shapes=[
            pltpu.VMEM((tokens, LANES), F32),
            pltpu.VMEM((tokens, LANES), F32),
            pltpu.VMEM((tokens, LANES), F32),
            pltpu.VMEM((tokens, GROUP_LANES), BF),
        ],
        compiler_params=pltpu.CompilerParams(vmem_limit_bytes=48 * 1024 * 1024),
        cost_estimate=QUICK,
        name="attention_backward",
    )(qkv, do, gather, cos, sin)


def feedforward_kernel(col_step, sub, rows_of, n2_ref, cot_ref, *refs):
    *blocks, out_bf_ref, dn2_bf_ref, out_ref, dn2_ref, h_ref, dgu_ref = refs
    sides = [blocks[k : k + rows_of] for k in range(0, len(blocks), rows_of)]
    weights, earlier, grads = sides[:2], sides[2:-2], sides[-2:]
    step, half = pl.program_id(0), pl.num_programs(0) // 2
    width = n2_ref.shape[1] // rows_of
    cut = [slice(i * width, (i + 1) * width) for i in range(rows_of)]

    @pl.when(step == 0)
    def _():
        out_ref[...] = jnp.zeros_like(out_ref)
        dn2_ref[...] = jnp.zeros_like(dn2_ref)

    def rows(ref, first, last):
        return jnp.concatenate([ref[c, first:last] for c in range(col_step)], axis=0)

    def work(whose):
        gate_up = [rows(r, 0, 2 * sub) for r in weights[whose]]
        down = [rows(r, 2 * sub, 3 * sub) for r in weights[whose]]
        dh = sum(dot_nt(cot_ref[:, cut[i]], down[i]) for i in range(rows_of))
        gu = sum(dot_nt(n2_ref[:, cut[i]], gate_up[i]) for i in range(rows_of))
        for c in range(col_step):
            gate, up = (gu[:, (2 * c + k) * sub : (2 * c + k + 1) * sub] for k in range(2))
            sig = jax.nn.sigmoid(gate)
            silu = gate * sig
            lanes = slice(c * sub, (c + 1) * sub)
            part = dh[:, lanes]
            h_ref[:, lanes] = (silu * up).astype(BF)
            dgu_ref[:, 2 * c * sub : (2 * c + 1) * sub] = (part * up * (sig + silu * (1 - sig))).astype(BF)
            dgu_ref[:, (2 * c + 1) * sub : (2 * c + 2) * sub] = (part * silu).astype(BF)
        hidden, dgu = h_ref[...], dgu_ref[...]
        hidden_t, dgu_t = hidden.T, dgu.T
        for i in range(rows_of):
            dn2_ref[:, cut[i]] += dot(dgu, gate_up[i])
            out_ref[:, cut[i]] += dot(hidden, down[i])
            gate_up_grad = dot(dgu_t, n2_ref[:, cut[i]])
            down_grad = dot(hidden_t, cot_ref[:, cut[i]])
            for c in range(col_step):
                new = (gate_up_grad[2 * c * sub : 2 * (c + 1) * sub], down_grad[c * sub : (c + 1) * sub])
                for part, here in zip(new, (slice(2 * sub), slice(2 * sub, None))):
                    if earlier:
                        part = part + earlier[whose][i][c, here].astype(F32)
                    grads[whose][i][c, here] = part.astype(BF)

    pl.when(step < half)(lambda: work(1))
    pl.when(step >= half)(lambda: work(0))

    @pl.when(step == 2 * half - 1)
    def _():
        out_bf_ref[...] = out_ref[...].astype(BF)
        dn2_bf_ref[...] = dn2_ref[...].astype(BF)


def feedforward(n2, cot, weights, col_step, earlier=()):
    tokens, model = n2.shape
    rows_of = len(weights[0])
    columns, rows, width = weights[0][0].shape
    sub = rows // 3
    half = columns // col_step
    once = lambda a: pl.BlockSpec(a.shape, lambda s: (0, 0), pipeline_mode=pl.Buffered(1))
    place = [lambda s: (jnp.maximum(s - half, 0), 0, 0), lambda s: (jnp.minimum(s, half - 1), 0, 0)]
    flat = [a for side in weights for a in side]
    specs = [pl.BlockSpec((col_step, rows, width), place[whose]) for whose in range(2) for _ in range(rows_of)]
    earlier = [a for side in earlier for a in side]
    total = jax.ShapeDtypeStruct((tokens, model), BF)
    outs = pl.pallas_call(
        functools.partial(feedforward_kernel, col_step, sub, rows_of),
        grid=(2 * half,),
        in_specs=[once(n2), once(cot)] + specs + (specs if earlier else []),
        out_specs=specs + [once(total), once(total)],
        out_shape=[jax.ShapeDtypeStruct(a.shape, BF) for a in flat] + [total, total],
        scratch_shapes=[
            pltpu.VMEM((tokens, model), F32),
            pltpu.VMEM((tokens, model), F32),
            pltpu.VMEM((tokens, col_step * sub), BF),
            pltpu.VMEM((tokens, 2 * col_step * sub), BF),
        ],
        compiler_params=pltpu.CompilerParams(vmem_limit_bytes=60 * 1024 * 1024),
        cost_estimate=QUICK,
        name="feedforward",
    )(n2, cot, *flat, *earlier)
    return [list(outs[:rows_of]), list(outs[rows_of : 2 * rows_of])], outs[2 * rows_of], outs[2 * rows_of + 1]


def place_kernel(*refs):
    cores, (gate_up_ref, down_ref) = refs[:2], refs[2:]
    parts, _, rows, block = cores[0].shape
    sub = rows // 3
    for core, ref in enumerate(cores):
        for y in range(2):
            for k in range(parts):
                tile = (2 * y + core) * parts + k
                for half in range(2):
                    piece = ref[k, y, half * sub : (half + 1) * sub].astype(F32)
                    gate_up_ref[pl.ds(2 * tile + half, block, stride=8 * parts), :] = piece.T
                down_ref[tile * sub : (tile + 1) * sub] = ref[k, y, 2 * sub :].astype(F32)


def place(first, second):
    parts, _, rows, block = first.shape
    sub = rows // 3
    tiles = 4 * parts
    gate_up, down = pl.pallas_call(
        place_kernel,
        out_shape=[
            jax.ShapeDtypeStruct((block * tiles * 2, sub), F32),
            jax.ShapeDtypeStruct((tiles * sub, block), F32),
        ],
        compiler_params=pltpu.CompilerParams(vmem_limit_bytes=48 * 1024 * 1024),
        cost_estimate=QUICK,
        name="place",
    )(first, second)
    return gate_up.reshape(block, tiles, 2, sub).transpose(0, 2, 1, 3).reshape(block, 2, -1), down


def combine_kernel(*refs):
    out_ref = refs[-1]
    *rows, mine, other = refs[:-1]
    qkv = sum(r[...].astype(F32) for r in rows).astype(BF)
    heads = (mine[...].astype(F32) + other[...].astype(F32)).astype(BF)
    split = qkv.shape[0]
    for p in range(2):
        out_ref[p, :split] = qkv[:, p * GROUP : (p + 1) * GROUP]
        for n in range(2 * split // GROUP):
            here = slice(split + n * HEAD_DIM, split + (n + 1) * HEAD_DIM)
            out_ref[p, here] = heads[p, :, n * GROUP : (n + 1) * GROUP]


def combine(rows, arrived, heads, heads_arrived):
    split, block = rows[0].shape[0], heads.shape[2]
    if block % GROUP:
        qkv = sum(r.astype(F32) for r in rows + [arrived])
        heads = heads.astype(F32) + heads_arrived.astype(F32)
        parts = [jnp.concatenate([qkv[:, p * GROUP : (p + 1) * GROUP], heads[p].reshape(-1, GROUP)]) for p in range(2)]
        return jnp.stack(parts).astype(BF)
    return pl.pallas_call(
        combine_kernel,
        out_shape=jax.ShapeDtypeStruct((2, split + HEAD_DIM * block // GROUP, GROUP), BF),
        compiler_params=pltpu.CompilerParams(vmem_limit_bytes=32 * 1024 * 1024),
        cost_estimate=QUICK,
        name="combine",
    )(*rows, arrived, heads, heads_arrived)


def place_attention_kernel(*refs):
    cores, (query_ref, pair_ref, projection_ref) = refs[:2], refs[2:]
    block = query_ref.shape[0]
    rows = block // 2
    for core, ref in enumerate(cores):
        here = slice(core * rows, (core + 1) * rows)
        for parity in range(2):
            g = ref[parity, :rows].astype(F32)
            query_ref[here, 2 * parity * HEAD_DIM : 2 * (parity + 1) * HEAD_DIM] = g[:, : 2 * HEAD_DIM]
            g = g.T
            for k in range(2):
                pair_ref[k, parity * HEAD_DIM : (parity + 1) * HEAD_DIM, here] = g[(2 + k) * HEAD_DIM : (3 + k) * HEAD_DIM]
            head = slice((2 * parity + core) * HEAD_DIM, (2 * parity + core + 1) * HEAD_DIM)
            for k in range(block // GROUP):
                piece = ref[parity, rows + k * HEAD_DIM : rows + (k + 1) * HEAD_DIM]
                projection_ref[head, k * GROUP : (k + 1) * GROUP] = piece.astype(F32)


def place_attention(first, second, block):
    folded = block % GROUP != 0
    query, pair, projection = pl.pallas_call(
        place_attention_kernel,
        out_shape=[
            jax.ShapeDtypeStruct((block, 4 * HEAD_DIM), F32),
            jax.ShapeDtypeStruct((2, 2 * HEAD_DIM, block), F32),
            jax.ShapeDtypeStruct((4 * HEAD_DIM, block), F32),
        ],
        compiler_params=pltpu.CompilerParams(vmem_limit_bytes=32 * 1024 * 1024),
        cost_estimate=QUICK,
        name="place_attention",
    )(first, second)
    if folded:
        both = jnp.stack([a[:, block // 2 :].reshape(2, HEAD_DIM, block) for a in (first, second)], axis=1)
        projection = both.astype(F32).reshape(-1, block)
    return query, pair.transpose(2, 0, 1), projection


def assemble_kernel(groups, core_ref, *refs):
    pieces, (qkv_ref, projection_ref) = refs[:-2], refs[-2:]
    first = core_ref[0] == 0
    blocks = len(pieces) // groups
    rows = qkv_ref.shape[0] // (2 * blocks)
    projection_ref[...] = jnp.zeros_like(projection_ref)
    for i in range(blocks):
        for k in range(groups // 2):
            mine, other = pieces[i * groups + 2 * k], pieces[i * groups + 2 * k + 1]
            for p in range(2):
                a, b = mine[p], other[p]
                group = 2 * k + p
                for core, piece in enumerate((jnp.where(first, a, b), jnp.where(first, b, a))):
                    start = (2 * i + core) * rows
                    qkv_ref[start : start + rows, group * GROUP : (group + 1) * GROUP] = piece[:rows]
                    place = group * 2 * LANES + core * LANES
                    for n in range(2 * rows // GROUP):
                        lanes = slice(2 * i * rows + n * GROUP, 2 * i * rows + (n + 1) * GROUP)
                        head = piece[rows + n * HEAD_DIM : rows + (n + 1) * HEAD_DIM]
                        projection_ref[place : place + HALF, lanes] = head[:HALF]
                        projection_ref[place + LANES // 2 : place + LANES // 2 + HALF, lanes] = head[HALF:]


def assemble(core, pieces, model):
    groups = len(pieces[0])
    flat = [a for row in pieces for a in row]
    return pl.pallas_call(
        functools.partial(assemble_kernel, groups),
        in_specs=[pl.BlockSpec(memory_space=pltpu.SMEM)] + [pl.BlockSpec(memory_space=pltpu.VMEM)] * len(flat),
        out_shape=[
            jax.ShapeDtypeStruct((model, groups * GROUP), BF),
            jax.ShapeDtypeStruct((groups * 2 * LANES, model), BF),
        ],
        compiler_params=pltpu.CompilerParams(vmem_limit_bytes=48 * 1024 * 1024),
        cost_estimate=QUICK,
        name="assemble",
    )(core.astype(jnp.int32)[None], *flat)


def halves_kernel(gap, core_ref, a_ref, b_ref, out_ref):
    g = dot_tn(a_ref[...], b_ref[...]).astype(BF)
    if gap:
        out_ref[0, 0, :HALF] = g[:HALF]
        out_ref[0, 0, HALF:] = g[LANES // 2 : LANES // 2 + HALF]
    else:
        out_ref[0, 0] = g


def gradient_halves(core, a, b, rows, gap=False):
    tokens, width = a.shape
    blocks = width // (2 * rows)
    kept = HEAD_DIM if gap else rows
    columns = b.shape[1]
    return pl.pallas_call(
        functools.partial(halves_kernel, gap),
        grid_spec=pltpu.PrefetchScalarGridSpec(
            num_scalar_prefetch=1,
            grid=(2, blocks),
            in_specs=[
                pl.BlockSpec((tokens, rows), lambda h, i, core: (0, 2 * i + (core[0] + h) % 2)),
                pl.BlockSpec(b.shape, lambda h, i, core: (0, 0)),
            ],
            out_specs=pl.BlockSpec((1, 1, kept, columns), lambda h, i, core: (h, i, 0, 0)),
        ),
        out_shape=jax.ShapeDtypeStruct((2, blocks, kept, columns), BF),
        compiler_params=pltpu.CompilerParams(vmem_limit_bytes=48 * 1024 * 1024),
        cost_estimate=QUICK,
        name="gradient_halves",
    )(core.astype(jnp.int32)[None], a, b)


def inverse_rms(field):
    return lax.rsqrt(jnp.mean(field * field, axis=-1, keepdims=True) + eps)


def norm_back(field, gain, grad):
    r = inverse_rms(field)
    scaled = gain * grad
    inner = jnp.mean(field * scaled, axis=-1, keepdims=True)
    return r * scaled - field * (r * r * r * inner), jnp.sum(grad * field * r, axis=0)


def norm_back_kernel(field_ref, gain_ref, skip_ref, *refs):
    *terms, out_ref, rounded_ref, gain_grad_ref = refs
    field = field_ref[...]
    grad = sum(t[...].astype(F32) for t in terms)
    r = inverse_rms(field)
    scaled = gain_ref[...] * grad
    inner = jnp.mean(field * scaled, axis=-1, keepdims=True)
    out = skip_ref[...].astype(F32) + r * scaled - field * (r * r * r * inner)
    out_ref[...] = out
    rounded_ref[...] = out.astype(BF)

    @pl.when(pl.program_id(0) == 0)
    def _():
        gain_grad_ref[...] = jnp.zeros_like(gain_grad_ref)

    gain_grad_ref[...] += jnp.sum(grad * (field * r), axis=0, keepdims=True)


def norm_back_rows(field, gain, skip, terms):
    tokens, model = field.shape
    rows = 128
    block = pl.BlockSpec((rows, model), lambda i: (i, 0))
    line = pl.BlockSpec((1, model), lambda i: (0, 0))
    out, rounded, gain_grad = pl.pallas_call(
        norm_back_kernel,
        grid=(tokens // rows,),
        in_specs=[block, line, block] + [block] * len(terms),
        out_specs=[block, block, line],
        out_shape=[
            jax.ShapeDtypeStruct(field.shape, F32),
            jax.ShapeDtypeStruct(field.shape, BF),
            jax.ShapeDtypeStruct((1, model), F32),
        ],
        compiler_params=pltpu.CompilerParams(vmem_limit_bytes=60 * 1024 * 1024),
        cost_estimate=QUICK,
        name="norm_back",
    )(field, gain[None], skip, *terms)
    return out, rounded, gain_grad[0]


def halves(first_is_mine, mine, other, axis):
    return jnp.where(
        first_is_mine, jnp.concatenate([mine, other], axis), jnp.concatenate([other, mine], axis)
    )


def per_device(
    tokens,
    attention_gain,
    feedforward_gain,
    query_weight,
    key_value_matrix,
    projection_weight,
    gate_up_weight,
    down_weight,
    cotangent,
    *,
    sizes,
):
    dp_size, row_size, col_size = sizes
    x, z, d = lax.axis_index("row"), lax.axis_index("col"), lax.axis_index("dp")
    core, y, parity = d % 2, d // 2, z % 2
    model = tokens.shape[1]
    own = tokens.shape[0]
    block = model // row_size
    hidden_block = down_weight.shape[0]
    sub = hidden_block // 4 // PARTS

    def swap(a, axis, bit):
        n = {"dp": dp_size, "col": col_size}[axis]
        return lax.ppermute(a, axis, [(i, i ^ bit) for i in range(n)])

    def to_core(a):
        return swap(a, "dp", 1)

    def to_y(a):
        return swap(a, "dp", 2)

    def to_pair(a):
        return swap(a, "col", 1)

    def shift(a, axis, by):
        n = {"row": row_size, "col": col_size}[axis]
        return lax.ppermute(a, axis, [(i, (i + by) % n) for i in range(n)])

    def rel(a):
        if row_size == 2:
            return jnp.where(x == 0, a, jnp.concatenate([a[..., block:], a[..., :block]], axis=-1))
        return lax.dynamic_slice_in_dim(jnp.concatenate([a, a], axis=-1), x * block, model, a.ndim - 1)

    def unrel(a):
        if row_size == 2:
            return rel(a)
        return lax.dynamic_slice_in_dim(
            jnp.concatenate([a, a], axis=-1), (row_size - x) % row_size * block, model, a.ndim - 1
        )

    def gather_rows(piece):
        return [piece] + [shift(piece, "row", -i) for i in range(1, row_size)]

    def pick(a, index, axis):
        return lax.dynamic_index_in_dim(a, index, axis, keepdims=False)

    def merge(rows):
        return rows if len(rows) * SPLIT_MODEL <= model else [jnp.concatenate(rows, axis=2)]

    def by_rows(blocks):
        return list(blocks) if len(blocks) == row_size else jnp.split(blocks[0], row_size, axis=2)

    fence = lax.optimization_barrier

    def fold(a):
        if block % GROUP:
            return a.reshape(-1, GROUP)
        return jnp.concatenate([a[:, k : k + GROUP] for k in range(0, block, GROUP)])

    def unfold(a):
        if block % GROUP:
            return a.reshape(a.shape[:-2] + (HEAD_DIM, block))
        return jnp.concatenate([a[..., k : k + HEAD_DIM, :] for k in range(0, a.shape[-2], HEAD_DIM)], axis=-1)


    def total(*parts):
        return sum(part.astype(F32) for part in parts)

    def small(*parts):
        return total(*parts).astype(BF)

    def in_sequence(a, other):
        return halves(parity == 0, a, other, 0)

    def rows_of(a, first):
        return lax.dynamic_slice_in_dim(a, first, own, 0)

    query_blocks = query_weight.reshape(block, 2, 2 * HEAD_DIM)
    pair_blocks = key_value_matrix.reshape(block, 2, 2, HEAD_DIM)
    packed = jnp.concatenate([query_blocks, pair_blocks[:, 0], pair_blocks[:, 1]], axis=-1)
    packed = lax.dynamic_slice_in_dim(packed, core * (block // 2), block // 2, 0)
    head_rows = pick(projection_weight.reshape(2, 2, HEAD_DIM, block), core, 1)
    packed = jnp.stack([jnp.concatenate([packed[:, p], fold(head_rows[p])]) for p in range(2)])
    packed, tokens, cotangent, gate_up_weight, down_weight = fence(
        (packed, tokens, cotangent, gate_up_weight, down_weight)
    )
    far_packed = shift(packed, "col", 2)
    own_packed = gather_rows(packed)

    pieces = []
    for part in range(PARTS):
        start = ((2 * y + core) * PARTS + part) * sub
        gate_up = lax.dynamic_slice_in_dim(gate_up_weight, start, sub, 2).transpose(1, 2, 0).reshape(2 * sub, block)
        pieces.append(jnp.concatenate([gate_up, lax.dynamic_slice_in_dim(down_weight, start, sub, 0)]))
    gain_one, gain_two = rel(attention_gain), rel(feedforward_gain)
    inputs = rel(tokens)
    wide_inputs = inputs.astype(F32)
    normed = (wide_inputs * inverse_rms(wide_inputs) * gain_one).astype(BF)
    normed_other = to_pair(normed)
    tables = rotary_tables()
    spread = spread_matrix()
    spread_back = spread.T
    far_packed, own_packed, pieces, inputs, normed, normed_other, tables = fence(
        (far_packed, own_packed, pieces, inputs, normed, normed_other, tables)
    )

    far_rows = gather_rows(far_packed)
    own_cores = [to_core(a) for a in own_packed]
    others = [shift(pieces[0], "col", 1)]
    late_others = [shift(pieces[1], "col", 1)]
    normed_all = in_sequence(normed, normed_other)
    grad_out = rel(cotangent)
    far_rows, own_cores, own_packed, others, late_others, normed_all, spread, spread_back, grad_out, pieces = fence(
        (far_rows, own_cores, own_packed, others, late_others, normed_all, spread, spread_back, grad_out, pieces)
    )
    own_rows = gather_rows(jnp.stack(pieces))
    rest_near = gather_rows(others[0])
    far_cores = [to_core(a) for a in far_rows]
    others += [shift(pieces[0], "col", j) for j in range(2, col_size)]
    split = block // 2
    if split % LANES == 0:
        rows = [list(parts) for parts in zip(far_rows, far_cores, own_packed, own_cores)]
        weight_qkv, weight_projection = assemble(core, rows, model)
    else:
        pick_core = lambda a, b: halves(core == 0, a[:, None], b[:, None], 1)
        pairs = [
            jnp.concatenate([pick_core(*far), pick_core(*mine)])
            for far, mine in zip(zip(far_rows, far_cores), zip(own_packed, own_cores))
        ]
        weight_qkv = jnp.concatenate([jnp.concatenate([p[j, :, :split] for j in range(col_size)], axis=-1) for p in pairs])
        weight_qkv = weight_qkv.reshape(model, -1)
        heads = jnp.concatenate([unfold(p[:, :, split:]) for p in pairs], axis=-1)
        gap = jnp.zeros(heads.shape[:2] + (LANES // 2 - HALF, model), BF)
        weight_projection = jnp.concatenate(
            [heads[:, :, :HALF], gap, heads[:, :, HALF:], gap], axis=2
        ).reshape(-1, model)
    weight_qkv, weight_projection = fence((weight_qkv, weight_projection))

    qkv, attended = attention_forward(normed_all, weight_qkv, spread, *tables)
    qkv, attended, others, late_others, own_rows, grad_out, weight_projection, rest_near = fence(
        (qkv, attended, others, late_others, own_rows, grad_out, weight_projection, rest_near)
    )

    sent = dot(rows_of(attended, (1 - parity) * own), weight_projection).astype(BF)
    stacked = jnp.stack(others[1:])
    sent, stacked, attended, weight_projection = fence((sent, stacked, attended, weight_projection))
    arrived = to_pair(sent)
    rest = gather_rows(stacked)
    grad_out_other = to_y(grad_out)
    fine = row_size * SPLIT_MODEL <= model
    own_first = [a[0] for a in own_rows]
    kept = dot(rows_of(attended, parity * own), weight_projection)
    kept, stacked = fence((kept, stacked))
    mine = [jnp.concatenate([own_first[0][None], rest_near[0][None], stacked])] if fine else []
    mine_other = [to_core(a) for a in mine]
    kept, arrived, rest, mine, mine_other, pieces, own_rows, grad_out, grad_out_other = fence(
        (kept, arrived, rest, mine, mine_other, pieces, own_rows, grad_out, grad_out_other)
    )

    middle = inputs.astype(F32) + kept + arrived.astype(F32)
    normed_two = (middle * inverse_rms(middle) * gain_two).astype(BF)
    n = len(mine)
    late = merge([jnp.concatenate([a[None], b[None], c]) for a, b, c in zip(own_first[n:], rest_near[n:], rest[n:])])
    normed_two, middle, late = fence((normed_two, middle, late))
    normed_two_other = to_y(normed_two)
    weights = [mine + late, mine_other + [to_core(a) for a in late]]
    others = [shift(pieces[1], "col", j) for j in (2, 3)]
    weights, normed_two = fence((weights, normed_two))

    rest = [gather_rows(late_others[0])]
    grads, *sums = feedforward(normed_two, grad_out, weights, PARTS)
    grads, sums, rest, others, normed_two_other, weights, middle, late_others = fence(
        (grads, sums, rest, others, normed_two_other, weights, middle, late_others)
    )
    own_sums = [sums]
    stacked = jnp.stack(others)
    early = (
        [jnp.concatenate([own_rows[0][1:], late_others[0][None], stacked])] if row_size * SPLIT_MODEL <= model else []
    )
    stacked, early, own_rows = fence((stacked, early, own_rows))
    rest.append(gather_rows(stacked))
    early_other = [to_core(a) for a in early]
    grads, *sums = feedforward(normed_two_other, grad_out_other, weights, PARTS, grads)
    grads, sums, rest, early, early_other, own_rows = fence((grads, sums, rest, early, early_other, own_rows))
    other_sums = [sums]
    n = len(early)
    late = merge([jnp.concatenate([a[1:], b[None], c]) for a, b, c in zip(own_rows[n:], rest[0][n:], rest[1][n:])])
    mine, other = by_rows(grads[0]), by_rows(grads[1])
    late, other[1:] = fence((late, other[1:]))
    late_other = [to_core(a) for a in late]
    arrived = [to_core(a) for a in other[1:]]
    mine, other[0], late, late_other, arrived = fence((mine, other[0], late, late_other, arrived))
    weights = [early + late, early_other + late_other]
    middle_columns = lambda a: a[1:3]
    outer_columns = lambda a: jnp.stack([a[0], a[3]])
    sent = [[small(cut(a), cut(b)) for a, b in zip(mine[1:], arrived)] for cut in (middle_columns, outer_columns)]
    weights, mine[0], other[0], sent, normed_two_other = fence((weights, mine[0], other[0], sent, normed_two_other))
    rows = [shift(a, "row", i) for i, a in enumerate(sent[0], 1)]
    arrived = to_core(other[0])
    grads, *sums = feedforward(normed_two_other, grad_out_other, weights, PARTS)
    grads, sums, rows, mine[0], arrived, sent, weights = fence((grads, sums, rows, mine[0], arrived, sent, weights))
    other_sums.append(sums)

    sums = small(*[p[1] for p in other_sums])
    sums, mine[0], arrived, rows, grads, other_sums, own_sums = fence(
        (sums, mine[0], arrived, rows, grads, other_sums, own_sums)
    )
    grad_two_other = to_y(sums)
    blocks = [small(mine[0][j], arrived[j], *[r[j - 1] for r in rows]) for j in (1, 2)]
    blocks, grads, normed_two = fence((blocks, grads, normed_two))
    rows = [shift(a, "row", i) for i, a in enumerate(sent[1], 1)]
    along = [shift(blocks[1], "col", -2)]
    grads, *sums = feedforward(normed_two, grad_out, weights, PARTS, grads)
    grads, sums, rows, along, blocks, mine[0], arrived, grad_two_other = fence(
        (grads, sums, rows, along, blocks, mine[0], arrived, grad_two_other)
    )
    near_block = blocks[0]
    own_sums.append(sums)
    last, other = by_rows(grads[0]), by_rows(grads[1])
    last_rows = [to_core(a) for a in other[1:]]
    terms = [grad_two_other] + [p[1] for p in own_sums]
    grad_middle, branch, gain_two_term = norm_back_rows(middle, gain_two, grad_out, terms)
    last_rows, branch, grad_middle, gain_two_term, last, other[0] = fence(
        (last_rows, branch, grad_middle, gain_two_term, last, other[0])
    )
    branch_other = to_pair(branch)
    sent = [[small(cut(a), cut(b)) for a, b in zip(last[1:], last_rows)] for cut in (middle_columns, outer_columns)]
    last_rows = [shift(a, "row", i) for i, a in enumerate(sent[0], 1)]
    last_core = to_core(other[0])
    blocks = [small(mine[0][j], arrived[j], *[r[j // 3] for r in rows]) for j in (0, 3)]
    blocks.append(near_block)
    branch, branch_other, last_core, last_rows, sent, own_sums, other_sums, blocks, grad_middle, gain_two_term = fence(
        (branch, branch_other, last_core, last_rows, sent, own_sums, other_sums, blocks, grad_middle, gain_two_term)
    )

    along += [blocks[0], shift(blocks[1], "col", -3), shift(blocks[2], "col", -1)]
    out_other = to_y(small(*[p[0] for p in other_sums]))
    outer_rows = [shift(a, "row", i) for i, a in enumerate(sent[1], 1)]
    branch_all = in_sequence(branch, branch_other)
    grad_attended = dot_nt(branch_all, weight_projection).astype(BF)
    count = col_size // 2
    wide = count * GROUP
    to_rows = lambda g: [shift(g[i], "row", i) for i in range(1, row_size)]

    def qkv_halves(part):
        if split % LANES == 0:
            return gradient_halves(core, normed_all, part, split)
        g = dot_tn(normed_all, part).astype(BF).reshape(row_size, 2, split, wide)
        return jnp.stack([pick(g, core, 1), pick(g, 1 - core, 1)])

    first = attention_backward(qkv, grad_attended, spread_back, *tables, 0, count)
    first, along, outer_rows, grad_attended, branch_all = fence((first, along, outer_rows, grad_attended, branch_all))
    rows = [[m[0] for m in outer_rows], [m[0] for m in last_rows], [m[1] for m in last_rows], [m[1] for m in outer_rows]]
    blocks = [small(last[0][j], last_core[j], *rows[j]) for j in range(col_size)]
    blocks, grad_attended, first, branch_all = fence((blocks, grad_attended, first, branch_all))
    last_along = [blocks[0]] + [shift(blocks[j], "col", -j) if j & 1 else blocks[j] for j in range(1, col_size)]
    projection_halves = gradient_halves(core, attended, branch_all, LANES, True)
    first_halves = qkv_halves(first)
    second = attention_backward(qkv, grad_attended, spread_back, *tables, count, count)
    second, last_along, along, first_halves, projection_halves, out_other = fence(
        (second, last_along, along, first_halves, projection_halves, out_other)
    )

    product = lambda rows: sum(
        dot_nt(rows(part), weight_qkv[:, k * wide : (k + 1) * wide]) for k, part in enumerate((first, second))
    )
    first_other, projection_other = to_core(first_halves[1]), to_core(projection_halves[1])
    sent = product(lambda a: rows_of(a, (1 - parity) * own)).astype(BF)
    second_halves = qkv_halves(second)
    sent, second_halves, along, last_along, first_other, projection_other, first_halves, projection_halves = fence(
        (sent, second_halves, along, last_along, first_other, projection_other, first_halves, projection_halves)
    )
    half = own // 2
    grad_one_other = [to_pair(sent[:half])]
    last_along[2] = shift(last_along[2], "col", -2)
    first_rows = small(first_halves[0], first_other)
    g = small(projection_halves[0], projection_other)
    sent, first_rows, g, second_halves, own_sums, along = fence((sent, first_rows, g, second_halves, own_sums, along))
    first_part = small(*along)
    out_kept = middle + total(*[p[0] for p in own_sums])
    first_rows = [first_rows[0]] + to_rows(first_rows)
    projection_rows = [g[:, :, i * block : (i + 1) * block] for i in range(row_size)]
    projection_rows[1:] = to_rows(projection_rows)
    second_other = to_core(second_halves[1])
    kept = product(lambda a: rows_of(a, parity * own))
    sent, grad_one_other, last_along, first_rows, projection_rows, second_halves, second_other, first_part, kept, out_kept = fence(
        (sent, grad_one_other, last_along, first_rows, projection_rows, second_halves, second_other, first_part, kept, out_kept)
    )

    second_rows = small(second_halves[0], second_other)
    first_rows = small(*first_rows)
    g = small(*projection_rows)
    both_parts = jnp.stack([first_part, small(*last_along)])
    second_rows, first_rows, both_parts, g = fence((second_rows, first_rows, both_parts, g))
    second_rows = [second_rows[0]] + to_rows(second_rows)
    first_rows = shift(first_rows, "col", 2)
    projection_far = shift(g[:2], "col", 2)
    grad_one_other.append(to_pair(sent[half:]))
    both_parts_other = to_y(both_parts)
    second_rows, first_rows, projection_far, grad_one_other, both_parts, both_parts_other, g = fence(
        (second_rows, first_rows, projection_far, grad_one_other, both_parts, both_parts_other, g)
    )

    both = combine(second_rows, first_rows, g[2:], projection_far)
    both, both_parts, both_parts_other, grad_one_other = fence((both, both_parts, both_parts_other, grad_one_other))
    both_other = to_y(both)
    both_parts = halves(y == 0, both_parts[:, None], both_parts_other[:, None], 1)
    both_parts_core = to_core(both_parts)
    arrived = jnp.concatenate(grad_one_other).astype(F32)
    grad_inputs, gain_one_term = norm_back(inputs.astype(F32), gain_one, kept + arrived)
    grad_inputs = unrel((grad_inputs + grad_middle).astype(BF))
    gains = unrel(jnp.stack([gain_one_term, gain_two_term]))
    for axis, n in (("row", row_size), ("col", col_size)):
        bit = 1
        while bit < n:
            gains = gains + lax.ppermute(gains, axis, [(i, i ^ bit) for i in range(n)])
            bit *= 2
    gains = gains + swap(gains, "dp", 1)
    gate_up_grad, down_grad = place(
        jnp.where(core == 0, both_parts, both_parts_core), jnp.where(core == 0, both_parts_core, both_parts)
    )
    output = unrel((out_kept + out_other.astype(F32)).astype(BF))
    both, both_other, gate_up_grad, down_grad, gains, output, grad_inputs = fence(
        (both, both_other, gate_up_grad, down_grad, gains, output, grad_inputs)
    )
    both = small(both, both_other)
    both_other = to_core(both)
    gains = gains + swap(gains, "dp", 2)
    attention_gain_grad, feedforward_gain_grad = gains[0], gains[1]
    query_grad, key_value_grad, projection_grad = place_attention(
        jnp.where(core == 0, both, both_other), jnp.where(core == 0, both_other, both), block
    )
    return (
        output,
        grad_inputs,
        attention_gain_grad,
        feedforward_gain_grad,
        query_grad,
        key_value_grad,
        projection_grad,
        gate_up_grad,
        down_grad,
    )


def solution(mesh):
    sizes = tuple(mesh.shape[name] for name in ("dp", "row", "col"))
    return jax.shard_map(
        functools.partial(per_device, sizes=sizes),
        mesh=mesh,
        in_specs=(
            P(("dp", "row", "col"), None),
            P(),
            P(),
            P("row", "col"),
            P("row", None, "col"),
            P("col", "row"),
            P("row", None, "col"),
            P("col", "row"),
            P(("dp", "row", "col"), None),
        ),
        out_specs=(
            P(("dp", "row", "col"), None),
            P(("dp", "row", "col"), None),
            P(),
            P(),
            P("row", "col"),
            P("row", None, "col"),
            P("col", "row"),
            P("row", None, "col"),
            P("col", "row"),
        ),
        check_vma=False,
    )
```

```python
import functools
import math

import jax
import jax.numpy as jnp
from jax import lax
from jax.experimental import pallas as pl
from jax.experimental.pallas import tpu as pltpu
from jax.sharding import PartitionSpec as P

QUERY_HEADS = 16
KEY_VALUE_HEADS = 8
HEAD_DIM = 96
SEQUENCE_TOKENS = 1024

eps = 1e-05
rope_base = 100000.0

BF = jnp.bfloat16
F32 = jnp.float32

HALF = HEAD_DIM // 2
LANES = 128
GROUP = 4 * HEAD_DIM
GROUP_LANES = 4 * LANES
BLOCK = 256
SCALE = HEAD_DIM ** (-0.5)
PARTS = 2
QUICK = pl.CostEstimate(flops=1, bytes_accessed=1, transcendentals=0)
SPLIT_MODEL = 768


def dot(a, b):
    return lax.dot_general(a, b, (((1,), (0,)), ((), ())), preferred_element_type=F32)


def dot_nt(a, b):
    return lax.dot_general(a, b, (((1,), (1,)), ((), ())), preferred_element_type=F32)


def dot_tn(a, b):
    return lax.dot_general(a, b, (((0,), (0,)), ((), ())), preferred_element_type=F32)


def exponentials_t(keys, queries, block):
    s = dot_nt(keys, queries)
    here = s[block * BLOCK :]
    later = lax.broadcasted_iota(jnp.int32, here.shape, 0) > lax.broadcasted_iota(jnp.int32, here.shape, 1)
    here = jnp.where(later, -1e30, here)
    s = jnp.concatenate([s[: block * BLOCK], here], axis=0) if block else here
    top = jnp.max(s, axis=0, keepdims=True)
    e = jnp.exp2((s - top) * (SCALE * math.log2(math.e)))
    return e, 1.0 / jnp.sum(e, axis=0, keepdims=True)


def attention_forward_kernel(n1_ref, w_ref, spread_ref, cos_ref, sin_ref, qkv_ref, o_ref):
    w = dot(w_ref[...], spread_ref[...]).astype(BF)
    h = dot(n1_ref[...], w)
    cos, sin = cos_ref[...], sin_ref[...]
    for part in range(4):
        c = h[:, part * LANES : (part + 1) * LANES]
        if part < 3:
            c = c * cos + pltpu.roll(c, LANES // 2, 1) * sin
        qkv_ref[:, part * LANES : (part + 1) * LANES] = c.astype(BF)
    v_t = h[:, 3 * LANES :].T.astype(BF)
    for head in range(2):
        lanes = slice(head * LANES, (head + 1) * LANES)
        for block in range(SEQUENCE_TOKENS // BLOCK):
            rows = slice(block * BLOCK, (block + 1) * BLOCK)
            length = (block + 1) * BLOCK
            e, inverse = exponentials_t(qkv_ref[:length, 2 * LANES : 3 * LANES], qkv_ref[rows, lanes], block)
            o_t = dot(v_t[:, :length], e.astype(BF)) * inverse
            o_ref[rows, lanes] = o_t.T.astype(BF)


def attention_backward_kernel(qkv_ref, do_ref, gather_ref, cos_ref, sin_ref, out_ref, dk_ref, dv_ref, dq_ref, d_ref):
    cos, sin = cos_ref[...], sin_ref[...]

    def unrotate(c):
        c = c * SCALE
        return (c * cos - pltpu.roll(c, LANES // 2, 1) * sin).astype(BF)

    k_t = qkv_ref[:, 2 * LANES : 3 * LANES].astype(F32).T.astype(BF)
    dk_ref[...] = jnp.zeros_like(dk_ref)
    dv_ref[...] = jnp.zeros_like(dv_ref)
    for head in range(2):
        lanes = slice(head * LANES, (head + 1) * LANES)
        for block in range(SEQUENCE_TOKENS // BLOCK):
            rows = slice(block * BLOCK, (block + 1) * BLOCK)
            length = (block + 1) * BLOCK
            q = qkv_ref[rows, lanes]
            do = do_ref[rows, lanes]
            e, inverse = exponentials_t(qkv_ref[:length, 2 * LANES : 3 * LANES], q, block)
            p = e * inverse
            dp = dot_nt(qkv_ref[:length, 3 * LANES :], do)
            ds = (p * (dp - jnp.sum(p * dp, axis=0, keepdims=True))).astype(BF)
            dv_ref[:length, :] += dot(p.astype(BF), do)
            dk_ref[:length, :] += dot(ds, q)
            dq_ref[rows, :] = dot(k_t[:, :length], ds).T
        d_ref[:, lanes] = unrotate(dq_ref[...])
    d_ref[:, 2 * LANES : 3 * LANES] = unrotate(dk_ref[...])
    d_ref[:, 3 * LANES :] = dv_ref[...].astype(BF)
    out_ref[...] = dot(d_ref[...], gather_ref[...]).astype(BF)


def rotary_tables():
    positions = jnp.arange(SEQUENCE_TOKENS).astype(F32)
    inverse_freq = jnp.exp(jnp.arange(HALF).astype(F32) * (-2.0 * math.log(rope_base) / HEAD_DIM))
    angles = positions[:, None] * inverse_freq[None, :]
    gap = ((0, 0), (0, LANES // 2 - HALF))
    cos, sin = jnp.pad(jnp.cos(angles), gap), jnp.pad(jnp.sin(angles), gap)
    return jnp.concatenate([cos, cos], axis=1), jnp.concatenate([-sin, sin], axis=1)


def spread_matrix():
    src = lax.broadcasted_iota(jnp.int32, (GROUP, GROUP_LANES), 0)
    lane = lax.broadcasted_iota(jnp.int32, (GROUP, GROUP_LANES), 1)
    head, comp = src // HEAD_DIM, src % HEAD_DIM
    place = head * LANES + jnp.where(comp < HALF, comp, comp + LANES // 2 - HALF)
    return (place == lane).astype(BF)


def attention_forward(n1, w, spread, cos, sin):
    tokens, width = n1.shape
    groups = w.shape[1] // GROUP
    whole = lambda a: pl.BlockSpec(a.shape, lambda j: (0, 0))
    return pl.pallas_call(
        attention_forward_kernel,
        grid=(groups,),
        in_specs=[
            whole(n1),
            pl.BlockSpec((width, GROUP), lambda j: (0, j)),
            whole(spread),
            whole(cos),
            whole(sin),
        ],
        out_specs=[
            pl.BlockSpec((tokens, GROUP_LANES), lambda j: (0, j)),
            pl.BlockSpec((tokens, 2 * LANES), lambda j: (0, j)),
        ],
        out_shape=[
            jax.ShapeDtypeStruct((tokens, groups * GROUP_LANES), BF),
            jax.ShapeDtypeStruct((tokens, groups * 2 * LANES), BF),
        ],
        compiler_params=pltpu.CompilerParams(vmem_limit_bytes=48 * 1024 * 1024),
        cost_estimate=QUICK,
        name="attention_forward",
    )(n1, w, spread, cos, sin)


def attention_backward(qkv, do, gather, cos, sin, first, groups):
    tokens = qkv.shape[0]
    whole = lambda a: pl.BlockSpec(a.shape, lambda j: (0, 0))
    return pl.pallas_call(
        attention_backward_kernel,
        grid=(groups,),
        in_specs=[
            pl.BlockSpec((tokens, GROUP_LANES), lambda j: (0, first + j)),
            pl.BlockSpec((tokens, 2 * LANES), lambda j: (0, first + j)),
            whole(gather),
            whole(cos),
            whole(sin),
        ],
        out_specs=pl.BlockSpec((tokens, GROUP), lambda j: (0, j)),
        out_shape=jax.ShapeDtypeStruct((tokens, groups * GROUP), BF),
        scratch_shapes=[
            pltpu.VMEM((tokens, LANES), F32),
            pltpu.VMEM((tokens, LANES), F32),
            pltpu.VMEM((tokens, LANES), F32),
            pltpu.VMEM((tokens, GROUP_LANES), BF),
        ],
        compiler_params=pltpu.CompilerParams(vmem_limit_bytes=48 * 1024 * 1024),
        cost_estimate=QUICK,
        name="attention_backward",
    )(qkv, do, gather, cos, sin)


def feedforward_kernel(col_step, sub, rows_of, n2_ref, cot_ref, *refs):
    *blocks, out_bf_ref, dn2_bf_ref, out_ref, dn2_ref, h_ref, dgu_ref = refs
    sides = [blocks[k : k + rows_of] for k in range(0, len(blocks), rows_of)]
    weights, earlier, grads = sides[:2], sides[2:-2], sides[-2:]
    step, half = pl.program_id(0), pl.num_programs(0) // 2
    width = n2_ref.shape[1] // rows_of
    cut = [slice(i * width, (i + 1) * width) for i in range(rows_of)]

    @pl.when(step == 0)
    def _():
        out_ref[...] = jnp.zeros_like(out_ref)
        dn2_ref[...] = jnp.zeros_like(dn2_ref)

    def rows(ref, first, last):
        return jnp.concatenate([ref[c, first:last] for c in range(col_step)], axis=0)

    def work(whose):
        gate_up = [rows(r, 0, 2 * sub) for r in weights[whose]]
        down = [rows(r, 2 * sub, 3 * sub) for r in weights[whose]]
        dh = sum(dot_nt(cot_ref[:, cut[i]], down[i]) for i in range(rows_of))
        gu = sum(dot_nt(n2_ref[:, cut[i]], gate_up[i]) for i in range(rows_of))
        for c in range(col_step):
            gate, up = (gu[:, (2 * c + k) * sub : (2 * c + k + 1) * sub] for k in range(2))
            sig = jax.nn.sigmoid(gate)
            silu = gate * sig
            lanes = slice(c * sub, (c + 1) * sub)
            part = dh[:, lanes]
            h_ref[:, lanes] = (silu * up).astype(BF)
            dgu_ref[:, 2 * c * sub : (2 * c + 1) * sub] = (part * up * (sig + silu * (1 - sig))).astype(BF)
            dgu_ref[:, (2 * c + 1) * sub : (2 * c + 2) * sub] = (part * silu).astype(BF)
        hidden, dgu = h_ref[...], dgu_ref[...]
        hidden_t, dgu_t = hidden.T, dgu.T
        for i in range(rows_of):
            dn2_ref[:, cut[i]] += dot(dgu, gate_up[i])
            out_ref[:, cut[i]] += dot(hidden, down[i])
            gate_up_grad = dot(dgu_t, n2_ref[:, cut[i]])
            down_grad = dot(hidden_t, cot_ref[:, cut[i]])
            for c in range(col_step):
                new = (gate_up_grad[2 * c * sub : 2 * (c + 1) * sub], down_grad[c * sub : (c + 1) * sub])
                for part, here in zip(new, (slice(2 * sub), slice(2 * sub, None))):
                    if earlier:
                        part = part + earlier[whose][i][c, here].astype(F32)
                    grads[whose][i][c, here] = part.astype(BF)

    pl.when(step < half)(lambda: work(1))
    pl.when(step >= half)(lambda: work(0))

    @pl.when(step == 2 * half - 1)
    def _():
        out_bf_ref[...] = out_ref[...].astype(BF)
        dn2_bf_ref[...] = dn2_ref[...].astype(BF)


def feedforward(n2, cot, weights, col_step, earlier=()):
    tokens, model = n2.shape
    rows_of = len(weights[0])
    columns, rows, width = weights[0][0].shape
    sub = rows // 3
    half = columns // col_step
    once = lambda a: pl.BlockSpec(a.shape, lambda s: (0, 0), pipeline_mode=pl.Buffered(1))
    place = [lambda s: (jnp.maximum(s - half, 0), 0, 0), lambda s: (jnp.minimum(s, half - 1), 0, 0)]
    flat = [a for side in weights for a in side]
    specs = [pl.BlockSpec((col_step, rows, width), place[whose]) for whose in range(2) for _ in range(rows_of)]
    earlier = [a for side in earlier for a in side]
    total = jax.ShapeDtypeStruct((tokens, model), BF)
    outs = pl.pallas_call(
        functools.partial(feedforward_kernel, col_step, sub, rows_of),
        grid=(2 * half,),
        in_specs=[once(n2), once(cot)] + specs + (specs if earlier else []),
        out_specs=specs + [once(total), once(total)],
        out_shape=[jax.ShapeDtypeStruct(a.shape, BF) for a in flat] + [total, total],
        scratch_shapes=[
            pltpu.VMEM((tokens, model), F32),
            pltpu.VMEM((tokens, model), F32),
            pltpu.VMEM((tokens, col_step * sub), BF),
            pltpu.VMEM((tokens, 2 * col_step * sub), BF),
        ],
        compiler_params=pltpu.CompilerParams(vmem_limit_bytes=60 * 1024 * 1024),
        cost_estimate=QUICK,
        name="feedforward",
    )(n2, cot, *flat, *earlier)
    return [list(outs[:rows_of]), list(outs[rows_of : 2 * rows_of])], outs[2 * rows_of], outs[2 * rows_of + 1]


def place_kernel(*refs):
    cores, (gate_up_ref, down_ref) = refs[:2], refs[2:]
    parts, _, rows, block = cores[0].shape
    sub = rows // 3
    for core, ref in enumerate(cores):
        for y in range(2):
            for k in range(parts):
                tile = (2 * y + core) * parts + k
                for half in range(2):
                    piece = ref[k, y, half * sub : (half + 1) * sub].astype(F32)
                    gate_up_ref[pl.ds(2 * tile + half, block, stride=8 * parts), :] = piece.T
                down_ref[tile * sub : (tile + 1) * sub] = ref[k, y, 2 * sub :].astype(F32)


def place(first, second):
    parts, _, rows, block = first.shape
    sub = rows // 3
    tiles = 4 * parts
    gate_up, down = pl.pallas_call(
        place_kernel,
        out_shape=[
            jax.ShapeDtypeStruct((block * tiles * 2, sub), F32),
            jax.ShapeDtypeStruct((tiles * sub, block), F32),
        ],
        compiler_params=pltpu.CompilerParams(vmem_limit_bytes=48 * 1024 * 1024),
        cost_estimate=QUICK,
        name="place",
    )(first, second)
    return gate_up.reshape(block, tiles, 2, sub).transpose(0, 2, 1, 3).reshape(block, 2, -1), down


def combine_kernel(*refs):
    out_ref = refs[-1]
    *rows, mine, other = refs[:-1]
    qkv = sum(r[...].astype(F32) for r in rows).astype(BF)
    heads = (mine[...].astype(F32) + other[...].astype(F32)).astype(BF)
    split = qkv.shape[0]
    for p in range(2):
        out_ref[p, :split] = qkv[:, p * GROUP : (p + 1) * GROUP]
        for n in range(2 * split // GROUP):
            here = slice(split + n * HEAD_DIM, split + (n + 1) * HEAD_DIM)
            out_ref[p, here] = heads[p, :, n * GROUP : (n + 1) * GROUP]


def combine(rows, arrived, heads, heads_arrived):
    split, block = rows[0].shape[0], heads.shape[2]
    if block % GROUP:
        qkv = sum(r.astype(F32) for r in rows + [arrived])
        heads = heads.astype(F32) + heads_arrived.astype(F32)
        parts = [jnp.concatenate([qkv[:, p * GROUP : (p + 1) * GROUP], heads[p].reshape(-1, GROUP)]) for p in range(2)]
        return jnp.stack(parts).astype(BF)
    return pl.pallas_call(
        combine_kernel,
        out_shape=jax.ShapeDtypeStruct((2, split + HEAD_DIM * block // GROUP, GROUP), BF),
        compiler_params=pltpu.CompilerParams(vmem_limit_bytes=32 * 1024 * 1024),
        cost_estimate=QUICK,
        name="combine",
    )(*rows, arrived, heads, heads_arrived)


def place_attention_kernel(*refs):
    cores, (query_ref, pair_ref, projection_ref) = refs[:2], refs[2:]
    block = query_ref.shape[0]
    rows = block // 2
    for core, ref in enumerate(cores):
        here = slice(core * rows, (core + 1) * rows)
        for parity in range(2):
            g = ref[parity, :rows].astype(F32)
            query_ref[here, 2 * parity * HEAD_DIM : 2 * (parity + 1) * HEAD_DIM] = g[:, : 2 * HEAD_DIM]
            g = g.T
            for k in range(2):
                pair_ref[k, parity * HEAD_DIM : (parity + 1) * HEAD_DIM, here] = g[(2 + k) * HEAD_DIM : (3 + k) * HEAD_DIM]
            head = slice((2 * parity + core) * HEAD_DIM, (2 * parity + core + 1) * HEAD_DIM)
            for k in range(block // GROUP):
                piece = ref[parity, rows + k * HEAD_DIM : rows + (k + 1) * HEAD_DIM]
                projection_ref[head, k * GROUP : (k + 1) * GROUP] = piece.astype(F32)


def place_attention(first, second, block):
    folded = block % GROUP != 0
    query, pair, projection = pl.pallas_call(
        place_attention_kernel,
        out_shape=[
            jax.ShapeDtypeStruct((block, 4 * HEAD_DIM), F32),
            jax.ShapeDtypeStruct((2, 2 * HEAD_DIM, block), F32),
            jax.ShapeDtypeStruct((4 * HEAD_DIM, block), F32),
        ],
        compiler_params=pltpu.CompilerParams(vmem_limit_bytes=32 * 1024 * 1024),
        cost_estimate=QUICK,
        name="place_attention",
    )(first, second)
    if folded:
        both = jnp.stack([a[:, block // 2 :].reshape(2, HEAD_DIM, block) for a in (first, second)], axis=1)
        projection = both.astype(F32).reshape(-1, block)
    return query, pair.transpose(2, 0, 1), projection


def assemble_kernel(groups, core_ref, *refs):
    pieces, (qkv_ref, projection_ref) = refs[:-2], refs[-2:]
    first = core_ref[0] == 0
    blocks = len(pieces) // groups
    rows = qkv_ref.shape[0] // (2 * blocks)
    projection_ref[...] = jnp.zeros_like(projection_ref)
    for i in range(blocks):
        for k in range(groups // 2):
            mine, other = pieces[i * groups + 2 * k], pieces[i * groups + 2 * k + 1]
            for p in range(2):
                a, b = mine[p], other[p]
                group = 2 * k + p
                for core, piece in enumerate((jnp.where(first, a, b), jnp.where(first, b, a))):
                    start = (2 * i + core) * rows
                    qkv_ref[start : start + rows, group * GROUP : (group + 1) * GROUP] = piece[:rows]
                    place = group * 2 * LANES + core * LANES
                    for n in range(2 * rows // GROUP):
                        lanes = slice(2 * i * rows + n * GROUP, 2 * i * rows + (n + 1) * GROUP)
                        head = piece[rows + n * HEAD_DIM : rows + (n + 1) * HEAD_DIM]
                        projection_ref[place : place + HALF, lanes] = head[:HALF]
                        projection_ref[place + LANES // 2 : place + LANES // 2 + HALF, lanes] = head[HALF:]


def assemble(core, pieces, model):
    groups = len(pieces[0])
    flat = [a for row in pieces for a in row]
    return pl.pallas_call(
        functools.partial(assemble_kernel, groups),
        in_specs=[pl.BlockSpec(memory_space=pltpu.SMEM)] + [pl.BlockSpec(memory_space=pltpu.VMEM)] * len(flat),
        out_shape=[
            jax.ShapeDtypeStruct((model, groups * GROUP), BF),
            jax.ShapeDtypeStruct((groups * 2 * LANES, model), BF),
        ],
        compiler_params=pltpu.CompilerParams(vmem_limit_bytes=48 * 1024 * 1024),
        cost_estimate=QUICK,
        name="assemble",
    )(core.astype(jnp.int32)[None], *flat)


def halves_kernel(gap, core_ref, a_ref, b_ref, out_ref):
    g = dot_tn(a_ref[...], b_ref[...]).astype(BF)
    rows = g.shape[0] // 2
    first = core_ref[0] == 0
    for h, (low, high) in enumerate(((0, rows), (rows, 0))):
        piece = jnp.where(first, g[low : low + rows], g[high : high + rows])
        if gap:
            out_ref[h, 0, :HALF] = piece[:HALF]
            out_ref[h, 0, HALF:] = piece[LANES // 2 : LANES // 2 + HALF]
        else:
            out_ref[h, 0] = piece


def gradient_halves(core, a, b, rows, gap=False):
    tokens, width = a.shape
    blocks = width // (2 * rows)
    kept = HEAD_DIM if gap else rows
    columns = b.shape[1]
    return pl.pallas_call(
        functools.partial(halves_kernel, gap),
        grid_spec=pltpu.PrefetchScalarGridSpec(
            num_scalar_prefetch=1,
            grid=(blocks,),
            in_specs=[
                pl.BlockSpec((tokens, 2 * rows), lambda i, core: (0, i)),
                pl.BlockSpec(b.shape, lambda i, core: (0, 0)),
            ],
            out_specs=pl.BlockSpec((2, 1, kept, columns), lambda i, core: (0, i, 0, 0)),
        ),
        out_shape=jax.ShapeDtypeStruct((2, blocks, kept, columns), BF),
        compiler_params=pltpu.CompilerParams(vmem_limit_bytes=48 * 1024 * 1024),
        cost_estimate=QUICK,
        name="gradient_halves",
    )(core.astype(jnp.int32)[None], a, b)


def inverse_rms(field):
    return lax.rsqrt(jnp.mean(field * field, axis=-1, keepdims=True) + eps)


def norm_back(field, gain, grad):
    r = inverse_rms(field)
    scaled = gain * grad
    inner = jnp.mean(field * scaled, axis=-1, keepdims=True)
    return r * scaled - field * (r * r * r * inner), jnp.sum(grad * field * r, axis=0)


def norm_back_kernel(field_ref, gain_ref, skip_ref, *refs):
    *terms, out_ref, rounded_ref, gain_grad_ref = refs
    field = field_ref[...]
    grad = sum(t[...].astype(F32) for t in terms)
    r = inverse_rms(field)
    scaled = gain_ref[...] * grad
    inner = jnp.mean(field * scaled, axis=-1, keepdims=True)
    out = skip_ref[...].astype(F32) + r * scaled - field * (r * r * r * inner)
    out_ref[...] = out
    rounded_ref[...] = out.astype(BF)

    @pl.when(pl.program_id(0) == 0)
    def _():
        gain_grad_ref[...] = jnp.zeros_like(gain_grad_ref)

    gain_grad_ref[...] += jnp.sum(grad * (field * r), axis=0, keepdims=True)


def norm_back_rows(field, gain, skip, terms):
    tokens, model = field.shape
    rows = 128
    block = pl.BlockSpec((rows, model), lambda i: (i, 0))
    line = pl.BlockSpec((1, model), lambda i: (0, 0))
    out, rounded, gain_grad = pl.pallas_call(
        norm_back_kernel,
        grid=(tokens // rows,),
        in_specs=[block, line, block] + [block] * len(terms),
        out_specs=[block, block, line],
        out_shape=[
            jax.ShapeDtypeStruct(field.shape, F32),
            jax.ShapeDtypeStruct(field.shape, BF),
            jax.ShapeDtypeStruct((1, model), F32),
        ],
        compiler_params=pltpu.CompilerParams(vmem_limit_bytes=60 * 1024 * 1024),
        cost_estimate=QUICK,
        name="norm_back",
    )(field, gain[None], skip, *terms)
    return out, rounded, gain_grad[0]


def halves(first_is_mine, mine, other, axis):
    return jnp.where(
        first_is_mine, jnp.concatenate([mine, other], axis), jnp.concatenate([other, mine], axis)
    )


def per_device(
    tokens,
    attention_gain,
    feedforward_gain,
    query_weight,
    key_value_matrix,
    projection_weight,
    gate_up_weight,
    down_weight,
    cotangent,
    *,
    sizes,
):
    dp_size, row_size, col_size = sizes
    x, z, d = lax.axis_index("row"), lax.axis_index("col"), lax.axis_index("dp")
    core, y, parity = d % 2, d // 2, z % 2
    model = tokens.shape[1]
    own = tokens.shape[0]
    block = model // row_size
    hidden_block = down_weight.shape[0]
    sub = hidden_block // 4 // PARTS

    def swap(a, axis, bit):
        n = {"dp": dp_size, "col": col_size}[axis]
        return lax.ppermute(a, axis, [(i, i ^ bit) for i in range(n)])

    def to_core(a):
        return swap(a, "dp", 1)

    def to_y(a):
        return swap(a, "dp", 2)

    def to_pair(a):
        return swap(a, "col", 1)

    def shift(a, axis, by):
        n = {"row": row_size, "col": col_size}[axis]
        return lax.ppermute(a, axis, [(i, (i + by) % n) for i in range(n)])

    def rel(a):
        if row_size == 2:
            return jnp.where(x == 0, a, jnp.concatenate([a[..., block:], a[..., :block]], axis=-1))
        return lax.dynamic_slice_in_dim(jnp.concatenate([a, a], axis=-1), x * block, model, a.ndim - 1)

    def unrel(a):
        if row_size == 2:
            return rel(a)
        return lax.dynamic_slice_in_dim(
            jnp.concatenate([a, a], axis=-1), (row_size - x) % row_size * block, model, a.ndim - 1
        )

    def gather_rows(piece):
        return [piece] + [shift(piece, "row", -i) for i in range(1, row_size)]

    def pick(a, index, axis):
        return lax.dynamic_index_in_dim(a, index, axis, keepdims=False)

    def merge(rows):
        return rows if len(rows) * SPLIT_MODEL <= model else [jnp.concatenate(rows, axis=2)]

    def by_rows(blocks):
        return list(blocks) if len(blocks) == row_size else jnp.split(blocks[0], row_size, axis=2)

    fence = lax.optimization_barrier

    def fold(a):
        if block % GROUP:
            return a.reshape(-1, GROUP)
        return jnp.concatenate([a[:, k : k + GROUP] for k in range(0, block, GROUP)])

    def unfold(a):
        if block % GROUP:
            return a.reshape(a.shape[:-2] + (HEAD_DIM, block))
        return jnp.concatenate([a[..., k : k + HEAD_DIM, :] for k in range(0, a.shape[-2], HEAD_DIM)], axis=-1)


    def total(*parts):
        return sum(part.astype(F32) for part in parts)

    def small(*parts):
        return total(*parts).astype(BF)

    def in_sequence(a, other):
        return halves(parity == 0, a, other, 0)

    def rows_of(a, first):
        return lax.dynamic_slice_in_dim(a, first, own, 0)

    query_blocks = query_weight.reshape(block, 2, 2 * HEAD_DIM)
    pair_blocks = key_value_matrix.reshape(block, 2, 2, HEAD_DIM)
    packed = jnp.concatenate([query_blocks, pair_blocks[:, 0], pair_blocks[:, 1]], axis=-1)
    packed = lax.dynamic_slice_in_dim(packed, core * (block // 2), block // 2, 0)
    head_rows = pick(projection_weight.reshape(2, 2, HEAD_DIM, block), core, 1)
    packed = jnp.stack([jnp.concatenate([packed[:, p], fold(head_rows[p])]) for p in range(2)])
    packed, tokens, cotangent, gate_up_weight, down_weight = fence(
        (packed, tokens, cotangent, gate_up_weight, down_weight)
    )
    far_packed = shift(packed, "col", 2)
    own_packed = gather_rows(packed)

    pieces = []
    for part in range(PARTS):
        start = ((2 * y + core) * PARTS + part) * sub
        gate_up = lax.dynamic_slice_in_dim(gate_up_weight, start, sub, 2).transpose(1, 2, 0).reshape(2 * sub, block)
        pieces.append(jnp.concatenate([gate_up, lax.dynamic_slice_in_dim(down_weight, start, sub, 0)]))
    gain_one, gain_two = rel(attention_gain), rel(feedforward_gain)
    inputs = rel(tokens)
    wide_inputs = inputs.astype(F32)
    normed = (wide_inputs * inverse_rms(wide_inputs) * gain_one).astype(BF)
    normed_other = to_pair(normed)
    tables = rotary_tables()
    spread = spread_matrix()
    spread_back = spread.T
    far_packed, own_packed, pieces, inputs, normed, normed_other, tables = fence(
        (far_packed, own_packed, pieces, inputs, normed, normed_other, tables)
    )

    far_rows = gather_rows(far_packed)
    own_cores = [to_core(a) for a in own_packed]
    others = [shift(pieces[0], "col", 1)]
    late_others = [shift(pieces[1], "col", 1)]
    normed_all = in_sequence(normed, normed_other)
    grad_out = rel(cotangent)
    far_rows, own_cores, own_packed, others, late_others, normed_all, spread, spread_back, grad_out, pieces = fence(
        (far_rows, own_cores, own_packed, others, late_others, normed_all, spread, spread_back, grad_out, pieces)
    )
    own_rows = gather_rows(jnp.stack(pieces))
    rest_near = gather_rows(others[0])
    far_cores = [to_core(a) for a in far_rows]
    others += [shift(pieces[0], "col", j) for j in range(2, col_size)]
    split = block // 2
    if split % LANES == 0:
        rows = [list(parts) for parts in zip(far_rows, far_cores, own_packed, own_cores)]
        weight_qkv, weight_projection = assemble(core, rows, model)
    else:
        pick_core = lambda a, b: halves(core == 0, a[:, None], b[:, None], 1)
        pairs = [
            jnp.concatenate([pick_core(*far), pick_core(*mine)])
            for far, mine in zip(zip(far_rows, far_cores), zip(own_packed, own_cores))
        ]
        weight_qkv = jnp.concatenate([jnp.concatenate([p[j, :, :split] for j in range(col_size)], axis=-1) for p in pairs])
        weight_qkv = weight_qkv.reshape(model, -1)
        heads = jnp.concatenate([unfold(p[:, :, split:]) for p in pairs], axis=-1)
        gap = jnp.zeros(heads.shape[:2] + (LANES // 2 - HALF, model), BF)
        weight_projection = jnp.concatenate(
            [heads[:, :, :HALF], gap, heads[:, :, HALF:], gap], axis=2
        ).reshape(-1, model)
    weight_qkv, weight_projection = fence((weight_qkv, weight_projection))

    qkv, attended = attention_forward(normed_all, weight_qkv, spread, *tables)
    qkv, attended, others, late_others, own_rows, grad_out, weight_projection, rest_near = fence(
        (qkv, attended, others, late_others, own_rows, grad_out, weight_projection, rest_near)
    )

    sent = dot(rows_of(attended, (1 - parity) * own), weight_projection).astype(BF)
    stacked = jnp.stack(others[1:])
    sent, stacked, attended, weight_projection = fence((sent, stacked, attended, weight_projection))
    arrived = to_pair(sent)
    rest = gather_rows(stacked)
    grad_out_other = to_y(grad_out)
    fine = row_size * SPLIT_MODEL <= model
    own_first = [a[0] for a in own_rows]
    kept = dot(rows_of(attended, parity * own), weight_projection)
    kept, stacked = fence((kept, stacked))
    mine = [jnp.concatenate([own_first[0][None], rest_near[0][None], stacked])] if fine else []
    mine_other = [to_core(a) for a in mine]
    kept, arrived, rest, mine, mine_other, pieces, own_rows, grad_out, grad_out_other = fence(
        (kept, arrived, rest, mine, mine_other, pieces, own_rows, grad_out, grad_out_other)
    )

    middle = inputs.astype(F32) + kept + arrived.astype(F32)
    normed_two = (middle * inverse_rms(middle) * gain_two).astype(BF)
    n = len(mine)
    late = merge([jnp.concatenate([a[None], b[None], c]) for a, b, c in zip(own_first[n:], rest_near[n:], rest[n:])])
    normed_two, middle, late = fence((normed_two, middle, late))
    normed_two_other = to_y(normed_two)
    weights = [mine + late, mine_other + [to_core(a) for a in late]]
    others = [shift(pieces[1], "col", j) for j in (2, 3)]
    weights, normed_two = fence((weights, normed_two))

    rest = [gather_rows(late_others[0])]
    grads, *sums = feedforward(normed_two, grad_out, weights, PARTS)
    grads, sums, rest, others, normed_two_other, weights, middle, late_others = fence(
        (grads, sums, rest, others, normed_two_other, weights, middle, late_others)
    )
    own_sums = [sums]
    stacked = jnp.stack(others)
    early = (
        [jnp.concatenate([own_rows[0][1:], late_others[0][None], stacked])] if row_size * SPLIT_MODEL <= model else []
    )
    stacked, early, own_rows = fence((stacked, early, own_rows))
    rest.append(gather_rows(stacked))
    early_other = [to_core(a) for a in early]
    grads, *sums = feedforward(normed_two_other, grad_out_other, weights, PARTS, grads)
    grads, sums, rest, early, early_other, own_rows = fence((grads, sums, rest, early, early_other, own_rows))
    other_sums = [sums]
    n = len(early)
    late = merge([jnp.concatenate([a[1:], b[None], c]) for a, b, c in zip(own_rows[n:], rest[0][n:], rest[1][n:])])
    mine, other = by_rows(grads[0]), by_rows(grads[1])
    late, other[1:] = fence((late, other[1:]))
    late_other = [to_core(a) for a in late]
    arrived = [to_core(a) for a in other[1:]]
    mine, other[0], late, late_other, arrived = fence((mine, other[0], late, late_other, arrived))
    weights = [early + late, early_other + late_other]
    middle_columns = lambda a: a[1:3]
    outer_columns = lambda a: jnp.stack([a[0], a[3]])
    sent = [[small(cut(a), cut(b)) for a, b in zip(mine[1:], arrived)] for cut in (middle_columns, outer_columns)]
    weights, mine[0], other[0], sent, normed_two_other = fence((weights, mine[0], other[0], sent, normed_two_other))
    rows = [shift(a, "row", i) for i, a in enumerate(sent[0], 1)]
    arrived = to_core(other[0])
    grads, *sums = feedforward(normed_two_other, grad_out_other, weights, PARTS)
    grads, sums, rows, mine[0], arrived, sent, weights = fence((grads, sums, rows, mine[0], arrived, sent, weights))
    other_sums.append(sums)

    sums = small(*[p[1] for p in other_sums])
    sums, mine[0], arrived, rows, grads, other_sums, own_sums = fence(
        (sums, mine[0], arrived, rows, grads, other_sums, own_sums)
    )
    grad_two_other = to_y(sums)
    blocks = [small(mine[0][j], arrived[j], *[r[j - 1] for r in rows]) for j in (1, 2)]
    blocks, grads, normed_two = fence((blocks, grads, normed_two))
    rows = [shift(a, "row", i) for i, a in enumerate(sent[1], 1)]
    along = [shift(blocks[1], "col", -2)]
    grads, *sums = feedforward(normed_two, grad_out, weights, PARTS, grads)
    grads, sums, rows, along, blocks, mine[0], arrived, grad_two_other = fence(
        (grads, sums, rows, along, blocks, mine[0], arrived, grad_two_other)
    )
    near_block = blocks[0]
    own_sums.append(sums)
    last, other = by_rows(grads[0]), by_rows(grads[1])
    last_rows = [to_core(a) for a in other[1:]]
    terms = [grad_two_other] + [p[1] for p in own_sums]
    grad_middle, branch, gain_two_term = norm_back_rows(middle, gain_two, grad_out, terms)
    last_rows, branch, grad_middle, gain_two_term, last, other[0] = fence(
        (last_rows, branch, grad_middle, gain_two_term, last, other[0])
    )
    branch_other = to_pair(branch)
    sent = [[small(cut(a), cut(b)) for a, b in zip(last[1:], last_rows)] for cut in (middle_columns, outer_columns)]
    last_rows = [shift(a, "row", i) for i, a in enumerate(sent[0], 1)]
    last_core = to_core(other[0])
    blocks = [small(mine[0][j], arrived[j], *[r[j // 3] for r in rows]) for j in (0, 3)]
    blocks.append(near_block)
    branch, branch_other, last_core, last_rows, sent, own_sums, other_sums, blocks, grad_middle, gain_two_term = fence(
        (branch, branch_other, last_core, last_rows, sent, own_sums, other_sums, blocks, grad_middle, gain_two_term)
    )

    along += [blocks[0], shift(blocks[1], "col", -3), shift(blocks[2], "col", -1)]
    out_other = to_y(small(*[p[0] for p in other_sums]))
    outer_rows = [shift(a, "row", i) for i, a in enumerate(sent[1], 1)]
    branch_all = in_sequence(branch, branch_other)
    grad_attended = dot_nt(branch_all, weight_projection).astype(BF)
    count = col_size // 2
    wide = count * GROUP
    to_rows = lambda g: [shift(g[i], "row", i) for i in range(1, row_size)]

    def qkv_halves(part):
        if split % LANES == 0:
            return gradient_halves(core, normed_all, part, split)
        g = dot_tn(normed_all, part).astype(BF).reshape(row_size, 2, split, wide)
        return jnp.stack([pick(g, core, 1), pick(g, 1 - core, 1)])

    first = attention_backward(qkv, grad_attended, spread_back, *tables, 0, count)
    first, along, outer_rows, grad_attended, branch_all = fence((first, along, outer_rows, grad_attended, branch_all))
    rows = [[m[0] for m in outer_rows], [m[0] for m in last_rows], [m[1] for m in last_rows], [m[1] for m in outer_rows]]
    blocks = [small(last[0][j], last_core[j], *rows[j]) for j in range(col_size)]
    blocks, grad_attended, first, branch_all = fence((blocks, grad_attended, first, branch_all))
    last_along = [blocks[0]] + [shift(blocks[j], "col", -j) if j & 1 else blocks[j] for j in range(1, col_size)]
    projection_halves = gradient_halves(core, attended, branch_all, LANES, True)
    first_halves = qkv_halves(first)
    second = attention_backward(qkv, grad_attended, spread_back, *tables, count, count)
    second, last_along, along, first_halves, projection_halves, out_other = fence(
        (second, last_along, along, first_halves, projection_halves, out_other)
    )

    product = lambda rows: sum(
        dot_nt(rows(part), weight_qkv[:, k * wide : (k + 1) * wide]) for k, part in enumerate((first, second))
    )
    first_other, projection_other = to_core(first_halves[1]), to_core(projection_halves[1])
    sent = product(lambda a: rows_of(a, (1 - parity) * own)).astype(BF)
    second_halves = qkv_halves(second)
    sent, second_halves, along, last_along, first_other, projection_other, first_halves, projection_halves = fence(
        (sent, second_halves, along, last_along, first_other, projection_other, first_halves, projection_halves)
    )
    half = own // 2
    grad_one_other = [to_pair(sent[:half])]
    last_along[2] = shift(last_along[2], "col", -2)
    first_rows = small(first_halves[0], first_other)
    g = small(projection_halves[0], projection_other)
    sent, first_rows, g, second_halves, own_sums, along = fence((sent, first_rows, g, second_halves, own_sums, along))
    first_part = small(*along)
    out_kept = middle + total(*[p[0] for p in own_sums])
    first_rows = [first_rows[0]] + to_rows(first_rows)
    projection_rows = [g[:, :, i * block : (i + 1) * block] for i in range(row_size)]
    projection_rows[1:] = to_rows(projection_rows)
    second_other = to_core(second_halves[1])
    kept = product(lambda a: rows_of(a, parity * own))
    sent, grad_one_other, last_along, first_rows, projection_rows, second_halves, second_other, first_part, kept, out_kept = fence(
        (sent, grad_one_other, last_along, first_rows, projection_rows, second_halves, second_other, first_part, kept, out_kept)
    )

    second_rows = small(second_halves[0], second_other)
    first_rows = small(*first_rows)
    g = small(*projection_rows)
    both_parts = jnp.stack([first_part, small(*last_along)])
    second_rows, first_rows, both_parts, g = fence((second_rows, first_rows, both_parts, g))
    second_rows = [second_rows[0]] + to_rows(second_rows)
    first_rows = shift(first_rows, "col", 2)
    projection_far = shift(g[:2], "col", 2)
    grad_one_other.append(to_pair(sent[half:]))
    both_parts_other = to_y(both_parts)
    second_rows, first_rows, projection_far, grad_one_other, both_parts, both_parts_other, g = fence(
        (second_rows, first_rows, projection_far, grad_one_other, both_parts, both_parts_other, g)
    )

    both = combine(second_rows, first_rows, g[2:], projection_far)
    both, both_parts, both_parts_other, grad_one_other = fence((both, both_parts, both_parts_other, grad_one_other))
    both_other = to_y(both)
    both_parts = halves(y == 0, both_parts[:, None], both_parts_other[:, None], 1)
    both_parts_core = to_core(both_parts)
    arrived = jnp.concatenate(grad_one_other).astype(F32)
    grad_inputs, gain_one_term = norm_back(inputs.astype(F32), gain_one, kept + arrived)
    grad_inputs = unrel((grad_inputs + grad_middle).astype(BF))
    gains = unrel(jnp.stack([gain_one_term, gain_two_term]))
    for axis, n in (("row", row_size), ("col", col_size)):
        bit = 1
        while bit < n:
            gains = gains + lax.ppermute(gains, axis, [(i, i ^ bit) for i in range(n)])
            bit *= 2
    gains = gains + swap(gains, "dp", 1)
    gate_up_grad, down_grad = place(
        jnp.where(core == 0, both_parts, both_parts_core), jnp.where(core == 0, both_parts_core, both_parts)
    )
    output = unrel((out_kept + out_other.astype(F32)).astype(BF))
    both, both_other, gate_up_grad, down_grad, gains, output, grad_inputs = fence(
        (both, both_other, gate_up_grad, down_grad, gains, output, grad_inputs)
    )
    both = small(both, both_other)
    both_other = to_core(both)
    gains = gains + swap(gains, "dp", 2)
    attention_gain_grad, feedforward_gain_grad = gains[0], gains[1]
    query_grad, key_value_grad, projection_grad = place_attention(
        jnp.where(core == 0, both, both_other), jnp.where(core == 0, both_other, both), block
    )
    return (
        output,
        grad_inputs,
        attention_gain_grad,
        feedforward_gain_grad,
        query_grad,
        key_value_grad,
        projection_grad,
        gate_up_grad,
        down_grad,
    )


def solution(mesh):
    sizes = tuple(mesh.shape[name] for name in ("dp", "row", "col"))
    return jax.shard_map(
        functools.partial(per_device, sizes=sizes),
        mesh=mesh,
        in_specs=(
            P(("dp", "row", "col"), None),
            P(),
            P(),
            P("row", "col"),
            P("row", None, "col"),
            P("col", "row"),
            P("row", None, "col"),
            P("col", "row"),
            P(("dp", "row", "col"), None),
        ),
        out_specs=(
            P(("dp", "row", "col"), None),
            P(("dp", "row", "col"), None),
            P(),
            P(),
            P("row", "col"),
            P("row", None, "col"),
            P("col", "row"),
            P("row", None, "col"),
            P("col", "row"),
        ),
        check_vma=False,
    )
```
